128 devices in a mesh: wide: 32 (over y, x_hi, z), narrow: 4 (over x_lo, core).
Axes of the slice: x: 4 (x_hi: 2, x_lo: 2; x = x_hi * 2 + x_lo), y: 4, z: 4, core: 2. Of those that a mesh axis runs over, the one named last changes fastest.
Arguments:
- tokens: bfloat16 [16384, 1536], P(('wide', 'narrow')), may hold values from -6 to 6
- lengths: int32 [128, 4], P(('wide', 'narrow')), may hold values from 0 to 128, as said below
- w_query: bfloat16 [1536, 1536], P('narrow'), may hold values from -0.15625 to 0.15625
- w_key: bfloat16 [1536, 1536], P('narrow'), may hold values from -0.15625 to 0.15625
- w_value: bfloat16 [1536, 1536], P('narrow'), may hold values from -0.15625 to 0.15625
- w_out: bfloat16 [1536, 1536], P('narrow'), may hold values from -0.625 to 0.625
- w_forget: bfloat16 [1536, 24], P('narrow'), may hold values from -0.15625 to 0.15625
- forget_bias: bfloat16 [24], P('narrow'), may hold values from 0.5 to 6
- norm_attn: bfloat16 [1536], P('narrow'), may hold values from 0.5 to 1.5
- w_gate: bfloat16 [1536, 4096], P('narrow'), may hold values from -0.15625 to 0.15625
- w_up: bfloat16 [1536, 4096], P('narrow'), may hold values from -0.15625 to 0.15625
- w_down: bfloat16 [4096, 1536], P('narrow'), may hold values from -0.09375 to 0.09375
- norm_ffn: bfloat16 [1536], P('narrow'), may hold values from 0.5 to 1.5
- cotangent: bfloat16 [16384, 1536], P(('wide', 'narrow')), may hold values from -6 to 6
Outputs:
- output: bfloat16 [16384, 1536], P(('wide', 'narrow'))
- grad_tokens: float32 [16384, 1536], P(('wide', 'narrow'))
- grad_query: float32 [1536, 1536], P('narrow')
- grad_key: float32 [1536, 1536], P('narrow')
- grad_value: float32 [1536, 1536], P('narrow')
- grad_out: float32 [1536, 1536], P('narrow')
- grad_forget: float32 [1536, 24], P('narrow')
- grad_bias: float32 [24], P('narrow')
- grad_norm_attn: float32 [1536], P('narrow')
- grad_gate: float32 [1536, 4096], P('narrow')
- grad_up: float32 [1536, 4096], P('narrow')
- grad_down: float32 [4096, 1536], P('narrow')
- grad_norm_ffn: float32 [1536], P('narrow')
The draws below stay inside these ranges and needn't reach their ends.
Inputs may be any that keep to these rules, and one draw needn't show every extreme that they name: Each row's lengths sum to at most 128; slots of length 0 hold no sequence; in every draw some device holds a single sequence of 128 rows.
All inputs are finite; a program needn't handle non-finite values.
Results may differ from the reference program's by a relative error of at most 0.028.
Values may be sent and summed in bfloat16 or wider, within the bound.
No kernel may reach another device: no remote copies, remote signals or barrier semaphores. Data moves between devices by JAX's collectives and lax.ppermute only.
A program may use at most 448 MiB of HBM per device.

```python
import jax
import jax.numpy as jnp
from jax import lax

D = 1536
H = 24
HD = 64
FF = 4096
TOK_DEV = 128
SLOTS = 4
TOKENS = 16384


def draw_lengths(key, part):
    key = jax.random.fold_in(key, 7)
    row_total = TOKENS // TOK_DEV
    raw_key, pad_key, pick_key = jax.random.split(key, 3)
    base = jax.random.randint(raw_key, (row_total, SLOTS), 1, 40)
    heavy = base * base * base
    padding = jax.random.randint(pad_key, (row_total, 1), 0, TOK_DEV // 4 + 1)
    spare = TOK_DEV - padding - SLOTS
    lengths = 1 + heavy * spare // jnp.sum(heavy, axis=1, keepdims=True)
    chosen = jax.random.randint(pick_key, (), 0, row_total)
    single = jnp.where(jnp.arange(SLOTS) == 0, TOK_DEV, 0)
    lengths = jnp.where((jnp.arange(row_total) == chosen)[:, None], single[None, :], lengths)
    return lengths.astype(jnp.int32)


def shard_levels(own_key, shape, pieces, least, top_value):
    gain, own = 1.0, jax.random.fold_in(own_key, 6)
    for dim, blocks in pieces:
        steps = jnp.exp(jax.random.uniform(jax.random.fold_in(own, dim), (blocks,), jnp.float32, least / len(pieces), top_value / len(pieces)))
        gain = gain * jnp.repeat(steps, shape[dim] // blocks).reshape([-1 if axis == dim else 1 for axis in range(len(shape))])
    return gain


def centred(rng, extent, deviation, limit, cuts=(), held_as=jnp.bfloat16):
    result = jax.random.normal(rng, extent, jnp.float32) * deviation
    if len(cuts) > 0:
        result = shard_levels(rng, extent, cuts, -0.22, 0.18) * result
    return jnp.clip(result, min=-limit, max=limit).astype(held_as)


def setup_inputs(seed: int = 0) -> dict:
    key_list = jax.random.split(jax.random.key(seed), 15)
    tokens = centred(key_list[0], (TOKENS, D), 1.0, 6.0, ((0, 128),))
    lengths = draw_lengths(jax.random.fold_in(key_list[14], 71), 0)
    w_query = centred(key_list[2], (D, D), D ** -0.5, 0.15625, ((0, 4),))
    w_key = centred(key_list[3], (D, D), D ** -0.5, 0.15625, ((0, 4),))
    w_value = centred(key_list[4], (D, D), D ** -0.5, 0.15625, ((0, 4),))
    w_out = centred(key_list[5], (D, D), (D // 16) ** -0.5, 0.625, ((0, 4),))
    w_forget = centred(key_list[6], (D, H), D ** -0.5, 0.15625, ((0, 4),))
    forget_bias = jnp.clip(0.5 + 5.5 * jax.random.uniform(key_list[7], (H,), jnp.float32) ** shard_levels(key_list[7], (H,), ((0, 4),), -0.2, 0.2), 0.5, 6.0).astype(jnp.bfloat16)
    norm_attn = jnp.clip(1.0 + 0.1 * jax.random.normal(key_list[8], (D,), jnp.float32), 0.5, 1.5).astype(jnp.bfloat16)
    w_gate = centred(key_list[9], (D, FF), D ** -0.5, 0.15625, ((0, 4),))
    w_up = centred(key_list[10], (D, FF), D ** -0.5, 0.15625, ((0, 4),))
    w_down = centred(key_list[11], (FF, D), FF ** -0.5, 0.09375, ((0, 4),))
    norm_ffn = jnp.clip(1.0 + 0.1 * jax.random.normal(key_list[12], (D,), jnp.float32), 0.5, 1.5).astype(jnp.bfloat16)
    cotangent = centred(key_list[13], (TOKENS, D), 1.0, 6.0, ((0, 128),))
    return {"tokens": tokens, "lengths": lengths, "w_query": w_query, "w_key": w_key, "w_value": w_value, "w_out": w_out, "w_forget": w_forget, "forget_bias": forget_bias, "norm_attn": norm_attn, "w_gate": w_gate, "w_up": w_up, "w_down": w_down, "norm_ffn": norm_ffn, "cotangent": cotangent}


EPSILON = 1e-06

@jax.custom_vjp
def low(v):
    return lax.optimization_barrier(v.astype(jnp.bfloat16)).astype(jnp.float32)

@jax.custom_vjp
def low_back(v):
    return v

def low_keep(v):
    return (low(v), None)

def low_pass(kept, grad):
    return (grad,)

def back_keep(v):
    return (v, None)

def back_low(kept, grad):
    return (low(grad),)
low.defvjp(low_keep, low_pass)
low_back.defvjp(back_keep, back_low)

def matmul(former, latter):
    return jnp.dot(former, latter, precision=lax.Precision.HIGHEST)

def rms_norm(values, gain_row):
    return values * lax.rsqrt(lax.optimization_barrier(jnp.mean(values * values, axis=-1, keepdims=True)) + EPSILON) * gain_row

def segment_ids(lengths):
    seq_ends = jnp.cumsum(lengths, axis=1)
    position = jnp.arange(TOK_DEV, dtype=jnp.int32)
    return lax.optimization_barrier(jnp.sum((position[None, :, None] >= seq_ends[:, None, :]).astype(jnp.int32), axis=2))

def attend(queries, key_rows, values, decays, segment):
    scores = jnp.einsum('ihd,jhd->hij', queries, key_rows, precision=lax.Precision.HIGHEST) * HD ** (-0.5)
    scores = scores + decays.T[:, :, None] - decays.T[:, None, :]
    scores = low_back(scores)
    position = jnp.arange(TOK_DEV, dtype=jnp.int32)
    allowed = (position[:, None] >= position[None, :]) & (segment[:, None] == segment[None, :])
    scores = jnp.where(allowed[None], scores, -1e+30)
    highest = lax.optimization_barrier(jnp.max(scores, axis=2, keepdims=True))
    weights = jnp.exp(scores - highest)
    attn_probs = low(weights / lax.optimization_barrier(jnp.sum(weights, axis=2, keepdims=True)))
    return jnp.einsum('hij,jhd->ihd', attn_probs, values, precision=lax.Precision.HIGHEST)

def reference(tokens, lengths, w_query, w_key, w_value, w_out, w_forget, forget_bias, norm_attn, w_gate, w_up, w_down, norm_ffn, cotangent):
    segment = segment_ids(lengths)
    live_rows = (segment < SLOTS).astype(jnp.float32).reshape(TOKENS, 1)
    blocks = TOKENS // TOK_DEV
    attend_saved = jax.checkpoint(attend)

    def attend_block(packed):
        return attend_saved(packed[0], packed[1], packed[2], packed[3], packed[4])

    def forward(inputs, w_query, w_key, w_value, w_out, w_forget, forget_bias, norm_attn, w_gate, w_up, w_down, norm_ffn):
        normed = low(rms_norm(inputs, norm_attn))
        queries = low(low_back(matmul(normed, w_query))).reshape(blocks, TOK_DEV, H, HD)
        key_rows = low(low_back(matmul(normed, w_key))).reshape(blocks, TOK_DEV, H, HD)
        values = low(low_back(matmul(normed, w_value))).reshape(blocks, TOK_DEV, H, HD)
        forget = low_back(matmul(normed, w_forget) + forget_bias)
        decays = jnp.cumsum(jax.nn.log_sigmoid(forget).reshape(blocks, TOK_DEV, H), axis=1)
        mixed = lax.map(attend_block, (queries, key_rows, values, decays, segment))
        mixed = low(low_back(mixed.reshape(TOKENS, D)))
        middle = inputs + low_back(matmul(mixed, w_out))
        normed_two = low(rms_norm(middle, norm_ffn))
        gate_pre = low_back(matmul(normed_two, w_gate))
        upward = low_back(matmul(normed_two, w_up))
        hidden = low(jax.nn.silu(gate_pre) * upward)
        return live_rows * (middle + low_back(matmul(hidden, w_down)))
    params = tuple((array_in.astype(jnp.float32) for array_in in (w_query, w_key, w_value, w_out, w_forget, forget_bias, norm_attn, w_gate, w_up, w_down, norm_ffn)))
    output, pullback = jax.vjp(forward, tokens.astype(jnp.float32), *params)
    gradients = pullback(cotangent.astype(jnp.float32))
    return (output.astype(jnp.bfloat16), gradients[0], gradients[1], gradients[2], gradients[3], gradients[4], gradients[5], gradients[6], gradients[7], gradients[8], gradients[9], gradients[10], gradients[11])
```

```python
import functools

import jax
import jax.numpy as jnp
from jax import lax
from jax.experimental import pallas as pl
from jax.experimental.pallas import tpu as pltpu
from jax.sharding import Mesh, PartitionSpec as P

D = 1536
H = 24
HD = 64
FF = 4096
ROWS = 128
SLOTS = 4
EPSILON = 1e-06
SHARD = D // 4
FSHARD = FF // 4
LOCAL_HEADS = H // 4
WIDTH = 3 * SHARD + 128
AXES = ("y", "xh", "z", "xl", "c")
PLANE = ("y", "z")
F32 = jnp.float32
BF16 = jnp.bfloat16


def dot(former, latter, dims):
    return lax.dot_general(former, latter, (dims, ((), ())), preferred_element_type=F32)


AB = ((1,), (0,))
ABT = ((1,), (1,))
ATB = ((0,), (0,))


def exact_dot(former, latter):
    return lax.dot_general(
        former, latter, ((AB), ((), ())), precision=lax.Precision.HIGHEST, preferred_element_type=F32
    )


def attend_mask(lens_ref, block):
    rows = lax.broadcasted_iota(jnp.int32, (ROWS, ROWS), 0)
    cols = lax.broadcasted_iota(jnp.int32, (ROWS, ROWS), 1)
    seg_rows = jnp.zeros((ROWS, ROWS), jnp.int32)
    seg_cols = jnp.zeros((ROWS, ROWS), jnp.int32)
    end = jnp.int32(0)
    for slot in range(SLOTS):
        end = end + lens_ref[block, slot]
        seg_rows = seg_rows + (rows >= end).astype(jnp.int32)
        seg_cols = seg_cols + (cols >= end).astype(jnp.int32)
    return (rows >= cols) & (seg_rows == seg_cols)


def half_masks():
    lane = lax.broadcasted_iota(jnp.int32, (ROWS, 128), 1)
    return lane < HD, lane >= HD


def forward_kernel(
    lens_ref, x_ref, gain_ref, w_ref, bias_ref, wo_ref,
    keep_ref, send_ref, normed_ref, qkv_ref, forget_ref, probs_ref, mixed_ref,
):
    block = pl.program_id(0)
    x = x_ref[...].astype(F32)
    factor = lax.rsqrt(jnp.mean(x * x, axis=1, keepdims=True) + EPSILON)
    normed = (x * factor * gain_ref[...]).astype(BF16)
    normed_ref[...] = normed
    proj = dot(normed, w_ref[...], AB)
    qkv = proj[:, : 3 * SHARD].astype(BF16)
    qkv_ref[...] = qkv
    forget = proj[:, 3 * SHARD :] + bias_ref[...]
    forget_ref[...] = forget
    logs = jax.nn.log_sigmoid(forget)
    rows = lax.broadcasted_iota(jnp.int32, (ROWS, ROWS), 0)
    cols = lax.broadcasted_iota(jnp.int32, (ROWS, ROWS), 1)
    decays = exact_dot((rows >= cols).astype(F32), logs)
    decays_t = decays.T
    allowed = attend_mask(lens_ref, block)
    halves = half_masks()
    parts = []
    for pair in range(LOCAL_HEADS // 2):
        q2 = qkv[:, 128 * pair : 128 * pair + 128]
        k2 = qkv[:, SHARD + 128 * pair : SHARD + 128 * pair + 128]
        v2 = qkv[:, 2 * SHARD + 128 * pair : 2 * SHARD + 128 * pair + 128]
        total = jnp.zeros((ROWS, 128), F32)
        for side in range(2):
            head = 2 * pair + side
            kh = jnp.where(halves[side], k2, jnp.zeros_like(k2))
            vh = jnp.where(halves[side], v2, jnp.zeros_like(v2))
            scores = dot(q2, kh, ABT) * (HD ** (-0.5))
            scores = scores + decays[:, head : head + 1] - decays_t[head : head + 1, :]
            scores = jnp.where(allowed, scores, -1e30)
            highest = jnp.max(scores, axis=1, keepdims=True)
            weights = jnp.exp(scores - highest)
            probs = weights / jnp.sum(weights, axis=1, keepdims=True)
            probs_ref[0, head] = probs
            total = total + dot(probs.astype(BF16), vh, AB)
        parts.append(total.astype(BF16))
    mixed = jnp.concatenate(parts, axis=1)
    mixed_ref[...] = mixed
    partial = dot(mixed, wo_ref[...], AB).astype(BF16)

    @pl.when(block < 2)
    def _():
        keep_ref[...] = partial

    @pl.when(block >= 2)
    def _():
        send_ref[...] = partial


def attention_forward(lens, x, gain, w, bias, wo):
    whole = lambda b: (0, 0)
    row = lambda b: (b, 0)
    return pl.pallas_call(
        forward_kernel,
        grid=(4,),
        in_specs=[
            pl.BlockSpec(memory_space=pltpu.SMEM),
            pl.BlockSpec((ROWS, D), row),
            pl.BlockSpec((1, D), whole),
            pl.BlockSpec((D, WIDTH), whole),
            pl.BlockSpec((1, 128), whole),
            pl.BlockSpec((SHARD, D), whole),
        ],
        out_specs=[
            pl.BlockSpec((ROWS, D), lambda b: (jnp.minimum(b, 1), 0)),
            pl.BlockSpec((ROWS, D), lambda b: (jnp.maximum(b - 2, 0), 0)),
            pl.BlockSpec((ROWS, D), row),
            pl.BlockSpec((ROWS, 3 * SHARD), row),
            pl.BlockSpec((ROWS, 128), row),
            pl.BlockSpec((1, LOCAL_HEADS, ROWS, ROWS), lambda b: (b, 0, 0, 0)),
            pl.BlockSpec((ROWS, SHARD), row),
        ],
        out_shape=[
            jax.ShapeDtypeStruct((2 * ROWS, D), BF16),
            jax.ShapeDtypeStruct((2 * ROWS, D), BF16),
            jax.ShapeDtypeStruct((4 * ROWS, D), BF16),
            jax.ShapeDtypeStruct((4 * ROWS, 3 * SHARD), BF16),
            jax.ShapeDtypeStruct((4 * ROWS, 128), F32),
            jax.ShapeDtypeStruct((4, LOCAL_HEADS, ROWS, ROWS), F32),
            jax.ShapeDtypeStruct((4 * ROWS, SHARD), BF16),
        ],
        compiler_params=pltpu.CompilerParams(vmem_limit_bytes=40 * 1024 * 1024),
        cost_estimate=pl.CostEstimate(
            flops=2 * 4 * ROWS * D * (WIDTH + SHARD), bytes_accessed=16 * 1024 * 1024, transcendentals=400000
        ),
    )(lens, x, gain, w, bias, wo)


def backward_kernel(
    x_ref, gain_ref, gab_ref, wo_ref, qkv_ref, forget_ref, probs_ref, w_ref,
    keep_ref, send_ref, dqkvf_ref, gain_grad_ref,
):
    block = pl.program_id(0)
    gm = dot(gab_ref[...], wo_ref[...], ABT).astype(BF16)
    qkv = qkv_ref[...]
    halves = half_masks()
    lane = lax.broadcasted_iota(jnp.int32, (ROWS, 128), 1)
    rows = lax.broadcasted_iota(jnp.int32, (ROWS, ROWS), 0)
    cols = lax.broadcasted_iota(jnp.int32, (ROWS, ROWS), 1)
    grad_decays = jnp.zeros((ROWS, 128), F32)
    dqs, dks, dvs = [], [], []
    for pair in range(LOCAL_HEADS // 2):
        q2 = qkv[:, 128 * pair : 128 * pair + 128]
        k2 = qkv[:, SHARD + 128 * pair : SHARD + 128 * pair + 128]
        v2 = qkv[:, 2 * SHARD + 128 * pair : 2 * SHARD + 128 * pair + 128]
        g2 = gm[:, 128 * pair : 128 * pair + 128]
        dq = jnp.zeros((ROWS, 128), F32)
        dk = jnp.zeros((ROWS, 128), F32)
        dv = jnp.zeros((ROWS, 128), F32)
        for side in range(2):
            head = 2 * pair + side
            zero = jnp.zeros_like(q2)
            gh = jnp.where(halves[side], g2, zero)
            probs = probs_ref[0, head]
            grad_probs = dot(gh, v2, ABT)
            inner = jnp.sum(probs * grad_probs, axis=1, keepdims=True)
            ds = (probs * (grad_probs - inner)).astype(BF16)
            dq = dq + dot(ds, jnp.where(halves[side], k2, zero), AB)
            dk = dk + dot(ds, jnp.where(halves[side], q2, zero), ATB)
            dv = dv + dot(probs.astype(BF16), gh, ATB)
            pick = (lane == head).astype(BF16)
            grad_decays = grad_decays + dot(ds, pick, AB) - dot(ds, pick, ATB)
        dqs.append((dq * (HD ** (-0.5))).astype(BF16))
        dks.append((dk * (HD ** (-0.5))).astype(BF16))
        dvs.append(dv.astype(BF16))
    grad_logs = exact_dot((rows <= cols).astype(F32), grad_decays)
    grad_forget = (grad_logs * jax.nn.sigmoid(-forget_ref[...])).astype(BF16)
    dqkvf = jnp.concatenate(dqs + dks + dvs + [grad_forget], axis=1)
    dqkvf_ref[...] = dqkvf
    incoming = dot(dqkvf, w_ref[...], ABT)
    x = x_ref[...].astype(F32)
    factor = lax.rsqrt(jnp.mean(x * x, axis=1, keepdims=True) + EPSILON)
    gain_part = jnp.sum(incoming * x * factor, axis=0, keepdims=True)

    @pl.when(block == 0)
    def _():
        gain_grad_ref[...] = gain_part

    @pl.when(block > 0)
    def _():
        gain_grad_ref[...] = gain_grad_ref[...] + gain_part

    low = incoming.astype(BF16)

    @pl.when(block < 2)
    def _():
        keep_ref[...] = low

    @pl.when(block >= 2)
    def _():
        send_ref[...] = low


def attention_backward(x, gain, gab, wo, qkv, forget, probs, w):
    whole = lambda b: (0, 0)
    row = lambda b: (b, 0)
    return pl.pallas_call(
        backward_kernel,
        grid=(4,),
        in_specs=[
            pl.BlockSpec((ROWS, D), row),
            pl.BlockSpec((1, D), whole),
            pl.BlockSpec((ROWS, D), row),
            pl.BlockSpec((SHARD, D), whole),
            pl.BlockSpec((ROWS, 3 * SHARD), row),
            pl.BlockSpec((ROWS, 128), row),
            pl.BlockSpec((1, LOCAL_HEADS, ROWS, ROWS), lambda b: (b, 0, 0, 0)),
            pl.BlockSpec((D, WIDTH), whole),
        ],
        out_specs=[
            pl.BlockSpec((ROWS, D), lambda b: (jnp.minimum(b, 1), 0)),
            pl.BlockSpec((ROWS, D), lambda b: (jnp.maximum(b - 2, 0), 0)),
            pl.BlockSpec((ROWS, WIDTH), row),
            pl.BlockSpec((1, D), whole),
        ],
        out_shape=[
            jax.ShapeDtypeStruct((2 * ROWS, D), BF16),
            jax.ShapeDtypeStruct((2 * ROWS, D), BF16),
            jax.ShapeDtypeStruct((4 * ROWS, WIDTH), BF16),
            jax.ShapeDtypeStruct((1, D), F32),
        ],
        compiler_params=pltpu.CompilerParams(vmem_limit_bytes=40 * 1024 * 1024),
        cost_estimate=pl.CostEstimate(
            flops=2 * 4 * ROWS * D * (WIDTH + SHARD), bytes_accessed=16 * 1024 * 1024, transcendentals=70000
        ),
    )(x, gain, gab, wo, qkv, forget, probs, w)


FBLOCK = 256


def ffn_kernel(
    n2_ref, gb_ref, wg_ref, wu_ref, wd_ref,
    keep_ref, send_ref, hidden_ref, dg_ref, du_ref, total_ref,
):
    step = pl.program_id(0)
    n2 = n2_ref[...]
    wg, wu = wg_ref[...], wu_ref[...]
    gate = dot(n2, wg, AB)
    up = dot(n2, wu, AB)
    grad_hidden = dot(gb_ref[...], wd_ref[...], ABT)
    sig = jax.nn.sigmoid(gate)
    act = gate * sig
    hidden_ref[...] = (act * up).astype(BF16)
    dg = (grad_hidden * up * sig * (1.0 + gate * (1.0 - sig))).astype(BF16)
    du = (grad_hidden * act).astype(BF16)
    dg_ref[...] = dg
    du_ref[...] = du
    part = dot(dg, wg, ABT) + dot(du, wu, ABT)

    @pl.when(step == 0)
    def _():
        total_ref[...] = part

    @pl.when(step > 0)
    def _():
        total_ref[...] = total_ref[...] + part

    @pl.when(step == pl.num_programs(0) - 1)
    def _():
        keep_ref[...] = total_ref[: 2 * ROWS, :].astype(BF16)
        send_ref[...] = total_ref[2 * ROWS :, :].astype(BF16)


def ffn(n2, gb, wgu, wd):
    whole = lambda b: (0, 0)
    col = lambda b: (0, b)
    steps = FSHARD // FBLOCK
    return pl.pallas_call(
        ffn_kernel,
        grid=(steps,),
        in_specs=[
            pl.BlockSpec((4 * ROWS, D), whole),
            pl.BlockSpec((4 * ROWS, D), whole),
            pl.BlockSpec((D, FBLOCK), col),
            pl.BlockSpec((D, FBLOCK), lambda b: (0, steps + b)),
            pl.BlockSpec((FBLOCK, D), lambda b: (b, 0)),
        ],
        out_specs=[
            pl.BlockSpec((2 * ROWS, D), whole),
            pl.BlockSpec((2 * ROWS, D), whole),
            pl.BlockSpec((4 * ROWS, FBLOCK), col),
            pl.BlockSpec((4 * ROWS, FBLOCK), col),
            pl.BlockSpec((4 * ROWS, FBLOCK), col),
        ],
        out_shape=[
            jax.ShapeDtypeStruct((2 * ROWS, D), BF16),
            jax.ShapeDtypeStruct((2 * ROWS, D), BF16),
            jax.ShapeDtypeStruct((4 * ROWS, FSHARD), BF16),
            jax.ShapeDtypeStruct((4 * ROWS, FSHARD), BF16),
            jax.ShapeDtypeStruct((4 * ROWS, FSHARD), BF16),
        ],
        scratch_shapes=[pltpu.VMEM((4 * ROWS, D), F32)],
        compiler_params=pltpu.CompilerParams(vmem_limit_bytes=48 * 1024 * 1024),
        cost_estimate=pl.CostEstimate(
            flops=2 * 4 * ROWS * D * FSHARD * 5, bytes_accessed=18 * 1024 * 1024, transcendentals=4 * ROWS * FSHARD
        ),
    )(n2, gb, wgu, wgu, wd)


def make_body(sizes):
    ny, nxh, nz = sizes
    np_ = ny * nz

    def send(value, move):
        pairs = []
        for y in range(ny):
            for x in range(2 * nxh):
                for z in range(nz):
                    for c in range(2):
                        tx, tc = move(x, c)
                        tx %= 2 * nxh
                        src = (((y * nxh + x // 2) * nz + z) * 2 + x % 2) * 2 + c
                        dst = (((y * nxh + tx // 2) * nz + z) * 2 + tx % 2) * 2 + tc
                        pairs.append((src, dst))
        return lax.ppermute(value, AXES, pairs)

    swap_core = lambda v: send(v, lambda x, c: (x, 1 - c))
    swap_x = lambda v: send(v, lambda x, c: (x ^ 1, c))
    swap_x_cross = lambda v: send(v, lambda x, c: (x ^ 1, 1 - c))
    swap_out = lambda v: send(v, lambda x, c: (x ^ 3, c))
    swap_out_cross = lambda v: send(v, lambda x, c: (x ^ 3, 1 - c))
    x_plus = lambda v: send(v, lambda x, c: (x + 1, c))
    x_minus = lambda v: send(v, lambda x, c: (x - 1, c))
    x_two = lambda v: send(v, lambda x, c: (x + 2, c))

    def exchange_weight(cols_for, j, width, near):
        mine = cols_for(j)
        sister = swap_core(cols_for(j ^ 1))
        same, cross = cols_for(j ^ 2), cols_for(j ^ 3)
        pieces = [
            (j, 0, mine),
            (j ^ 1, 0, sister),
            (j ^ 2, 0, swap_x(same[:near])),
            (j ^ 3, 0, swap_x_cross(cross[:near])),
            (j ^ 2, near, swap_out(same[near:])),
            (j ^ 3, near, swap_out_cross(cross[near:])),
        ]
        out = jnp.zeros((D, width), BF16)
        for owner, offset, piece in pieces:
            out = lax.dynamic_update_slice(out, piece, (owner * SHARD + offset, 0))
        return out

    def combine(keep, received):
        return (keep.astype(F32) + received.astype(F32)).astype(BF16)

    def all_reduce_rows(keep, sent):
        chip = combine(keep, swap_core(sent))
        other = swap_x(chip)
        other = jnp.concatenate([other[ROWS:], other[:ROWS]], axis=0)
        return chip.astype(F32) + other.astype(F32)

    def reduce_rows(keep, sent):
        chip = combine(keep, swap_core(sent))
        return chip[:ROWS].astype(F32) + swap_x(chip[ROWS:]).astype(F32)

    def reorder(blocks, j):
        return jnp.concatenate(
            [lax.dynamic_index_in_dim(blocks, j ^ r, 0, keepdims=True) for r in range(4)], axis=0
        )

    def spread(pieces, j):
        rel = reorder(pieces, j)
        sister = swap_core(jnp.stack([rel[1], rel[3]]))
        far = jnp.stack([rel[2], sister[1]])
        near = jnp.stack([rel[0], sister[0]])
        a, b, t = x_plus(far), x_minus(far), x_two(near)
        got = jnp.concatenate([combine(near, t), combine(a, b)], axis=0)
        return reorder(got, j)

    def body(
        tokens, lengths, w_query, w_key, w_value, w_out, w_forget, forget_bias, norm_attn,
        w_gate, w_up, w_down, norm_ffn, cotangent,
    ):
        j = lax.axis_index("xl") * 2 + lax.axis_index("c")

        small = jnp.concatenate([norm_attn, norm_ffn, lengths[0].astype(BF16)])
        small = jnp.pad(small[None], ((0, 15), (0, D - small.shape[0])))
        packed = jnp.concatenate([tokens, small], axis=0)
        pair = jnp.stack([packed, swap_x(packed)])
        packed_all = jnp.concatenate([pair, swap_core(pair)], axis=0)
        x_rows = packed_all[:, :ROWS].reshape(4 * ROWS, D)
        small_all = packed_all[:, ROWS]
        lens = small_all[:, 2 * SHARD : 2 * SHARD + SLOTS].astype(jnp.int32)
        by_device = jnp.stack([small_all[0], small_all[2], small_all[1], small_all[3]])
        by_device = reorder(by_device, j).astype(F32)
        gain_one = by_device[:, :SHARD].reshape(1, D)
        gain_two = by_device[:, SHARD : 2 * SHARD].reshape(1, D)
        bias = jnp.pad(forget_bias.astype(F32), (0, 128 - LOCAL_HEADS))[None]

        def qkvf_for(i):
            cols = [lax.dynamic_slice_in_dim(w, i * SHARD, SHARD, 1) for w in (w_query, w_key, w_value)]
            part = lax.dynamic_slice_in_dim(w_forget, i * LOCAL_HEADS, LOCAL_HEADS, 1)
            return jnp.concatenate(cols + [jnp.pad(part, ((0, 0), (0, 128 - LOCAL_HEADS)))], axis=1)

        def gate_up_for(i):
            return jnp.concatenate(
                [lax.dynamic_slice_in_dim(w, i * FSHARD, FSHARD, 1) for w in (w_gate, w_up)], axis=1
            )

        w_qkvf = exchange_weight(qkvf_for, j, WIDTH, SHARD // 2)
        w_gate_up = exchange_weight(gate_up_for, j, 2 * FSHARD, SHARD // 3)

        cot_pair = jnp.stack([cotangent, swap_x(cotangent)])
        cot_rows = jnp.concatenate([cot_pair, swap_core(cot_pair)], axis=0).reshape(4 * ROWS, D)
        live = (jnp.arange(ROWS)[None, :] < jnp.sum(lens, axis=1, keepdims=True)).reshape(4 * ROWS, 1)
        grad_branch = jnp.where(live, cot_rows, jnp.zeros_like(cot_rows))

        keep, sent, normed, qkv, forget, probs, mixed = attention_forward(
            lens, x_rows, gain_one, w_qkvf, bias, w_out
        )
        half = x_rows[: 2 * ROWS].astype(F32)
        middle = half + all_reduce_rows(keep, sent)
        factor_two = lax.rsqrt(jnp.mean(middle * middle, axis=1, keepdims=True) + EPSILON)
        n2_half = (middle * factor_two * gain_two).astype(BF16)
        n2 = jnp.concatenate([n2_half, swap_core(n2_half)], axis=0)

        keep, sent, hidden, dgate, dup = ffn(n2, grad_branch, w_gate_up, w_down)
        incoming_two = all_reduce_rows(keep, sent)
        scaled = incoming_two * gain_two
        inner = jnp.mean(scaled * middle, axis=1, keepdims=True)
        grad_middle = grad_branch[: 2 * ROWS].astype(F32) + (
            scaled * factor_two - middle * (factor_two * factor_two * factor_two) * inner
        )
        gain_two_part = 0.5 * jnp.sum(incoming_two * middle * factor_two, axis=0)
        gab_half = grad_middle.astype(BF16)
        gab = jnp.concatenate([gab_half, swap_core(gab_half)], axis=0)

        g_down = dot(hidden, grad_branch, ATB).astype(BF16)
        g_gate = dot(n2, dgate, ATB).astype(BF16)
        g_up = dot(n2, dup, ATB).astype(BF16)
        down = dot(hidden, w_down, AB).astype(BF16)
        branch = reduce_rows(down[: 2 * ROWS], down[2 * ROWS :])
        output = jnp.where(live[:ROWS], middle[:ROWS] + branch, 0.0).astype(BF16)

        def plane_sum(parts):
            return lax.psum_scatter(parts, PLANE, scatter_dimension=0, tiled=True)

        def plane_gather(part):
            return lax.all_gather(part, PLANE, axis=0, tiled=True)

        rows_of, cols_of = SHARD // ny, FSHARD // nz

        def plane_split(g):
            g = g.reshape(4, ny, rows_of, nz, cols_of)
            return g.transpose(1, 3, 0, 2, 4).reshape(np_, 4, rows_of, cols_of)

        down_piece = plane_sum(g_down)
        down_piece = combine(down_piece, x_two(down_piece))
        gu_parts = jnp.concatenate([plane_split(g_gate), plane_split(g_up)], axis=3)
        gu_piece = plane_sum(gu_parts.reshape(np_ * 4 * rows_of, 2 * cols_of))
        gu_piece = spread(gu_piece.reshape(4, rows_of, 2 * cols_of), j)

        keep, sent, dqkvf, gain_one_part = attention_backward(
            x_rows, gain_one, gab, w_out, qkv, forget, probs, w_qkvf
        )
        own = x_rows[:ROWS].astype(F32)
        factor_one = lax.rsqrt(jnp.mean(own * own, axis=1, keepdims=True) + EPSILON)
        scaled = reduce_rows(keep, sent) * gain_one
        inner = jnp.mean(scaled * own, axis=1, keepdims=True)
        grad_tokens = grad_middle[:ROWS] + (
            scaled * factor_one - own * (factor_one * factor_one * factor_one) * inner
        )
        g_out = dot(mixed, gab, ATB).astype(BF16)
        g_qkvf = dot(normed, dqkvf, ATB)
        bias_part = jnp.sum(dqkvf[:, 3 * SHARD : 3 * SHARD + LOCAL_HEADS].astype(F32), axis=0)
        extra = jnp.concatenate(
            [
                g_qkvf[:, 3 * SHARD : 3 * SHARD + LOCAL_HEADS],
                gain_one_part.reshape(D, 1),
                gain_two_part.reshape(D, 1),
                jnp.broadcast_to(bias_part[None], (D, LOCAL_HEADS)),
            ],
            axis=1,
        )
        extra = jnp.pad(extra, ((0, 0), (0, 128 - extra.shape[1])))
        g_qkvf = jnp.concatenate([g_qkvf[:, : 3 * SHARD], extra], axis=1).astype(BF16)
        out_rows = SHARD // np_
        g_qkvf = g_qkvf.reshape(4, np_, out_rows, WIDTH).transpose(1, 0, 2, 3)
        out_piece = plane_sum(g_out)
        qkvf_piece = plane_sum(g_qkvf.reshape(D, WIDTH))
        out_piece = combine(out_piece, x_two(out_piece))
        qkvf_piece = spread(qkvf_piece.reshape(4, out_rows, WIDTH), j)

        grad_down = plane_gather(down_piece).astype(F32)
        gu = plane_gather(gu_piece.reshape(4 * rows_of, 2 * cols_of)).reshape(ny, nz, 4, rows_of, 2, cols_of)
        gu = gu.transpose(4, 0, 3, 2, 1, 5).astype(F32)
        grad_gate = gu[0].reshape(SHARD, FF)
        grad_up = gu[1].reshape(SHARD, FF)
        grad_out = plane_gather(out_piece).astype(F32)
        rows = plane_gather(qkvf_piece.reshape(4 * out_rows, WIDTH))
        rows = rows.reshape(np_, 4, out_rows, WIDTH).transpose(0, 2, 1, 3).reshape(SHARD, 4, WIDTH).astype(F32)
        grad_query = rows[:, :, :SHARD].reshape(SHARD, D)
        grad_key = rows[:, :, SHARD : 2 * SHARD].reshape(SHARD, D)
        grad_value = rows[:, :, 2 * SHARD : 3 * SHARD].reshape(SHARD, D)
        tail = rows[:, :, 3 * SHARD :]
        grad_forget = tail[:, :, :LOCAL_HEADS].reshape(SHARD, H)
        grad_norm_attn = jnp.sum(tail[:, :, LOCAL_HEADS], axis=1)
        grad_norm_ffn = jnp.sum(tail[:, :, LOCAL_HEADS + 1], axis=1)
        grad_bias = lax.dynamic_index_in_dim(tail[0], j, 0, keepdims=False)[
            LOCAL_HEADS + 2 : 2 * LOCAL_HEADS + 2
        ]
        return (
            output, grad_tokens, grad_query, grad_key, grad_value, grad_out, grad_forget, grad_bias,
            grad_norm_attn, grad_gate, grad_up, grad_down, grad_norm_ffn,
        )

    return body


SIZES = {32: (4, 2, 4), 4: (2, 2, 1)}


def solution(mesh):
    sizes = SIZES[mesh.shape["wide"]]
    ny, nxh, nz = sizes
    fine = Mesh(mesh.devices.reshape(ny, nxh, nz, 2, 2), AXES)
    rows, shard, vector = P(AXES, None), P(("xl", "c"), None), P(("xl", "c"))
    return jax.shard_map(
        make_body(sizes),
        mesh=fine,
        in_specs=(
            rows, rows, shard, shard, shard, shard, shard, vector, vector, shard, shard, shard, vector, rows,
        ),
        out_specs=(
            rows, rows, shard, shard, shard, shard, shard, vector, vector, shard, shard, shard, vector,
        ),
        check_vma=False,
    )
```

```python
import functools

import jax
import jax.numpy as jnp
from jax import lax
from jax.experimental import pallas as pl
from jax.experimental.pallas import tpu as pltpu
from jax.sharding import Mesh, PartitionSpec as P

D = 1536
H = 24
HD = 64
FF = 4096
ROWS = 128
SLOTS = 4
EPSILON = 1e-06
SHARD = D // 4
FSHARD = FF // 4
LOCAL_HEADS = H // 4
WIDTH = 3 * SHARD + 128
AXES = ("y", "xh", "z", "xl", "c")
PLANE = ("y", "z")
F32 = jnp.float32
BF16 = jnp.bfloat16


def dot(former, latter, dims):
    return lax.dot_general(former, latter, (dims, ((), ())), preferred_element_type=F32)


AB = ((1,), (0,))
ABT = ((1,), (1,))
ATB = ((0,), (0,))


def exact_dot(former, latter):
    return lax.dot_general(
        former, latter, ((AB), ((), ())), precision=lax.Precision.HIGHEST, preferred_element_type=F32
    )


def attend_mask(lens_ref, block):
    rows = lax.broadcasted_iota(jnp.int32, (ROWS, ROWS), 0)
    cols = lax.broadcasted_iota(jnp.int32, (ROWS, ROWS), 1)
    seg_rows = jnp.zeros((ROWS, ROWS), jnp.int32)
    seg_cols = jnp.zeros((ROWS, ROWS), jnp.int32)
    end = jnp.int32(0)
    for slot in range(SLOTS):
        end = end + lens_ref[block, slot]
        seg_rows = seg_rows + (rows >= end).astype(jnp.int32)
        seg_cols = seg_cols + (cols >= end).astype(jnp.int32)
    return (rows >= cols) & (seg_rows == seg_cols)


def half_masks():
    lane = lax.broadcasted_iota(jnp.int32, (ROWS, 128), 1)
    return lane < HD, lane >= HD


def forward_kernel(
    lens_ref, x_ref, gain_ref, w_ref, bias_ref, wo_ref,
    keep_ref, send_ref, normed_ref, qkv_ref, forget_ref, probs_ref, mixed_ref,
):
    block = pl.program_id(0)
    x = x_ref[...].astype(F32)
    factor = lax.rsqrt(jnp.mean(x * x, axis=1, keepdims=True) + EPSILON)
    normed = (x * factor * gain_ref[...]).astype(BF16)
    normed_ref[...] = normed
    proj = dot(normed, w_ref[...], AB)
    qkv = proj[:, : 3 * SHARD].astype(BF16)
    qkv_ref[...] = qkv
    forget = proj[:, 3 * SHARD :] + bias_ref[...]
    forget_ref[...] = forget
    logs = jax.nn.log_sigmoid(forget)
    rows = lax.broadcasted_iota(jnp.int32, (ROWS, ROWS), 0)
    cols = lax.broadcasted_iota(jnp.int32, (ROWS, ROWS), 1)
    decays = exact_dot((rows >= cols).astype(F32), logs)
    decays_t = decays.T
    allowed = attend_mask(lens_ref, block)
    halves = half_masks()
    parts = []
    for pair in range(LOCAL_HEADS // 2):
        q2 = qkv[:, 128 * pair : 128 * pair + 128]
        k2 = qkv[:, SHARD + 128 * pair : SHARD + 128 * pair + 128]
        v2 = qkv[:, 2 * SHARD + 128 * pair : 2 * SHARD + 128 * pair + 128]
        total = jnp.zeros((ROWS, 128), F32)
        for side in range(2):
            head = 2 * pair + side
            kh = jnp.where(halves[side], k2, jnp.zeros_like(k2))
            vh = jnp.where(halves[side], v2, jnp.zeros_like(v2))
            scores = dot(q2, kh, ABT) * (HD ** (-0.5))
            scores = scores + decays[:, head : head + 1] - decays_t[head : head + 1, :]
            scores = jnp.where(allowed, scores, -1e30)
            highest = jnp.max(scores, axis=1, keepdims=True)
            weights = jnp.exp(scores - highest)
            probs = weights / jnp.sum(weights, axis=1, keepdims=True)
            probs_ref[0, head] = probs
            total = total + dot(probs.astype(BF16), vh, AB)
        parts.append(total.astype(BF16))
    mixed = jnp.concatenate(parts, axis=1)
    mixed_ref[...] = mixed
    partial = dot(mixed, wo_ref[...], AB).astype(BF16)

    @pl.when(block < 2)
    def _():
        keep_ref[...] = partial

    @pl.when(block >= 2)
    def _():
        send_ref[...] = partial


def attention_forward(lens, x, gain, w, bias, wo):
    whole = lambda b: (0, 0)
    row = lambda b: (b, 0)
    return pl.pallas_call(
        forward_kernel,
        grid=(4,),
        in_specs=[
            pl.BlockSpec(memory_space=pltpu.SMEM),
            pl.BlockSpec((ROWS, D), row),
            pl.BlockSpec((1, D), whole),
            pl.BlockSpec((D, WIDTH), whole),
            pl.BlockSpec((1, 128), whole),
            pl.BlockSpec((SHARD, D), whole),
        ],
        out_specs=[
            pl.BlockSpec((ROWS, D), lambda b: (jnp.minimum(b, 1), 0)),
            pl.BlockSpec((ROWS, D), lambda b: (jnp.maximum(b - 2, 0), 0)),
            pl.BlockSpec((ROWS, D), row),
            pl.BlockSpec((ROWS, 3 * SHARD), row),
            pl.BlockSpec((ROWS, 128), row),
            pl.BlockSpec((1, LOCAL_HEADS, ROWS, ROWS), lambda b: (b, 0, 0, 0)),
            pl.BlockSpec((ROWS, SHARD), row),
        ],
        out_shape=[
            jax.ShapeDtypeStruct((2 * ROWS, D), BF16),
            jax.ShapeDtypeStruct((2 * ROWS, D), BF16),
            jax.ShapeDtypeStruct((4 * ROWS, D), BF16),
            jax.ShapeDtypeStruct((4 * ROWS, 3 * SHARD), BF16),
            jax.ShapeDtypeStruct((4 * ROWS, 128), F32),
            jax.ShapeDtypeStruct((4, LOCAL_HEADS, ROWS, ROWS), F32),
            jax.ShapeDtypeStruct((4 * ROWS, SHARD), BF16),
        ],
        compiler_params=pltpu.CompilerParams(vmem_limit_bytes=40 * 1024 * 1024),
        cost_estimate=pl.CostEstimate(
            flops=2 * 4 * ROWS * D * (WIDTH + SHARD), bytes_accessed=16 * 1024 * 1024, transcendentals=400000
        ),
    )(lens, x, gain, w, bias, wo)


def backward_kernel(
    x_ref, gain_ref, gab_ref, wo_ref, qkv_ref, forget_ref, probs_ref, w_ref,
    keep_ref, send_ref, dqkvf_ref, gain_grad_ref,
):
    block = pl.program_id(0)
    gm = dot(gab_ref[...], wo_ref[...], ABT).astype(BF16)
    qkv = qkv_ref[...]
    halves = half_masks()
    lane = lax.broadcasted_iota(jnp.int32, (ROWS, 128), 1)
    rows = lax.broadcasted_iota(jnp.int32, (ROWS, ROWS), 0)
    cols = lax.broadcasted_iota(jnp.int32, (ROWS, ROWS), 1)
    grad_decays = jnp.zeros((ROWS, 128), F32)
    dqs, dks, dvs = [], [], []
    for pair in range(LOCAL_HEADS // 2):
        q2 = qkv[:, 128 * pair : 128 * pair + 128]
        k2 = qkv[:, SHARD + 128 * pair : SHARD + 128 * pair + 128]
        v2 = qkv[:, 2 * SHARD + 128 * pair : 2 * SHARD + 128 * pair + 128]
        g2 = gm[:, 128 * pair : 128 * pair + 128]
        dq = jnp.zeros((ROWS, 128), F32)
        dk = jnp.zeros((ROWS, 128), F32)
        dv = jnp.zeros((ROWS, 128), F32)
        for side in range(2):
            head = 2 * pair + side
            zero = jnp.zeros_like(q2)
            gh = jnp.where(halves[side], g2, zero)
            probs = probs_ref[0, head]
            grad_probs = dot(gh, v2, ABT)
            inner = jnp.sum(probs * grad_probs, axis=1, keepdims=True)
            ds = (probs * (grad_probs - inner)).astype(BF16)
            dq = dq + dot(ds, jnp.where(halves[side], k2, zero), AB)
            dk = dk + dot(ds, jnp.where(halves[side], q2, zero), ATB)
            dv = dv + dot(probs.astype(BF16), gh, ATB)
            pick = (lane == head).astype(BF16)
            grad_decays = grad_decays + dot(ds, pick, AB) - dot(ds, pick, ATB)
        dqs.append((dq * (HD ** (-0.5))).astype(BF16))
        dks.append((dk * (HD ** (-0.5))).astype(BF16))
        dvs.append(dv.astype(BF16))
    grad_logs = exact_dot((rows <= cols).astype(F32), grad_decays)
    grad_forget = (grad_logs * jax.nn.sigmoid(-forget_ref[...])).astype(BF16)
    dqkvf = jnp.concatenate(dqs + dks + dvs + [grad_forget], axis=1)
    dqkvf_ref[...] = dqkvf
    incoming = dot(dqkvf, w_ref[...], ABT)
    x = x_ref[...].astype(F32)
    factor = lax.rsqrt(jnp.mean(x * x, axis=1, keepdims=True) + EPSILON)
    gain_part = jnp.sum(incoming * x * factor, axis=0, keepdims=True)

    @pl.when(block == 0)
    def _():
        gain_grad_ref[...] = gain_part

    @pl.when(block > 0)
    def _():
        gain_grad_ref[...] = gain_grad_ref[...] + gain_part

    low = incoming.astype(BF16)

    @pl.when(block < 2)
    def _():
        keep_ref[...] = low

    @pl.when(block >= 2)
    def _():
        send_ref[...] = low


def attention_backward(x, gain, gab, wo, qkv, forget, probs, w):
    whole = lambda b: (0, 0)
    row = lambda b: (b, 0)
    return pl.pallas_call(
        backward_kernel,
        grid=(4,),
        in_specs=[
            pl.BlockSpec((ROWS, D), row),
            pl.BlockSpec((1, D), whole),
            pl.BlockSpec((ROWS, D), row),
            pl.BlockSpec((SHARD, D), whole),
            pl.BlockSpec((ROWS, 3 * SHARD), row),
            pl.BlockSpec((ROWS, 128), row),
            pl.BlockSpec((1, LOCAL_HEADS, ROWS, ROWS), lambda b: (b, 0, 0, 0)),
            pl.BlockSpec((D, WIDTH), whole),
        ],
        out_specs=[
            pl.BlockSpec((ROWS, D), lambda b: (jnp.minimum(b, 1), 0)),
            pl.BlockSpec((ROWS, D), lambda b: (jnp.maximum(b - 2, 0), 0)),
            pl.BlockSpec((ROWS, WIDTH), row),
            pl.BlockSpec((1, D), whole),
        ],
        out_shape=[
            jax.ShapeDtypeStruct((2 * ROWS, D), BF16),
            jax.ShapeDtypeStruct((2 * ROWS, D), BF16),
            jax.ShapeDtypeStruct((4 * ROWS, WIDTH), BF16),
            jax.ShapeDtypeStruct((1, D), F32),
        ],
        compiler_params=pltpu.CompilerParams(vmem_limit_bytes=40 * 1024 * 1024),
        cost_estimate=pl.CostEstimate(
            flops=2 * 4 * ROWS * D * (WIDTH + SHARD), bytes_accessed=16 * 1024 * 1024, transcendentals=70000
        ),
    )(x, gain, gab, wo, qkv, forget, probs, w)


FBLOCK = 256


def ffn_kernel(
    n2_ref, gb_ref, wg_ref, wu_ref, wd_ref,
    keep_ref, send_ref, hidden_ref, dg_ref, du_ref, total_ref,
):
    step = pl.program_id(0)
    n2 = n2_ref[...]
    wg, wu = wg_ref[...], wu_ref[...]
    gate = dot(n2, wg, AB)
    up = dot(n2, wu, AB)
    grad_hidden = dot(gb_ref[...], wd_ref[...], ABT)
    sig = jax.nn.sigmoid(gate)
    act = gate * sig
    hidden_ref[...] = (act * up).astype(BF16)
    dg = (grad_hidden * up * sig * (1.0 + gate * (1.0 - sig))).astype(BF16)
    du = (grad_hidden * act).astype(BF16)
    dg_ref[...] = dg
    du_ref[...] = du
    part = dot(dg, wg, ABT) + dot(du, wu, ABT)

    @pl.when(step == 0)
    def _():
        total_ref[...] = part

    @pl.when(step > 0)
    def _():
        total_ref[...] = total_ref[...] + part

    @pl.when(step == pl.num_programs(0) - 1)
    def _():
        keep_ref[...] = total_ref[: 2 * ROWS, :].astype(BF16)
        send_ref[...] = total_ref[2 * ROWS :, :].astype(BF16)


def ffn(n2, gb, wgu, wd):
    whole = lambda b: (0, 0)
    col = lambda b: (0, b)
    steps = FSHARD // FBLOCK
    return pl.pallas_call(
        ffn_kernel,
        grid=(steps,),
        in_specs=[
            pl.BlockSpec((4 * ROWS, D), whole),
            pl.BlockSpec((4 * ROWS, D), whole),
            pl.BlockSpec((D, FBLOCK), col),
            pl.BlockSpec((D, FBLOCK), lambda b: (0, steps + b)),
            pl.BlockSpec((FBLOCK, D), lambda b: (b, 0)),
        ],
        out_specs=[
            pl.BlockSpec((2 * ROWS, D), whole),
            pl.BlockSpec((2 * ROWS, D), whole),
            pl.BlockSpec((4 * ROWS, FBLOCK), col),
            pl.BlockSpec((4 * ROWS, FBLOCK), col),
            pl.BlockSpec((4 * ROWS, FBLOCK), col),
        ],
        out_shape=[
            jax.ShapeDtypeStruct((2 * ROWS, D), BF16),
            jax.ShapeDtypeStruct((2 * ROWS, D), BF16),
            jax.ShapeDtypeStruct((4 * ROWS, FSHARD), BF16),
            jax.ShapeDtypeStruct((4 * ROWS, FSHARD), BF16),
            jax.ShapeDtypeStruct((4 * ROWS, FSHARD), BF16),
        ],
        scratch_shapes=[pltpu.VMEM((4 * ROWS, D), F32)],
        compiler_params=pltpu.CompilerParams(vmem_limit_bytes=48 * 1024 * 1024),
        cost_estimate=pl.CostEstimate(
            flops=2 * 4 * ROWS * D * FSHARD * 5, bytes_accessed=18 * 1024 * 1024, transcendentals=4 * ROWS * FSHARD
        ),
    )(n2, gb, wgu, wgu, wd)


EVEN = (0, 3, 1, 2)
ODD = (0, 1, 3, 2)
PARTS = (("z", EVEN), ("z", ODD), ("y", EVEN), ("y", ODD))
STEPS = {EVEN: (1, 3), ODD: (3, 1)}


def piece_of(part, index):
    first, order = PARTS[part]
    a, b = order[index // 4], order[index % 4]
    return (b, a) if first == "z" else (a, b)


def place(outs, part, index):
    return outs[2 * part + index // 8], index % 8


FUNITS = 36
QUNITS = ((0, 4), (4, 8), (8, 12), (12, 15))
OUNITS = ((0, 4), (4, 8), (8, 12), (12, 18))
AUNITS = tuple(4 * (q1 - q0) + (o1 - o0) for (q0, q1), (o0, o1) in zip(QUNITS, OUNITS))
NQ, NO = 240, 288


def ffn_grad_kernel(at_ref, n2_ref, gb_ref, hidden_ref, dg_ref, du_ref, *rest):
    outs, (gate_ref, up_ref, down_ref) = rest[:8], rest[8:]
    y, z, j = at_ref[0], at_ref[1], at_ref[2]
    n2 = n2_ref[...]
    for rz in range(4):
        lanes = pl.ds(pl.multiple_of((rz ^ z) * FBLOCK, FBLOCK), FBLOCK)
        gate_ref[...] = dot(n2, dg_ref[:, lanes], ATB).astype(BF16).reshape(16, 96, FBLOCK)
        up_ref[...] = dot(n2, du_ref[:, lanes], ATB).astype(BF16).reshape(16, 96, FBLOCK)
        down_ref[...] = dot(hidden_ref[:, lanes], gb_ref[...], ATB).astype(BF16).reshape(4, 64, D)
        for part in range(4):
            source = (gate_ref, gate_ref, up_ref, up_ref)[part]
            left = part % 2 * 128
            for index in range(16):
                ry, own_rz = piece_of(part, index)
                if own_rz != rz:
                    continue
                out, slot = place(outs, part, index)
                py = ry ^ y
                for r in range(4):
                    block = source[(r ^ j) * 4 + py, :, left : left + 128]
                    out[slot, 6 * r : 6 * r + 6] = block.reshape(6, 16, 128)
                for t in range(3):
                    lane = 384 * part + 128 * t
                    block = down_ref[py, :, lane : lane + 128]
                    out[slot, 24 + 4 * t : 28 + 4 * t] = block.reshape(4, 16, 128)


def ffn_gradients(at, n2, gb, hidden, dg, du):
    vmem = pl.BlockSpec(memory_space=pltpu.VMEM)
    return pl.pallas_call(
        ffn_grad_kernel,
        in_specs=[pl.BlockSpec(memory_space=pltpu.SMEM)] + [vmem] * 5,
        out_specs=[vmem] * 8,
        out_shape=[jax.ShapeDtypeStruct((8, FUNITS, 16, 128), BF16)] * 8,
        scratch_shapes=[
            pltpu.VMEM((16, 96, FBLOCK), BF16),
            pltpu.VMEM((16, 96, FBLOCK), BF16),
            pltpu.VMEM((4, 64, D), BF16),
        ],
        compiler_params=pltpu.CompilerParams(vmem_limit_bytes=48 * 1024 * 1024),
        cost_estimate=pl.CostEstimate(
            flops=2 * 4 * ROWS * D * FSHARD * 3, bytes_accessed=16 * 1024 * 1024, transcendentals=0
        ),
    )(at, n2, gb, hidden, dg, du)


def ffn_unpack_kernel(at_ref, *refs):
    ins, (gate_ref, up_ref, down_ref) = refs[:8], refs[8:]
    y, z, j = at_ref[0], at_ref[1], at_ref[2]
    for part in range(4):
        target = (gate_ref, gate_ref, up_ref, up_ref)[part]
        for index in range(16):
            ry, rz = piece_of(part, index)
            source, slot = place(ins, part, index)
            py, pz = ry ^ y, rz ^ z
            rows = pl.ds(pl.multiple_of(py * 96, 32), 96)
            for r in range(4):
                left = (r ^ j) * FSHARD + pz * FBLOCK + part % 2 * 128
                block = source[slot, 6 * r : 6 * r + 6].reshape(96, 128)
                target[rows, pl.ds(pl.multiple_of(left, 128), 128)] = block.astype(F32)
            rows = pl.ds(pl.multiple_of(pz * 256 + py * 64, 64), 64)
            for t in range(3):
                left = 384 * part + 128 * t
                block = source[slot, 24 + 4 * t : 28 + 4 * t].reshape(64, 128)
                down_ref[rows, left : left + 128] = block.astype(F32)


def ffn_unpack(at, pieces):
    vmem = pl.BlockSpec(memory_space=pltpu.VMEM)
    return pl.pallas_call(
        ffn_unpack_kernel,
        in_specs=[pl.BlockSpec(memory_space=pltpu.SMEM)] + [vmem] * 8,
        out_specs=[vmem] * 3,
        out_shape=[
            jax.ShapeDtypeStruct((SHARD, FF), F32),
            jax.ShapeDtypeStruct((SHARD, FF), F32),
            jax.ShapeDtypeStruct((FSHARD, D), F32),
        ],
        compiler_params=pltpu.CompilerParams(vmem_limit_bytes=48 * 1024 * 1024),
        cost_estimate=pl.CostEstimate(flops=0, bytes_accessed=28 * 1024 * 1024, transcendentals=0),
    )(at, *pieces)


def attention_grad_kernel(at_ref, normed_ref, dqkvf_ref, mixed_ref, gab_ref, gains_ref, *rest):
    outs, (q_ref, o_ref) = rest[:8], rest[8:]
    y, z, j = at_ref[0], at_ref[1], at_ref[2]
    dqkvf = dqkvf_ref[...]
    row = lax.broadcasted_iota(jnp.int32, (16, 128), 0)
    lane = lax.broadcasted_iota(jnp.int32, (16, 128), 1)
    pick = (lane == row + LOCAL_HEADS).astype(BF16)
    pick = jnp.where(row < 2, pick, jnp.zeros_like(pick))
    bias = jnp.sum(dqkvf[:, 3 * SHARD :].astype(F32), axis=0, keepdims=True)
    bias = pltpu.roll(bias, 8, 1)
    pieces = [[piece_of(part, index) for index in range(16)] for part in range(4)]
    for r in range(4):
        lanes = pl.ds(pl.multiple_of((r ^ j) * SHARD, SHARD), SHARD)
        grad = dot(normed_ref[:, lanes], dqkvf, ATB)
        extra = grad[:, 3 * SHARD :] + dot(gains_ref[:, lanes], pick, ATB) + bias
        for col in range(9):
            block = grad[:, 128 * col : 128 * col + 128].astype(BF16).reshape(24, 1, 16, 128)
            q_ref[:, col : col + 1] = block
        q_ref[:, 9:10] = extra.astype(BF16).reshape(24, 1, 16, 128)
        for part in range(4):
            lo, hi = QUNITS[part]
            for index in range(16):
                ry, rz = pieces[part][index]
                out, slot = place(outs, part, index)
                p = (ry ^ y) * 4 + (rz ^ z)
                odd = p & 1
                base = (p >> 1) * 3
                for t in range(lo, hi):
                    group = base + jnp.where(odd == 1, (15 + t) // 10, t // 10)
                    col = jnp.where(odd == 1, (15 + t) % 10, t % 10)
                    out[slot, (hi - lo) * r + t - lo] = q_ref[group, col]
    grad = dot(mixed_ref[...], gab_ref[...], ATB)
    for col in range(12):
        o_ref[:, col : col + 1] = grad[:, 128 * col : 128 * col + 128].astype(BF16).reshape(24, 1, 16, 128)
    for part in range(4):
        lo, hi = OUNITS[part]
        first = AUNITS[part] - (hi - lo)
        for index in range(16):
            ry, rz = pieces[part][index]
            out, slot = place(outs, part, index)
            p = (ry ^ y) * 4 + (rz ^ z)
            odd = p & 1
            base = (p >> 1) * 3
            for t in range(lo, hi):
                group = base + jnp.where(odd == 1, (18 + t) // 12, t // 12)
                col = jnp.where(odd == 1, (18 + t) % 12, t % 12)
                out[slot, first + t - lo] = o_ref[group, col]


def attention_gradients(at, normed, dqkvf, mixed, gab, gains):
    vmem = pl.BlockSpec(memory_space=pltpu.VMEM)
    return pl.pallas_call(
        attention_grad_kernel,
        in_specs=[pl.BlockSpec(memory_space=pltpu.SMEM)] + [vmem] * 5,
        out_specs=[vmem] * 8,
        out_shape=[jax.ShapeDtypeStruct((8, AUNITS[i // 2], 16, 128), BF16) for i in range(8)],
        scratch_shapes=[
            pltpu.VMEM((24, 10, 16, 128), BF16),
            pltpu.VMEM((24, 12, 16, 128), BF16),
        ],
        compiler_params=pltpu.CompilerParams(vmem_limit_bytes=48 * 1024 * 1024),
        cost_estimate=pl.CostEstimate(
            flops=2 * 4 * ROWS * D * (WIDTH + SHARD), bytes_accessed=10 * 1024 * 1024, transcendentals=0
        ),
    )(at, normed, dqkvf, mixed, gab, gains)


def attention_unpack_kernel(at_ref, *refs):
    ins, (gq_ref, gk_ref, gv_ref, go_ref, extra_ref, q_ref, o_ref) = refs[:8], refs[8:]
    y, z, j = at_ref[0], at_ref[1], at_ref[2]
    for part in range(4):
        qlo, qhi = QUNITS[part]
        olo, ohi = OUNITS[part]
        for index in range(16):
            ry, rz = piece_of(part, index)
            source, slot = place(ins, part, index)
            p = (ry ^ y) * 4 + (rz ^ z)
            n = qhi - qlo
            for r in range(4):
                q_ref[r ^ j, pl.ds(p * 15 + qlo, n)] = source[slot, n * r : n * r + n]
            o_ref[pl.ds(p * 18 + olo, ohi - olo)] = source[slot, 4 * n : 4 * n + ohi - olo]
    for group in range(24):
        rows = slice(16 * group, 16 * group + 16)
        for device in range(4):
            for col in range(10):
                value = q_ref[device, 10 * group + col].astype(F32)
                target = (gq_ref, gk_ref, gv_ref, extra_ref)[col // 3]
                left = 128 * device if col == 9 else SHARD * device + 128 * (col % 3)
                target[rows, left : left + 128] = value
        for col in range(12):
            go_ref[rows, 128 * col : 128 * col + 128] = o_ref[12 * group + col].astype(F32)


def attention_unpack(at, pieces):
    vmem = pl.BlockSpec(memory_space=pltpu.VMEM)
    return pl.pallas_call(
        attention_unpack_kernel,
        in_specs=[pl.BlockSpec(memory_space=pltpu.SMEM)] + [vmem] * 8,
        out_specs=[vmem] * 5,
        out_shape=[jax.ShapeDtypeStruct((SHARD, D), F32)] * 4 + [jax.ShapeDtypeStruct((SHARD, 512), F32)],
        scratch_shapes=[
            pltpu.VMEM((4, NQ, 16, 128), BF16),
            pltpu.VMEM((NO, 16, 128), BF16),
        ],
        compiler_params=pltpu.CompilerParams(vmem_limit_bytes=48 * 1024 * 1024),
        cost_estimate=pl.CostEstimate(flops=0, bytes_accessed=16 * 1024 * 1024, transcendentals=0),
    )(at, *pieces)


def make_body(sizes):
    ny, nxh, nz = sizes

    def send(value, move):
        pairs = []
        for y in range(ny):
            for x in range(2 * nxh):
                for z in range(nz):
                    for c in range(2):
                        ty, tx, tz, tc = move(y, x, z, c)
                        tx %= 2 * nxh
                        src = (((y * nxh + x // 2) * nz + z) * 2 + x % 2) * 2 + c
                        dst = (((ty * nxh + tx // 2) * nz + tz) * 2 + tx % 2) * 2 + tc
                        pairs.append((src, dst))
        return lax.ppermute(value, AXES, pairs)

    def swap_plane(value, axis, bits):
        if axis == "y":
            return send(value, lambda y, x, z, c: (y ^ bits, x, z, c))
        return send(value, lambda y, x, z, c: (y, x, z ^ bits, c))

    swap_core = lambda v: send(v, lambda y, x, z, c: (y, x, z, 1 - c))
    swap_x = lambda v: send(v, lambda y, x, z, c: (y, x ^ 1, z, c))
    swap_out = lambda v: send(v, lambda y, x, z, c: (y, x ^ 3, z, c))
    x_plus = lambda v: send(v, lambda y, x, z, c: (y, x + 1, z, c))
    x_minus = lambda v: send(v, lambda y, x, z, c: (y, x - 1, z, c))
    x_two = lambda v: send(v, lambda y, x, z, c: (y, x + 2, z, c))

    def exchange_weight(cols_for, j, width, near):
        far = jnp.concatenate([cols_for(j ^ 2), cols_for(j ^ 3)], axis=1)
        inner, outer = swap_x(far[:near]), swap_out(far[near:])
        sister = swap_core(cols_for(j ^ 1))
        cross_inner, cross_outer = swap_core(inner[:, width:]), swap_core(outer[:, width:])
        pieces = [
            (j, 0, cols_for(j)),
            (j ^ 1, 0, sister),
            (j ^ 2, 0, inner[:, :width]),
            (j ^ 2, near, outer[:, :width]),
            (j ^ 3, 0, cross_inner),
            (j ^ 3, near, cross_outer),
        ]
        out = jnp.zeros((D, width), BF16)
        for owner, offset, piece in pieces:
            out = lax.dynamic_update_slice(out, piece, (owner * SHARD + offset, 0))
        return out

    def total(parts):
        return functools.reduce(lambda a, b: a + b, [p.astype(F32) for p in parts])

    def combine(keep, received):
        return total([keep, received]).astype(BF16)

    def all_reduce_rows(keep, sent):
        chip = combine(keep, swap_core(sent))
        other = swap_x(chip)
        other = jnp.concatenate([other[ROWS:], other[:ROWS]], axis=0)
        return chip.astype(F32) + other.astype(F32)

    def reduce_rows(keep, sent):
        chip = combine(keep, swap_core(sent))
        return chip[:ROWS].astype(F32) + swap_x(chip[ROWS:]).astype(F32)

    def moves(part):
        first, order = PARTS[part]
        second = "y" if first == "z" else "z"
        return [(axis, bits) for axis in (first, second) for bits in STEPS[order]]

    def plane_sum(parts):
        held = [[parts[2 * k]] for k in range(4)]
        sending = [parts[2 * k + 1] for k in range(4)]
        for step in range(4):
            half = 4 >> step
            for k in range(4):
                axis, bits = moves(k)[step]
                held[k].append(swap_plane(sending[k], axis, bits))
            for k in range(4):
                if half:
                    sending[k] = total([h[half : 2 * half] for h in held[k]]).astype(BF16)
        return [total([h[:1] for h in held[k]]).astype(BF16)[0] for k in range(4)]

    def plane_gather(pieces):
        out = [p[None] for p in pieces]
        for step in (3, 2, 1, 0):
            got = [swap_plane(out[k], *moves(k)[step]) for k in range(4)]
            if step:
                out = [jnp.concatenate([out[k], got[k]], axis=0) for k in range(4)]
        return [v for k in range(4) for v in (out[k], got[k])]

    def spread(pieces, columns):
        rel = [p[: 4 * n].reshape(4, n, 16, 128) for p, n in zip(pieces, columns)]
        own = [p[4 * n :] for p, n in zip(pieces, columns)]
        sister = swap_core(jnp.concatenate([r[i] for i in (1, 3) for r in rel], axis=0))
        n = sum(columns)
        far = jnp.concatenate([r[2] for r in rel] + [sister[n:]], axis=0)
        near = jnp.concatenate([r[0] for r in rel] + [sister[:n]] + own, axis=0)
        a, b, t = x_plus(far), x_minus(far), x_two(near)
        near, far = combine(near, t), combine(a, b)
        out, at, tail = [], 0, 2 * n
        for p, m in zip(pieces, columns):
            last = p.shape[0] - 4 * m
            blocks = [v[lo + at : lo + at + m] for v in (near, far) for lo in (0, n)]
            out.append(jnp.concatenate(blocks + [near[tail : tail + last]], axis=0))
            at, tail = at + m, tail + last
        return out

    def body(
        tokens, lengths, w_query, w_key, w_value, w_out, w_forget, forget_bias, norm_attn,
        w_gate, w_up, w_down, norm_ffn, cotangent,
    ):
        j = lax.axis_index("xl") * 2 + lax.axis_index("c")
        at = jnp.stack([lax.axis_index("y"), lax.axis_index("z"), j]).astype(jnp.int32)

        small = jnp.concatenate([norm_attn, norm_ffn, lengths[0].astype(BF16)])
        small = jnp.pad(small[None], ((0, 15), (0, D - small.shape[0])))
        packed = jnp.concatenate([tokens, small], axis=0)
        pair = jnp.stack([packed, swap_x(packed)])
        packed_all = jnp.concatenate([pair, swap_core(pair)], axis=0)
        x_rows = packed_all[:, :ROWS].reshape(4 * ROWS, D)
        small_all = packed_all[:, ROWS]
        lens = small_all[:, 2 * SHARD : 2 * SHARD + SLOTS].astype(jnp.int32)
        by_device = jnp.stack([small_all[0], small_all[2], small_all[1], small_all[3]])
        by_device = jnp.concatenate(
            [lax.dynamic_index_in_dim(by_device, j ^ r, 0, keepdims=True) for r in range(4)], axis=0
        ).astype(F32)
        gain_one = by_device[:, :SHARD].reshape(1, D)
        gain_two = by_device[:, SHARD : 2 * SHARD].reshape(1, D)
        bias = jnp.pad(forget_bias.astype(F32), (0, 128 - LOCAL_HEADS))[None]

        def qkvf_for(i):
            cols = [lax.dynamic_slice_in_dim(w, i * SHARD, SHARD, 1) for w in (w_query, w_key, w_value)]
            part = lax.dynamic_slice_in_dim(w_forget, i * LOCAL_HEADS, LOCAL_HEADS, 1)
            return jnp.concatenate(cols + [jnp.pad(part, ((0, 0), (0, 128 - LOCAL_HEADS)))], axis=1)

        def gate_up_for(i):
            return jnp.concatenate(
                [lax.dynamic_slice_in_dim(w, i * FSHARD, FSHARD, 1) for w in (w_gate, w_up)], axis=1
            )

        w_qkvf = exchange_weight(qkvf_for, j, WIDTH, 144)
        w_gate_up = exchange_weight(gate_up_for, j, 2 * FSHARD, SHARD // 3)

        cot_pair = jnp.stack([cotangent, swap_x(cotangent)])
        cot_rows = jnp.concatenate([cot_pair, swap_core(cot_pair)], axis=0).reshape(4 * ROWS, D)
        live = (jnp.arange(ROWS)[None, :] < jnp.sum(lens, axis=1, keepdims=True)).reshape(4 * ROWS, 1)
        grad_branch = jnp.where(live, cot_rows, jnp.zeros_like(cot_rows))

        keep, sent, normed, qkv, forget, probs, mixed = attention_forward(
            lens, x_rows, gain_one, w_qkvf, bias, w_out
        )
        half = x_rows[: 2 * ROWS].astype(F32)
        middle = half + all_reduce_rows(keep, sent)
        factor_two = lax.rsqrt(jnp.mean(middle * middle, axis=1, keepdims=True) + EPSILON)
        n2_half = (middle * factor_two * gain_two).astype(BF16)
        n2 = jnp.concatenate([n2_half, swap_core(n2_half)], axis=0)

        keep, sent, hidden, dgate, dup = ffn(n2, grad_branch, w_gate_up, w_down)
        incoming_two = all_reduce_rows(keep, sent)
        scaled = incoming_two * gain_two
        inner = jnp.mean(scaled * middle, axis=1, keepdims=True)
        grad_middle = grad_branch[: 2 * ROWS].astype(F32) + (
            scaled * factor_two - middle * (factor_two * factor_two * factor_two) * inner
        )
        gain_two_part = 0.5 * jnp.sum(incoming_two * middle * factor_two, axis=0)
        gab_half = grad_middle.astype(BF16)
        gab = jnp.concatenate([gab_half, swap_core(gab_half)], axis=0)

        ffn_pieces = plane_sum(ffn_gradients(at, n2, grad_branch, hidden, dgate, dup))
        ffn_pieces = spread(ffn_pieces, [6] * 4)

        down = dot(hidden, w_down, AB).astype(BF16)
        branch = reduce_rows(down[: 2 * ROWS], down[2 * ROWS :])
        output = jnp.where(live[:ROWS], middle[:ROWS] + branch, 0.0).astype(BF16)

        keep, sent, dqkvf, gain_one_part = attention_backward(
            x_rows, gain_one, gab, w_out, qkv, forget, probs, w_qkvf
        )
        gains = jnp.concatenate([gain_one_part, gain_two_part[None]], axis=0).astype(BF16)
        gains = jnp.pad(gains, ((0, 14), (0, 0)))
        attn_pieces = plane_sum(attention_gradients(at, normed, dqkvf, mixed, gab, gains))
        attn_pieces = spread(attn_pieces, [hi - lo for lo, hi in QUNITS])

        own = x_rows[:ROWS].astype(F32)
        factor_one = lax.rsqrt(jnp.mean(own * own, axis=1, keepdims=True) + EPSILON)
        scaled = reduce_rows(keep, sent) * gain_one
        inner = jnp.mean(scaled * own, axis=1, keepdims=True)
        grad_tokens = grad_middle[:ROWS] + (
            scaled * factor_one - own * (factor_one * factor_one * factor_one) * inner
        )

        grad_gate, grad_up, grad_down = ffn_unpack(at, plane_gather(ffn_pieces))
        grad_query, grad_key, grad_value, grad_out, extra = attention_unpack(at, plane_gather(attn_pieces))
        extra = extra.reshape(SHARD, 4, 128)
        grad_forget = extra[:, :, :LOCAL_HEADS].reshape(SHARD, H)
        grad_norm_attn = jnp.sum(extra[:, :, LOCAL_HEADS], axis=1)
        grad_norm_ffn = jnp.sum(extra[:, :, LOCAL_HEADS + 1], axis=1)
        grad_bias = lax.dynamic_index_in_dim(extra[0], j, 0, keepdims=False)[8 : 8 + LOCAL_HEADS]
        return (
            output, grad_tokens, grad_query, grad_key, grad_value, grad_out, grad_forget, grad_bias,
            grad_norm_attn, grad_gate, grad_up, grad_down, grad_norm_ffn,
        )

    return body


SIZES = {32: (4, 2, 4), 16: (4, 1, 4)}


def solution(mesh):
    sizes = SIZES[mesh.shape["wide"]]
    ny, nxh, nz = sizes
    fine = Mesh(mesh.devices.reshape(ny, nxh, nz, 2, 2), AXES)
    rows, shard, vector = P(AXES, None), P(("xl", "c"), None), P(("xl", "c"))
    return jax.shard_map(
        make_body(sizes),
        mesh=fine,
        in_specs=(
            rows, rows, shard, shard, shard, shard, shard, vector, vector, shard, shard, shard, vector, rows,
        ),
        out_specs=(
            rows, rows, shard, shard, shard, shard, shard, vector, vector, shard, shard, shard, vector,
        ),
        check_vma=False,
    )
```

```python
import functools

import jax
import jax.numpy as jnp
from jax import lax
from jax.experimental import pallas as pl
from jax.experimental.pallas import tpu as pltpu
from jax.sharding import Mesh, PartitionSpec as P

D = 1536
H = 24
HD = 64
FF = 4096
ROWS = 128
SLOTS = 4
EPSILON = 1e-06
SHARD = D // 4
FSHARD = FF // 4
LOCAL_HEADS = H // 4
WIDTH = 3 * SHARD + 128
AXES = ("y", "xh", "z", "xl", "c")
PLANE = ("y", "z")
F32 = jnp.float32
BF16 = jnp.bfloat16


def dot(former, latter, dims):
    return lax.dot_general(former, latter, (dims, ((), ())), preferred_element_type=F32)


AB = ((1,), (0,))
ABT = ((1,), (1,))
ATB = ((0,), (0,))


def exact_dot(former, latter):
    return lax.dot_general(
        former, latter, ((AB), ((), ())), precision=lax.Precision.HIGHEST, preferred_element_type=F32
    )


def attend_mask(lens_ref, block):
    rows = lax.broadcasted_iota(jnp.int32, (ROWS, ROWS), 0)
    cols = lax.broadcasted_iota(jnp.int32, (ROWS, ROWS), 1)
    seg_rows = jnp.zeros((ROWS, ROWS), jnp.int32)
    seg_cols = jnp.zeros((ROWS, ROWS), jnp.int32)
    end = jnp.int32(0)
    for slot in range(SLOTS):
        end = end + lens_ref[block, slot]
        seg_rows = seg_rows + (rows >= end).astype(jnp.int32)
        seg_cols = seg_cols + (cols >= end).astype(jnp.int32)
    return (rows >= cols) & (seg_rows == seg_cols)


def half_masks():
    lane = lax.broadcasted_iota(jnp.int32, (ROWS, 128), 1)
    return lane < HD, lane >= HD


def columns_kernel(at_ref, q_ref, k_ref, v_ref, f_ref, own_ref, far_ref, sister_ref):
    j = at_ref[2]
    forget = jnp.concatenate([f_ref[...].astype(F32), jnp.zeros((SHARD, 128 - H), F32)], axis=1)
    lane = lax.broadcasted_iota(jnp.int32, (SHARD, 128), 1)
    targets = ((0, own_ref, None), (1, sister_ref, 0), (2, far_ref, None), (3, sister_ref, 1))
    for r, ref, row in targets:
        i = r ^ j
        lanes = pl.ds(pl.multiple_of(i * SHARD, SHARD), SHARD)
        mine = pltpu.roll(forget, lax.rem(128 - LOCAL_HEADS * i, 128), 1)
        mine = jnp.where(lane < LOCAL_HEADS, mine, 0.0).astype(BF16)
        first = 0 if row is None else row * SHARD
        rows = slice(first, first + SHARD)
        for n, source in enumerate((q_ref, k_ref, v_ref)):
            ref[rows, SHARD * n : SHARD * n + SHARD] = source[:, lanes]
        ref[rows, 3 * SHARD :] = mine


def columns(at, w_query, w_key, w_value, w_forget):
    vmem = pl.BlockSpec(memory_space=pltpu.VMEM)
    return pl.pallas_call(
        columns_kernel,
        in_specs=[pl.BlockSpec(memory_space=pltpu.SMEM)] + [vmem] * 4,
        out_specs=[vmem] * 3,
        out_shape=[jax.ShapeDtypeStruct((n * SHARD, WIDTH), BF16) for n in (1, 1, 2)],
        compiler_params=pltpu.CompilerParams(vmem_limit_bytes=32 * 1024 * 1024),
        cost_estimate=pl.CostEstimate(flops=0, bytes_accessed=8 * 1024 * 1024, transcendentals=0),
    )(at, w_query, w_key, w_value, w_forget)


def fill(copies):
    copies = [pltpu.make_async_copy(*c) for c in copies]
    for c in copies:
        c.start()
    for c in copies:
        c.wait()


def forward_kernel(
    lens_ref, at_ref, x_ref, gain_ref, bias_ref, wo_ref, own_ref, sister_ref, far_ref, cross_ref, rest_ref,
    keep_ref, send_ref, normed_ref, qkv_ref, forget_ref, probs_ref, mixed_ref, w_ref, sem,
):
    @pl.when(pl.program_id(0) == 0)
    def _():
        j = at_ref[2]

        def rows(r, first, count):
            return w_ref.at[pl.ds(pl.multiple_of((r ^ j) * SHARD + first, 96), count)]

        near = cross_ref.shape[0]
        fill(
            [
                (own_ref, rows(0, 0, SHARD), sem.at[0]),
                (sister_ref.at[pl.ds(0, SHARD)], rows(1, 0, SHARD), sem.at[1]),
                (far_ref, rows(2, 0, SHARD), sem.at[2]),
                (cross_ref, rows(3, 0, near), sem.at[3]),
                (rest_ref, rows(3, near, SHARD - near), sem.at[4]),
            ]
        )

    block = pl.program_id(0)
    x = x_ref[...].astype(F32)
    factor = lax.rsqrt(jnp.mean(x * x, axis=1, keepdims=True) + EPSILON)
    normed = (x * factor * gain_ref[...]).astype(BF16)
    normed_ref[...] = normed
    proj = dot(normed, w_ref[...], AB)
    qkv = proj[:, : 3 * SHARD].astype(BF16)
    qkv_ref[...] = qkv
    forget = proj[:, 3 * SHARD :] + bias_ref[...]
    forget_ref[...] = forget
    logs = jax.nn.log_sigmoid(forget)
    rows = lax.broadcasted_iota(jnp.int32, (ROWS, ROWS), 0)
    cols = lax.broadcasted_iota(jnp.int32, (ROWS, ROWS), 1)
    decays = exact_dot((rows >= cols).astype(F32), logs)
    decays_t = decays.T
    allowed = attend_mask(lens_ref, block)
    halves = half_masks()
    parts = []
    for pair in range(LOCAL_HEADS // 2):
        q2 = qkv[:, 128 * pair : 128 * pair + 128]
        k2 = qkv[:, SHARD + 128 * pair : SHARD + 128 * pair + 128]
        v2 = qkv[:, 2 * SHARD + 128 * pair : 2 * SHARD + 128 * pair + 128]
        total = jnp.zeros((ROWS, 128), F32)
        for side in range(2):
            head = 2 * pair + side
            kh = jnp.where(halves[side], k2, jnp.zeros_like(k2))
            vh = jnp.where(halves[side], v2, jnp.zeros_like(v2))
            scores = dot(q2, kh, ABT) * (HD ** (-0.5))
            scores = scores + decays[:, head : head + 1] - decays_t[head : head + 1, :]
            scores = jnp.where(allowed, scores, -1e30)
            highest = jnp.max(scores, axis=1, keepdims=True)
            weights = jnp.exp(scores - highest)
            probs = weights / jnp.sum(weights, axis=1, keepdims=True)
            probs_ref[0, head] = probs
            total = total + dot(probs.astype(BF16), vh, AB)
        parts.append(total.astype(BF16))
    mixed = jnp.concatenate(parts, axis=1)
    mixed_ref[...] = mixed
    partial = dot(mixed, wo_ref[...], AB).astype(BF16)

    @pl.when(block < 2)
    def _():
        keep_ref[...] = partial

    @pl.when(block >= 2)
    def _():
        send_ref[...] = partial


def attention_forward(lens, at, x, gain, bias, wo, pieces):
    whole = lambda b: (0, 0)
    row = lambda b: (b, 0)
    smem = pl.BlockSpec(memory_space=pltpu.SMEM)
    return pl.pallas_call(
        forward_kernel,
        grid=(4,),
        in_specs=[
            smem,
            smem,
            pl.BlockSpec((ROWS, D), row),
            pl.BlockSpec((1, D), whole),
            pl.BlockSpec((1, 128), whole),
            pl.BlockSpec((SHARD, D), whole),
        ]
        + [pl.BlockSpec(memory_space=pl.ANY)] * 5,
        out_specs=[
            pl.BlockSpec((ROWS, D), lambda b: (jnp.minimum(b, 1), 0)),
            pl.BlockSpec((ROWS, D), lambda b: (jnp.maximum(b - 2, 0), 0)),
            pl.BlockSpec((ROWS, D), row),
            pl.BlockSpec((ROWS, 3 * SHARD), row),
            pl.BlockSpec((ROWS, 128), row),
            pl.BlockSpec((1, LOCAL_HEADS, ROWS, ROWS), lambda b: (b, 0, 0, 0)),
            pl.BlockSpec((ROWS, SHARD), row),
            pl.BlockSpec((D, WIDTH), whole),
        ],
        out_shape=[
            jax.ShapeDtypeStruct((2 * ROWS, D), BF16),
            jax.ShapeDtypeStruct((2 * ROWS, D), BF16),
            jax.ShapeDtypeStruct((4 * ROWS, D), BF16),
            jax.ShapeDtypeStruct((4 * ROWS, 3 * SHARD), BF16),
            jax.ShapeDtypeStruct((4 * ROWS, 128), F32),
            jax.ShapeDtypeStruct((4, LOCAL_HEADS, ROWS, ROWS), F32),
            jax.ShapeDtypeStruct((4 * ROWS, SHARD), BF16),
            jax.ShapeDtypeStruct((D, WIDTH), BF16),
        ],
        scratch_shapes=[pltpu.SemaphoreType.DMA((5,))],
        compiler_params=pltpu.CompilerParams(vmem_limit_bytes=40 * 1024 * 1024),
        cost_estimate=pl.CostEstimate(
            flops=2 * 4 * ROWS * D * (WIDTH + SHARD), bytes_accessed=16 * 1024 * 1024, transcendentals=400000
        ),
    )(lens, at, x, gain, bias, wo, *pieces)


def backward_kernel(
    x_ref, gain_ref, gab_ref, wo_ref, qkv_ref, forget_ref, probs_ref, w_ref,
    keep_ref, send_ref, dqkvf_ref, gain_grad_ref,
):
    block = pl.program_id(0)
    gm = dot(gab_ref[...], wo_ref[...], ABT).astype(BF16)
    qkv = qkv_ref[...]
    halves = half_masks()
    lane = lax.broadcasted_iota(jnp.int32, (ROWS, 128), 1)
    rows = lax.broadcasted_iota(jnp.int32, (ROWS, ROWS), 0)
    cols = lax.broadcasted_iota(jnp.int32, (ROWS, ROWS), 1)
    grad_decays = jnp.zeros((ROWS, 128), F32)
    dqs, dks, dvs = [], [], []
    for pair in range(LOCAL_HEADS // 2):
        q2 = qkv[:, 128 * pair : 128 * pair + 128]
        k2 = qkv[:, SHARD + 128 * pair : SHARD + 128 * pair + 128]
        v2 = qkv[:, 2 * SHARD + 128 * pair : 2 * SHARD + 128 * pair + 128]
        g2 = gm[:, 128 * pair : 128 * pair + 128]
        dq = jnp.zeros((ROWS, 128), F32)
        dk = jnp.zeros((ROWS, 128), F32)
        dv = jnp.zeros((ROWS, 128), F32)
        for side in range(2):
            head = 2 * pair + side
            zero = jnp.zeros_like(q2)
            gh = jnp.where(halves[side], g2, zero)
            probs = probs_ref[0, head]
            grad_probs = dot(gh, v2, ABT)
            inner = jnp.sum(probs * grad_probs, axis=1, keepdims=True)
            ds = (probs * (grad_probs - inner)).astype(BF16)
            dq = dq + dot(ds, jnp.where(halves[side], k2, zero), AB)
            dk = dk + dot(ds, jnp.where(halves[side], q2, zero), ATB)
            dv = dv + dot(probs.astype(BF16), gh, ATB)
            pick = (lane == head).astype(BF16)
            grad_decays = grad_decays + dot(ds, pick, AB) - dot(ds, pick, ATB)
        dqs.append((dq * (HD ** (-0.5))).astype(BF16))
        dks.append((dk * (HD ** (-0.5))).astype(BF16))
        dvs.append(dv.astype(BF16))
    grad_logs = exact_dot((rows <= cols).astype(F32), grad_decays)
    grad_forget = (grad_logs * jax.nn.sigmoid(-forget_ref[...])).astype(BF16)
    dqkvf = jnp.concatenate(dqs + dks + dvs + [grad_forget], axis=1)
    dqkvf_ref[...] = dqkvf
    incoming = dot(dqkvf, w_ref[...], ABT)
    x = x_ref[...].astype(F32)
    factor = lax.rsqrt(jnp.mean(x * x, axis=1, keepdims=True) + EPSILON)
    gain_part = jnp.sum(incoming * x * factor, axis=0, keepdims=True)

    @pl.when(block == 0)
    def _():
        gain_grad_ref[...] = gain_part

    @pl.when(block > 0)
    def _():
        gain_grad_ref[...] = gain_grad_ref[...] + gain_part

    low = incoming.astype(BF16)

    @pl.when(block < 2)
    def _():
        keep_ref[...] = low

    @pl.when(block >= 2)
    def _():
        send_ref[...] = low


def attention_backward(x, gain, gab, wo, qkv, forget, probs, w):
    whole = lambda b: (0, 0)
    row = lambda b: (b, 0)
    return pl.pallas_call(
        backward_kernel,
        grid=(4,),
        in_specs=[
            pl.BlockSpec((ROWS, D), row),
            pl.BlockSpec((1, D), whole),
            pl.BlockSpec((ROWS, D), row),
            pl.BlockSpec((SHARD, D), whole),
            pl.BlockSpec((ROWS, 3 * SHARD), row),
            pl.BlockSpec((ROWS, 128), row),
            pl.BlockSpec((1, LOCAL_HEADS, ROWS, ROWS), lambda b: (b, 0, 0, 0)),
            pl.BlockSpec((D, WIDTH), whole),
        ],
        out_specs=[
            pl.BlockSpec((ROWS, D), lambda b: (jnp.minimum(b, 1), 0)),
            pl.BlockSpec((ROWS, D), lambda b: (jnp.maximum(b - 2, 0), 0)),
            pl.BlockSpec((ROWS, WIDTH), row),
            pl.BlockSpec((1, D), whole),
        ],
        out_shape=[
            jax.ShapeDtypeStruct((2 * ROWS, D), BF16),
            jax.ShapeDtypeStruct((2 * ROWS, D), BF16),
            jax.ShapeDtypeStruct((4 * ROWS, WIDTH), BF16),
            jax.ShapeDtypeStruct((1, D), F32),
        ],
        compiler_params=pltpu.CompilerParams(vmem_limit_bytes=40 * 1024 * 1024),
        cost_estimate=pl.CostEstimate(
            flops=2 * 4 * ROWS * D * (WIDTH + SHARD), bytes_accessed=16 * 1024 * 1024, transcendentals=70000
        ),
    )(x, gain, gab, wo, qkv, forget, probs, w)


FBLOCK = 256


def ffn_kernel(
    at_ref, n2_ref, gb_ref, wd_ref, gate_ref, up_ref, sister_ref, z_ref, z_other_ref, y_ref, y_other_ref,
    keep_ref, send_ref, hidden_ref, dg_ref, du_ref, w_ref, sem,
):
    j, bit_z, bit_y = at_ref[2], at_ref[3], at_ref[4]
    lanes = pl.ds(pl.multiple_of(j * FSHARD, FSHARD), FSHARD)

    def rows(r, first, count):
        return pl.ds(pl.multiple_of((r ^ j) * SHARD + first, 192), count)

    half = SHARD // 2
    pieces = (
        (sister_ref, rows(1, 0, SHARD)),
        (z_ref, rows(2, bit_z * half, half)),
        (z_other_ref, rows(2, half - bit_z * half, half)),
        (y_ref, rows(3, bit_y * half, half)),
        (y_other_ref, rows(3, half - bit_y * half, half)),
    )
    own = rows(0, 0, SHARD)
    fill(
        [
            (gate_ref.at[:, lanes], w_ref.at[own, pl.ds(0, FSHARD)], sem.at[0]),
            (up_ref.at[:, lanes], w_ref.at[own, pl.ds(FSHARD, FSHARD)], sem.at[1]),
        ]
        + [(ref, w_ref.at[at], sem.at[2 + n]) for n, (ref, at) in enumerate(pieces)]
    )
    n2, gb = n2_ref[...], gb_ref[...]
    for step in range(FSHARD // FBLOCK):
        cols = slice(step * FBLOCK, step * FBLOCK + FBLOCK)
        gate = dot(n2, w_ref[:, cols], AB)
        up = dot(n2, w_ref[:, FSHARD + step * FBLOCK : FSHARD + step * FBLOCK + FBLOCK], AB)
        grad_hidden = dot(gb, wd_ref[cols, :], ABT)
        sig = jax.nn.sigmoid(gate)
        act = gate * sig
        hidden_ref[:, cols] = (act * up).astype(BF16)
        dg_ref[:, cols] = (grad_hidden * up * sig * (1.0 + gate * (1.0 - sig))).astype(BF16)
        du_ref[:, cols] = (grad_hidden * act).astype(BF16)
    for step in range(4):
        feat = slice(step * SHARD, step * SHARD + SHARD)
        part = dot(dg_ref[...], w_ref[feat, :FSHARD], ABT) + dot(du_ref[...], w_ref[feat, FSHARD:], ABT)
        part = part.astype(BF16)
        keep_ref[:, feat] = part[: 2 * ROWS]
        send_ref[:, feat] = part[2 * ROWS :]


def ffn(at, n2, gb, wd, w_gate, w_up, pieces):
    vmem = pl.BlockSpec(memory_space=pltpu.VMEM)
    wide = [jax.ShapeDtypeStruct((4 * ROWS, FSHARD), BF16)] * 3
    return pl.pallas_call(
        ffn_kernel,
        in_specs=[pl.BlockSpec(memory_space=pltpu.SMEM)] + [vmem] * 3 + [pl.BlockSpec(memory_space=pl.ANY)] * 7,
        out_specs=[vmem] * 5,
        out_shape=[jax.ShapeDtypeStruct((2 * ROWS, D), BF16)] * 2 + wide,
        scratch_shapes=[pltpu.VMEM((D, 2 * FSHARD), BF16), pltpu.SemaphoreType.DMA((7,))],
        compiler_params=pltpu.CompilerParams(vmem_limit_bytes=48 * 1024 * 1024),
        cost_estimate=pl.CostEstimate(
            flops=2 * 4 * ROWS * D * FSHARD * 5, bytes_accessed=18 * 1024 * 1024, transcendentals=4 * ROWS * FSHARD
        ),
    )(at, n2, gb, wd, w_gate, w_up, *pieces)


STAGES = ((1, 3), (3, 1))


def labels(j):
    core = j & 1
    return (0, 3 - 2 * core, 1 + 2 * core, 2)


def piece_of(part, index, label):
    a, b = label[index // 4], label[index % 4]
    return (b, a) if part == 0 else (a, b)


def place(outs, part, index):
    return outs[2 * part + index // 8], index % 8


FUNITS = 72
QUNITS = ((0, 8), (8, 15))
OUNITS = ((0, 8), (8, 18))
AUNITS = tuple(4 * (q1 - q0) + (o1 - o0) for (q0, q1), (o0, o1) in zip(QUNITS, OUNITS))
NQ, NO = 240, 288


def ffn_grad_kernel(at_ref, n2_ref, gb_ref, hidden_ref, dg_ref, du_ref, *rest):
    outs, (gate_ref, up_ref, down_ref) = rest[:4], rest[4:]
    y, z, j = at_ref[0], at_ref[1], at_ref[2]
    label = labels(j)
    n2 = n2_ref[...]
    for step in range(4):
        pz = label[step] ^ z
        lanes = pl.ds(pl.multiple_of(pz * FBLOCK, FBLOCK), FBLOCK)
        gate_ref[...] = dot(n2, dg_ref[:, lanes], ATB).astype(BF16).reshape(16, 96, FBLOCK)
        up_ref[...] = dot(n2, du_ref[:, lanes], ATB).astype(BF16).reshape(16, 96, FBLOCK)
        down_ref[...] = dot(hidden_ref[:, lanes], gb_ref[...], ATB).astype(BF16).reshape(4, 64, D)
        for part in range(2):
            source = (gate_ref, up_ref)[part]
            for other in range(4):
                py = label[other] ^ y
                out, slot = place(outs, part, 4 * step + other if part == 0 else 4 * other + step)
                for r in range(4):
                    for half in range(2):
                        block = source[(r ^ j) * 4 + py, :, 128 * half : 128 * half + 128]
                        out[slot, 12 * r + 6 * half : 12 * r + 6 * half + 6] = block.reshape(6, 16, 128)
                for t in range(6):
                    lane = 768 * part + 128 * t
                    block = down_ref[py, :, lane : lane + 128]
                    out[slot, 48 + 4 * t : 52 + 4 * t] = block.reshape(4, 16, 128)


def ffn_gradients(at, n2, gb, hidden, dg, du):
    vmem = pl.BlockSpec(memory_space=pltpu.VMEM)
    return pl.pallas_call(
        ffn_grad_kernel,
        in_specs=[pl.BlockSpec(memory_space=pltpu.SMEM)] + [vmem] * 5,
        out_specs=[vmem] * 4,
        out_shape=[jax.ShapeDtypeStruct((8, FUNITS, 16, 128), BF16)] * 4,
        scratch_shapes=[
            pltpu.VMEM((16, 96, FBLOCK), BF16),
            pltpu.VMEM((16, 96, FBLOCK), BF16),
            pltpu.VMEM((4, 64, D), BF16),
        ],
        compiler_params=pltpu.CompilerParams(vmem_limit_bytes=48 * 1024 * 1024),
        cost_estimate=pl.CostEstimate(
            flops=2 * 4 * ROWS * D * FSHARD * 3, bytes_accessed=16 * 1024 * 1024, transcendentals=0
        ),
    )(at, n2, gb, hidden, dg, du)


def ffn_unpack_kernel(at_ref, *refs):
    ins, (gate_ref, up_ref, down_ref) = refs[:4], refs[4:]
    y, z, j = at_ref[0], at_ref[1], at_ref[2]
    label = labels(j)
    for part in range(2):
        target = (gate_ref, up_ref)[part]
        for index in range(16):
            ry, rz = piece_of(part, index, label)
            source, slot = place(ins, part, index)
            py, pz = ry ^ y, rz ^ z
            rows = pl.ds(pl.multiple_of(py * 96, 32), 96)
            for r in range(4):
                for half in range(2):
                    left = (r ^ j) * FSHARD + pz * FBLOCK + half * 128
                    block = source[slot, 12 * r + 6 * half : 12 * r + 6 * half + 6].reshape(96, 128)
                    target[rows, pl.ds(pl.multiple_of(left, 128), 128)] = block.astype(F32)
            rows = pl.ds(pl.multiple_of(pz * 256 + py * 64, 64), 64)
            for t in range(6):
                left = 768 * part + 128 * t
                block = source[slot, 48 + 4 * t : 52 + 4 * t].reshape(64, 128)
                down_ref[rows, left : left + 128] = block.astype(F32)


def ffn_unpack(at, pieces):
    vmem = pl.BlockSpec(memory_space=pltpu.VMEM)
    return pl.pallas_call(
        ffn_unpack_kernel,
        in_specs=[pl.BlockSpec(memory_space=pltpu.SMEM)] + [vmem] * 4,
        out_specs=[vmem] * 3,
        out_shape=[
            jax.ShapeDtypeStruct((SHARD, FF), F32),
            jax.ShapeDtypeStruct((SHARD, FF), F32),
            jax.ShapeDtypeStruct((FSHARD, D), F32),
        ],
        compiler_params=pltpu.CompilerParams(vmem_limit_bytes=48 * 1024 * 1024),
        cost_estimate=pl.CostEstimate(flops=0, bytes_accessed=28 * 1024 * 1024, transcendentals=0),
    )(at, *pieces)


def attention_grad_kernel(at_ref, normed_ref, dqkvf_ref, mixed_ref, gab_ref, gains_ref, *rest):
    outs, (q_ref, o_ref) = rest[:4], rest[4:]
    y, z, j = at_ref[0], at_ref[1], at_ref[2]
    label = labels(j)
    dqkvf = dqkvf_ref[...]
    row = lax.broadcasted_iota(jnp.int32, (16, 128), 0)
    lane = lax.broadcasted_iota(jnp.int32, (16, 128), 1)
    pick = (lane == row + LOCAL_HEADS).astype(BF16)
    pick = jnp.where(row < 2, pick, jnp.zeros_like(pick))
    bias = jnp.sum(dqkvf[:, 3 * SHARD :].astype(F32), axis=0, keepdims=True)
    bias = pltpu.roll(bias, 8, 1)

    def units(source, width, per, p, t):
        odd = (p & 1) == 1
        group = (p >> 1) * 3 + jnp.where(odd, (per + t) // width, t // width)
        return source[group, jnp.where(odd, (per + t) % width, t % width)]

    def piece(part, index):
        ry, rz = piece_of(part, index, label)
        return (ry ^ y) * 4 + (rz ^ z)

    for r in range(4):
        lanes = pl.ds(pl.multiple_of((r ^ j) * SHARD, SHARD), SHARD)
        grad = dot(normed_ref[:, lanes], dqkvf, ATB)
        extra = grad[:, 3 * SHARD :] + dot(gains_ref[:, lanes], pick, ATB) + bias
        for col in range(9):
            block = grad[:, 128 * col : 128 * col + 128].astype(BF16).reshape(24, 1, 16, 128)
            q_ref[:, col : col + 1] = block
        q_ref[:, 9:10] = extra.astype(BF16).reshape(24, 1, 16, 128)
        for part in range(2):
            lo, hi = QUNITS[part]
            for index in range(16):
                out, slot = place(outs, part, index)
                for t in range(lo, hi):
                    out[slot, (hi - lo) * r + t - lo] = units(q_ref, 10, 15, piece(part, index), t)
    grad = dot(mixed_ref[...], gab_ref[...], ATB)
    for col in range(12):
        o_ref[:, col : col + 1] = grad[:, 128 * col : 128 * col + 128].astype(BF16).reshape(24, 1, 16, 128)
    for part in range(2):
        lo, hi = OUNITS[part]
        first = AUNITS[part] - (hi - lo)
        for index in range(16):
            out, slot = place(outs, part, index)
            for t in range(lo, hi):
                out[slot, first + t - lo] = units(o_ref, 12, 18, piece(part, index), t)


def attention_gradients(at, normed, dqkvf, mixed, gab, gains):
    vmem = pl.BlockSpec(memory_space=pltpu.VMEM)
    return pl.pallas_call(
        attention_grad_kernel,
        in_specs=[pl.BlockSpec(memory_space=pltpu.SMEM)] + [vmem] * 5,
        out_specs=[vmem] * 4,
        out_shape=[jax.ShapeDtypeStruct((8, AUNITS[i // 2], 16, 128), BF16) for i in range(4)],
        scratch_shapes=[
            pltpu.VMEM((24, 10, 16, 128), BF16),
            pltpu.VMEM((24, 12, 16, 128), BF16),
        ],
        compiler_params=pltpu.CompilerParams(vmem_limit_bytes=48 * 1024 * 1024),
        cost_estimate=pl.CostEstimate(
            flops=2 * 4 * ROWS * D * (WIDTH + SHARD), bytes_accessed=10 * 1024 * 1024, transcendentals=0
        ),
    )(at, normed, dqkvf, mixed, gab, gains)


def attention_unpack_kernel(at_ref, *refs):
    ins, (gq_ref, gk_ref, gv_ref, go_ref, forget_ref, small_ref, q_ref, o_ref) = refs[:4], refs[4:]
    y, z, j = at_ref[0], at_ref[1], at_ref[2]
    label = labels(j)
    for part in range(2):
        qlo, qhi = QUNITS[part]
        olo, ohi = OUNITS[part]
        n = qhi - qlo
        for index in range(16):
            ry, rz = piece_of(part, index, label)
            source, slot = place(ins, part, index)
            p = (ry ^ y) * 4 + (rz ^ z)
            for r in range(4):
                q_ref[r ^ j, pl.ds(p * 15 + qlo, n)] = source[slot, n * r : n * r + n]
            o_ref[pl.ds(p * 18 + olo, ohi - olo)] = source[slot, 4 * n : 4 * n + ohi - olo]
    for group in range(24):
        rows = slice(16 * group, 16 * group + 16)
        for device in range(4):
            for col in range(10):
                if col < 9:
                    target = (gq_ref, gk_ref, gv_ref)[col // 3]
                    left = SHARD * device + 128 * (col % 3)
                    target[rows, left : left + 128] = q_ref[device, 10 * group + col].astype(F32)
        for col in range(12):
            go_ref[rows, 128 * col : 128 * col + 128] = o_ref[12 * group + col].astype(F32)
    lane = lax.broadcasted_iota(jnp.int32, (128, 128), 1)
    for third in range(3):
        forget = jnp.zeros((128, 128), F32)
        total = jnp.zeros((128, 128), F32)
        for device in range(4):
            parts = [q_ref[device, 10 * group + 9] for group in range(8 * third, 8 * third + 8)]
            extra = jnp.concatenate(parts, axis=0).astype(F32)
            mine = (lane >= LOCAL_HEADS * device) & (lane < LOCAL_HEADS * device + LOCAL_HEADS)
            moved = pltpu.roll(extra, LOCAL_HEADS * device, 1) if device else extra
            forget = jnp.where(mine, moved, forget)
            total = total + extra
        forget_ref[128 * third : 128 * third + 128, :] = forget[:, :H]
        small_ref[:, 128 * third : 128 * third + 128] = total.T[:16]
    first = q_ref[j, pl.ds(9, 1)].astype(F32)
    small_ref[8:16, 0:128] = first.reshape(16, 128)[:8]


def attention_unpack(at, pieces):
    vmem = pl.BlockSpec(memory_space=pltpu.VMEM)
    return pl.pallas_call(
        attention_unpack_kernel,
        in_specs=[pl.BlockSpec(memory_space=pltpu.SMEM)] + [vmem] * 4,
        out_specs=[vmem] * 6,
        out_shape=[jax.ShapeDtypeStruct((SHARD, D), F32)] * 4
        + [jax.ShapeDtypeStruct((SHARD, H), F32), jax.ShapeDtypeStruct((16, SHARD), F32)],
        scratch_shapes=[
            pltpu.VMEM((4, NQ, 16, 128), BF16),
            pltpu.VMEM((NO, 16, 128), BF16),
        ],
        compiler_params=pltpu.CompilerParams(vmem_limit_bytes=48 * 1024 * 1024),
        cost_estimate=pl.CostEstimate(flops=0, bytes_accessed=16 * 1024 * 1024, transcendentals=0),
    )(at, *pieces)


def make_body(sizes):
    ny, nxh, nz = sizes

    def send(value, move):
        pairs = []
        for y in range(ny):
            for x in range(2 * nxh):
                for z in range(nz):
                    for c in range(2):
                        ty, tx, tz, tc = move(y, x, z, c)
                        tx %= 2 * nxh
                        src = (((y * nxh + x // 2) * nz + z) * 2 + x % 2) * 2 + c
                        dst = (((ty * nxh + tx // 2) * nz + tz) * 2 + tx % 2) * 2 + tc
                        pairs.append((src, dst))
        return lax.ppermute(value, AXES, pairs)

    def swap_plane(value, axis, stage):
        if axis == "y":
            return send(value, lambda y, x, z, c: (y ^ STAGES[c][stage], x, z, c))
        return send(value, lambda y, x, z, c: (y, x, z ^ STAGES[c][stage], c))

    def after(value, *others):
        return lax.optimization_barrier((value, *others))[0]

    swap_core = lambda v: send(v, lambda y, x, z, c: (y, x, z, 1 - c))
    swap_x = lambda v: send(v, lambda y, x, z, c: (y, x ^ 1, z, c))
    swap_out = lambda v: send(v, lambda y, x, z, c: (y, x ^ 3, z, c))
    x_plus = lambda v: send(v, lambda y, x, z, c: (y, x + 1, z, c))
    x_minus = lambda v: send(v, lambda y, x, z, c: (y, x - 1, z, c))
    x_two = lambda v: send(v, lambda y, x, z, c: (y, x + 2, z, c))

    def total(parts):
        return functools.reduce(lambda a, b: a + b, [p.astype(F32) for p in parts])

    def combine(keep, received):
        return total([keep, received]).astype(BF16)

    class Order:
        def __init__(self):
            self.work = ()

        def arrive(self, *values):
            out = lax.optimization_barrier((*values, *self.work))[: len(values)]
            return out if len(values) > 1 else out[0]

        def then(self, *work):
            self.work = work

    def move(part, step):
        return ("zy"[part != step // 2], step % 2)

    def sum_steps(order, parts):
        held = [[parts[0]], [parts[2]]]
        sending = [parts[1], parts[3]]
        for step in range(4):
            half = 4 >> step
            got = [swap_plane(sending[k], *move(k, step)) for k in range(2)]
            yield
            got = order.arrive(*got)
            for k in range(2):
                held[k].append(got[k])
                if half:
                    sending[k] = total([h[half : 2 * half] for h in held[k]]).astype(BF16)
            if half:
                order.then(*sending)
        out = [total([h[:1] for h in held[k]]).astype(BF16)[0] for k in range(2)]
        order.then(*out)
        return out

    def gather_steps(order, pieces):
        out = [p[None] for p in pieces]
        for step in (3, 2, 1, 0):
            got = [swap_plane(out[k], *move(k, step)) for k in range(2)]
            yield
            got = order.arrive(*got)
            if step:
                out = [jnp.concatenate([out[k], got[k]], axis=0) for k in range(2)]
                order.then(*out)
        return [v for k in range(2) for v in (out[k], got[k])]

    def spread_steps(order, pieces, columns):
        rel = [p[: 4 * n].reshape(4, n, 16, 128) for p, n in zip(pieces, columns)]
        own = [p[4 * n :] for p, n in zip(pieces, columns)]
        sister = swap_core(jnp.concatenate([r[i] for i in (1, 3) for r in rel], axis=0))
        yield
        sister = order.arrive(sister)
        n = sum(columns)
        far = jnp.concatenate([r[2] for r in rel] + [sister[n:]], axis=0)
        near = jnp.concatenate([r[0] for r in rel] + [sister[:n]] + own, axis=0)
        order.then(far, near)
        a, b, t = x_plus(far), x_minus(far), x_two(near)
        yield
        a, b, t = order.arrive(a, b, t)
        near, far = combine(near, t), combine(a, b)
        out, at, tail = [], 0, 2 * n
        for p, m in zip(pieces, columns):
            last = p.shape[0] - 4 * m
            blocks = [v[lo + at : lo + at + m] for v in (near, far) for lo in (0, n)]
            out.append(jnp.concatenate(blocks + [near[tail : tail + last]], axis=0))
            at, tail = at + m, tail + last
        order.then(*out)
        return out

    def chain(order, parts, columns):
        pieces = yield from sum_steps(order, parts)
        pieces = yield from spread_steps(order, pieces, columns)
        return (yield from gather_steps(order, pieces))

    def body(
        tokens, lengths, w_query, w_key, w_value, w_out, w_forget, forget_bias, norm_attn,
        w_gate, w_up, w_down, norm_ffn, cotangent,
    ):
        y, z, core = lax.axis_index("y"), lax.axis_index("z"), lax.axis_index("c")
        j = lax.axis_index("xl") * 2 + core
        bits = [(jnp.where(n == 0, z & 1, z >> 1), jnp.where(n == 0, y & 1, y >> 1)) for n in (core, 1 - core)]
        (bit_z, bit_y), (_, sister_bit_y) = bits
        at = jnp.stack([y, z, j, bit_z, bit_y]).astype(jnp.int32)

        small = jnp.concatenate([norm_attn, norm_ffn, lengths[0].astype(BF16)])
        small = jnp.pad(small[None], ((0, 15), (0, D - small.shape[0])))
        packed = jnp.concatenate([tokens, small], axis=0)
        pair = jnp.stack([packed, swap_x(packed)])
        packed_all = jnp.concatenate([pair, swap_core(pair)], axis=0)
        x_rows = packed_all[:, :ROWS].reshape(4 * ROWS, D)
        small_all = packed_all[:, ROWS]
        lens = small_all[:, 2 * SHARD : 2 * SHARD + SLOTS].astype(jnp.int32)
        by_device = jnp.stack([small_all[0], small_all[2], small_all[1], small_all[3]])
        by_device = jnp.concatenate(
            [lax.dynamic_index_in_dim(by_device, j ^ r, 0, keepdims=True) for r in range(4)], axis=0
        ).astype(F32)
        gain_one = by_device[:, :SHARD].reshape(1, D)
        gain_two = by_device[:, SHARD : 2 * SHARD].reshape(1, D)
        bias = jnp.pad(forget_bias.astype(F32), (0, 128 - LOCAL_HEADS))[None]

        near = 288
        own_cols, far_cols, sister_cols = columns(at, w_query, w_key, w_value, w_forget)
        far = swap_out(far_cols)
        sister = swap_core(sister_cols)
        cross = swap_x(sister[SHARD : SHARD + near])
        rest = swap_out(sister[SHARD + near :])

        half = SHARD // 2

        def gate_up_for(i, row, count):
            parts = [lax.dynamic_slice(w, (row, i * FSHARD), (count, FSHARD)) for w in (w_gate, w_up)]
            return jnp.concatenate(parts, axis=1)

        sister_gu = swap_core(after(gate_up_for(j ^ 1, 0, SHARD), sister))
        cross_gu = swap_core(after(gate_up_for(j ^ 3, sister_bit_y * half, half), sister))
        cot_first = swap_x(after(cotangent, cross))
        fetch_z = swap_out(after(gate_up_for(j ^ 2, bit_z * half, half), far))
        fetch_y = swap_x(after(cross_gu, cross))

        keep, sent, normed, qkv, forget, probs, mixed, w_qkvf = attention_forward(
            lens, at, x_rows, gain_one, bias, w_out, (own_cols, sister, far, cross, rest)
        )
        keep, fetch_z, fetch_y, cot_first, sister_gu = lax.optimization_barrier(
            (keep, fetch_z, fetch_y, cot_first, sister_gu)
        )
        chip = combine(keep, swap_core(sent))
        other = swap_x(chip)
        other_z, other_y = swap_plane(fetch_z, "z", 0), swap_plane(fetch_y, "y", 0)
        cot_pair = jnp.stack([cotangent, cot_first])
        cot_rows = jnp.concatenate([cot_pair, swap_core(cot_pair)], axis=0).reshape(4 * ROWS, D)
        live = (jnp.arange(ROWS)[None, :] < jnp.sum(lens, axis=1, keepdims=True)).reshape(4 * ROWS, 1)
        grad_branch = jnp.where(live, cot_rows, jnp.zeros_like(cot_rows))
        other, other_z, other_y, grad_branch = lax.optimization_barrier((other, other_z, other_y, grad_branch))

        def both_chips(chip, other):
            return chip.astype(F32) + jnp.concatenate([other[ROWS:], other[:ROWS]], axis=0).astype(F32)

        middle = x_rows[: 2 * ROWS].astype(F32) + both_chips(chip, other)
        factor_two = lax.rsqrt(jnp.mean(middle * middle, axis=1, keepdims=True) + EPSILON)
        n2_half = (middle * factor_two * gain_two).astype(BF16)
        n2 = jnp.concatenate([n2_half, swap_core(n2_half)], axis=0)

        keep, sent, hidden, dgate, dup = ffn(
            at, n2, grad_branch, w_down, w_gate, w_up, (sister_gu, fetch_z, other_z, fetch_y, other_y)
        )
        order = Order()
        ffn_parts = ffn_gradients(at, n2, grad_branch, hidden, dgate, dup)
        first = swap_core(sent)
        order.then(ffn_parts[0])
        ffn_chain = chain(order, ffn_parts, [12, 12])
        next(ffn_chain)
        chip = combine(keep, order.arrive(first))
        order.then(chip)
        other = swap_x(chip)
        down = dot(after(hidden, chip), w_down, AB).astype(BF16)
        order.then(down)
        incoming_two = both_chips(chip, order.arrive(other))
        scaled = incoming_two * gain_two
        inner = jnp.mean(scaled * middle, axis=1, keepdims=True)
        grad_middle = grad_branch[: 2 * ROWS].astype(F32) + (
            scaled * factor_two - middle * (factor_two * factor_two * factor_two) * inner
        )
        gain_two_part = 0.5 * jnp.sum(incoming_two * middle * factor_two, axis=0)
        gab_half = grad_middle.astype(BF16)
        order.then(gab_half)
        gab_other = swap_core(gab_half)
        next(ffn_chain)
        gab = jnp.concatenate([gab_half, order.arrive(gab_other)], axis=0)

        keep, sent, dqkvf, gain_one_part = attention_backward(
            x_rows, gain_one, gab, w_out, qkv, forget, probs, w_qkvf
        )
        gains = jnp.concatenate([gain_one_part, gain_two_part[None]], axis=0).astype(BF16)
        gains = jnp.pad(gains, ((0, 14), (0, 0)))
        order.then(dqkvf)
        token_first = swap_core(sent)
        next(ffn_chain)
        attn_parts = attention_gradients(at, normed, order.arrive(dqkvf), mixed, gab, gains)
        order.then(attn_parts[0])
        attn_chain = chain(order, attn_parts, [hi - lo for lo, hi in QUNITS])
        next(attn_chain)
        token_chip = combine(keep, order.arrive(token_first))
        order.then(token_chip)
        token_other = swap_x(token_chip[ROWS:])
        next(ffn_chain)
        next(ffn_chain)
        next(attn_chain)
        next(ffn_chain)
        next(ffn_chain)
        token_other = order.arrive(token_other)
        down_first = swap_core(down[2 * ROWS :])
        next(attn_chain)
        next(ffn_chain)
        next(attn_chain)
        down_chip = combine(down[: 2 * ROWS], order.arrive(down_first))
        order.then(down_chip)
        down_other = swap_x(down_chip[ROWS:])
        next(ffn_chain)
        next(attn_chain)
        next(attn_chain)
        next(ffn_chain)
        next(attn_chain)
        down_other = order.arrive(down_other)
        next(attn_chain)
        next(attn_chain)
        next(attn_chain)

        def finish(steps):
            try:
                next(steps)
            except StopIteration as stop:
                return stop.value

        ffn_pieces = finish(ffn_chain)
        branch = down_chip[:ROWS].astype(F32) + down_other.astype(F32)
        output = jnp.where(live[:ROWS], middle[:ROWS] + branch, 0.0).astype(BF16)

        own = x_rows[:ROWS].astype(F32)
        factor_one = lax.rsqrt(jnp.mean(own * own, axis=1, keepdims=True) + EPSILON)
        scaled = (token_chip[:ROWS].astype(F32) + token_other.astype(F32)) * gain_one
        inner = jnp.mean(scaled * own, axis=1, keepdims=True)
        grad_tokens = grad_middle[:ROWS] + (
            scaled * factor_one - own * (factor_one * factor_one * factor_one) * inner
        )

        grad_gate, grad_up, grad_down = ffn_unpack(at, ffn_pieces)
        order.then(grad_down)
        grad_query, grad_key, grad_value, grad_out, grad_forget, small = attention_unpack(at, finish(attn_chain))
        grad_norm_attn, grad_norm_ffn = small[LOCAL_HEADS], small[LOCAL_HEADS + 1]
        grad_bias = small[8, 8 : 8 + LOCAL_HEADS]
        return (
            output, grad_tokens, grad_query, grad_key, grad_value, grad_out, grad_forget, grad_bias,
            grad_norm_attn, grad_gate, grad_up, grad_down, grad_norm_ffn,
        )

    return body


SIZES = {32: (4, 2, 4), 16: (4, 1, 4)}


def solution(mesh):
    sizes = SIZES[mesh.shape["wide"]]
    ny, nxh, nz = sizes
    fine = Mesh(mesh.devices.reshape(ny, nxh, nz, 2, 2), AXES)
    rows, shard, vector = P(AXES, None), P(("xl", "c"), None), P(("xl", "c"))
    return jax.shard_map(
        make_body(sizes),
        mesh=fine,
        in_specs=(
            rows, rows, shard, shard, shard, shard, shard, vector, vector, shard, shard, shard, vector, rows,
        ),
        out_specs=(
            rows, rows, shard, shard, shard, shard, shard, vector, vector, shard, shard, shard, vector,
        ),
        check_vma=False,
    )
```

```python
import functools

import jax
import jax.numpy as jnp
from jax import lax
from jax.experimental import pallas as pl
from jax.experimental.pallas import tpu as pltpu
from jax.sharding import Mesh, PartitionSpec as P

D = 1536
H = 24
HD = 64
FF = 4096
ROWS = 128
SLOTS = 4
EPSILON = 1e-06
SHARD = D // 4
FSHARD = FF // 4
LOCAL_HEADS = H // 4
WIDTH = 3 * SHARD + 128
AXES = ("y", "xh", "z", "xl", "c")
PLANE = ("y", "z")
F32 = jnp.float32
BF16 = jnp.bfloat16


def dot(former, latter, dims):
    return lax.dot_general(former, latter, (dims, ((), ())), preferred_element_type=F32)


COST = pl.CostEstimate(flops=0, bytes_accessed=0, transcendentals=0)

AB = ((1,), (0,))
ABT = ((1,), (1,))
ATB = ((0,), (0,))


def exact_dot(former, latter):
    return lax.dot_general(
        former, latter, ((AB), ((), ())), precision=lax.Precision.HIGHEST, preferred_element_type=F32
    )


def attend_mask(lens):
    rows = lax.broadcasted_iota(jnp.int32, (ROWS, ROWS), 0).astype(F32)
    cols = lax.broadcasted_iota(jnp.int32, (ROWS, ROWS), 1).astype(F32)
    seg_rows = jnp.zeros((ROWS, ROWS), F32)
    seg_cols = jnp.zeros((ROWS, ROWS), F32)
    end = jnp.zeros((1, 1), F32)
    for slot in range(SLOTS):
        end = end + lens[:, slot : slot + 1]
        seg_rows = seg_rows + (rows >= end).astype(F32)
        seg_cols = seg_cols + (cols >= end).astype(F32)
    return (rows >= cols) & (seg_rows == seg_cols)


def half_masks():
    lane = lax.broadcasted_iota(jnp.int32, (ROWS, 128), 1)
    return lane < HD, lane >= HD


def fill(copies):
    copies = [pltpu.make_async_copy(*c) for c in copies]
    for c in copies:
        c.start()
    for c in copies:
        c.wait()


def columns_kernel(at_ref, f_ref, q_ref, k_ref, v_ref, own_ref, far_ref, sister_ref, cross_ref, held_ref, sem):
    j = at_ref[2]
    targets = (2, 3, 1, 0)
    ins = []
    for n, r in enumerate(targets):
        lanes = pl.ds(pl.multiple_of((r ^ j) * SHARD, SHARD), SHARD)
        for m, source in enumerate((q_ref, k_ref, v_ref)):
            target = held_ref.at[n, :, pl.ds(SHARD * m, SHARD)]
            ins.append(pltpu.make_async_copy(source.at[:, lanes], target, sem.at[3 * n + m]))
            ins[-1].start()
    forget = jnp.concatenate([f_ref[...].astype(F32), jnp.zeros((SHARD, 128 - H), F32)], axis=1)
    lane = lax.broadcasted_iota(jnp.int32, (SHARD, 128), 1)
    for n, r in enumerate(targets):
        mine = pltpu.roll(forget, lax.rem(128 - LOCAL_HEADS * (r ^ j), 128), 1)
        held_ref[n, :, 3 * SHARD :] = jnp.where(lane < LOCAL_HEADS, mine, 0.0).astype(BF16)
    for copy in ins:
        copy.wait()
    fill(
        [
            (held_ref.at[0], far_ref, sem.at[12]),
            (held_ref.at[1], cross_ref, sem.at[13]),
            (held_ref.at[2], sister_ref, sem.at[14]),
            (held_ref.at[3], own_ref, sem.at[15]),
        ]
    )


def columns(at, w_query, w_key, w_value, w_forget):
    anywhere = pl.BlockSpec(memory_space=pl.ANY)
    return pl.pallas_call(
        columns_kernel,
        in_specs=[pl.BlockSpec(memory_space=pltpu.SMEM), pl.BlockSpec(memory_space=pltpu.VMEM)] + [anywhere] * 3,
        out_specs=[anywhere] * 4,
        out_shape=[jax.ShapeDtypeStruct((SHARD, WIDTH), BF16)] * 4,
        scratch_shapes=[pltpu.VMEM((4, SHARD, WIDTH), BF16), pltpu.SemaphoreType.DMA((16,))],
        compiler_params=pltpu.CompilerParams(vmem_limit_bytes=60 * 1024 * 1024),
        cost_estimate=COST,
    )(at, w_forget, w_query, w_key, w_value)


def gate_up_columns_kernel(at_ref, gate_ref, up_ref, sister_ref, cross_ref, far_ref, held_ref, sem):
    j, bit_z, sister_bit_y = at_ref[2], at_ref[3], at_ref[5]
    half = SHARD // 2
    some = lambda bit: pl.ds(pl.multiple_of(bit * half, half), half)
    targets = ((1, sister_ref, pl.ds(0, SHARD)), (3, cross_ref, some(sister_bit_y)), (2, far_ref, some(bit_z)))
    ins, outs, first = [], [], 0
    for n, (r, ref, rows) in enumerate(targets):
        lanes = pl.ds(pl.multiple_of((r ^ j) * FSHARD, FSHARD), FSHARD)
        held = held_ref.at[pl.ds(first, ref.shape[0])]
        for m, source in enumerate((gate_ref, up_ref)):
            ins.append((source.at[rows, lanes], held.at[:, pl.ds(FSHARD * m, FSHARD)], sem.at[2 * n + m]))
        outs.append((held, ref, sem.at[6 + n]))
        first += ref.shape[0]
    fill(ins)
    fill(outs)


def gate_up_columns(at, w_gate, w_up):
    anywhere = pl.BlockSpec(memory_space=pl.ANY)
    return pl.pallas_call(
        gate_up_columns_kernel,
        in_specs=[pl.BlockSpec(memory_space=pltpu.SMEM)] + [anywhere] * 2,
        out_specs=[anywhere] * 3,
        out_shape=[jax.ShapeDtypeStruct((n, 2 * FSHARD), BF16) for n in (SHARD, SHARD // 2, SHARD // 2)],
        scratch_shapes=[pltpu.VMEM((2 * SHARD, 2 * FSHARD), BF16), pltpu.SemaphoreType.DMA((9,))],
        compiler_params=pltpu.CompilerParams(vmem_limit_bytes=60 * 1024 * 1024),
        cost_estimate=COST,
    )(at, w_gate, w_up)


def forward_kernel(
    at_ref, first_ref, second_ref, bias_ref, wo_ref, own_ref, sister_ref, far_ref, cross_ref,
    keep_ref, send_ref, normed_ref, qkv_ref, forget_ref, probs_ref, mixed_ref, w_ref, gain_ref, sem,
):
    block = pl.program_id(0)

    @pl.when(block == 0)
    def _():
        j = at_ref[2]
        copies = []
        for r, ref in enumerate((own_ref, sister_ref, far_ref, cross_ref)):
            rows = pl.ds(pl.multiple_of((r ^ j) * SHARD, SHARD), SHARD)
            copies.append((ref, w_ref.at[rows], sem.at[r]))
        fill(copies)
        for r in range(4):
            lanes = pl.ds(pl.multiple_of((r ^ j) * SHARD, SHARD), SHARD)
            ref = (first_ref, second_ref)[r % 2]
            gain_ref[:, lanes] = ref[r // 2, ROWS : ROWS + 1, :SHARD].astype(F32)

    rows = jnp.where(block < 2, first_ref[block % 2], second_ref[block % 2])
    lens = rows[ROWS : ROWS + 1, 2 * SHARD : 2 * SHARD + SLOTS].astype(F32)
    x = rows[:ROWS].astype(F32)
    factor = lax.rsqrt(jnp.mean(x * x, axis=1, keepdims=True) + EPSILON)
    normed = (x * factor * gain_ref[...]).astype(BF16)
    normed_ref[...] = normed
    proj = dot(normed, w_ref[...], AB)
    qkv = proj[:, : 3 * SHARD].astype(BF16)
    qkv_ref[...] = qkv
    forget = proj[:, 3 * SHARD :] + bias_ref[...]
    forget_ref[...] = forget
    logs = jax.nn.log_sigmoid(forget)
    rows = lax.broadcasted_iota(jnp.int32, (ROWS, ROWS), 0)
    cols = lax.broadcasted_iota(jnp.int32, (ROWS, ROWS), 1)
    decays = exact_dot((rows >= cols).astype(F32), logs)
    decays_t = decays.T
    allowed = attend_mask(lens)
    halves = half_masks()
    parts = []
    for pair in range(LOCAL_HEADS // 2):
        q2 = qkv[:, 128 * pair : 128 * pair + 128]
        k2 = qkv[:, SHARD + 128 * pair : SHARD + 128 * pair + 128]
        v2 = qkv[:, 2 * SHARD + 128 * pair : 2 * SHARD + 128 * pair + 128]
        total = jnp.zeros((ROWS, 128), F32)
        for side in range(2):
            head = 2 * pair + side
            kh = jnp.where(halves[side], k2, jnp.zeros_like(k2))
            vh = jnp.where(halves[side], v2, jnp.zeros_like(v2))
            scores = dot(q2, kh, ABT) * (HD ** (-0.5))
            scores = scores + decays[:, head : head + 1] - decays_t[head : head + 1, :]
            scores = jnp.where(allowed, scores, -1e30)
            highest = jnp.max(scores, axis=1, keepdims=True)
            weights = jnp.exp(scores - highest)
            probs = weights / jnp.sum(weights, axis=1, keepdims=True)
            probs_ref[0, head] = probs
            total = total + dot(probs.astype(BF16), vh, AB)
        parts.append(total.astype(BF16))
    mixed = jnp.concatenate(parts, axis=1)
    mixed_ref[...] = mixed
    partial = dot(mixed, wo_ref[...], AB).astype(BF16)

    @pl.when(block < 2)
    def _():
        keep_ref[...] = partial

    @pl.when(block >= 2)
    def _():
        send_ref[...] = partial


def attention_forward(at, first, second, bias, wo, pieces):
    whole = lambda b: (0, 0)
    row = lambda b: (b, 0)
    smem = pl.BlockSpec(memory_space=pltpu.SMEM)
    return pl.pallas_call(
        forward_kernel,
        grid=(4,),
        in_specs=[
            smem,
            pl.BlockSpec((2, ROWS + 16, D), lambda b: (0, 0, 0)),
            pl.BlockSpec((2, ROWS + 16, D), lambda b: (0, 0, 0)),
            pl.BlockSpec((1, 128), whole),
            pl.BlockSpec((SHARD, D), whole),
        ]
        + [pl.BlockSpec(memory_space=pl.ANY)] * 4,
        out_specs=[
            pl.BlockSpec((ROWS, D), lambda b: (jnp.minimum(b, 1), 0)),
            pl.BlockSpec((ROWS, D), lambda b: (jnp.maximum(b - 2, 0), 0)),
            pl.BlockSpec((ROWS, D), row),
            pl.BlockSpec((ROWS, 3 * SHARD), row),
            pl.BlockSpec((ROWS, 128), row),
            pl.BlockSpec((1, LOCAL_HEADS, ROWS, ROWS), lambda b: (b, 0, 0, 0)),
            pl.BlockSpec((ROWS, SHARD), row),
            pl.BlockSpec((D, WIDTH), whole),
        ],
        out_shape=[
            jax.ShapeDtypeStruct((2 * ROWS, D), BF16),
            jax.ShapeDtypeStruct((2 * ROWS, D), BF16),
            pltpu.HBM((4 * ROWS, D), BF16),
            pltpu.HBM((4 * ROWS, 3 * SHARD), BF16),
            pltpu.HBM((4 * ROWS, 128), F32),
            pltpu.HBM((4, LOCAL_HEADS, ROWS, ROWS), F32),
            pltpu.HBM((4 * ROWS, SHARD), BF16),
            pltpu.HBM((D, WIDTH), BF16),
        ],
        scratch_shapes=[pltpu.VMEM((1, D), F32), pltpu.SemaphoreType.DMA((4,))],
        compiler_params=pltpu.CompilerParams(vmem_limit_bytes=32 * 1024 * 1024),
        cost_estimate=pl.CostEstimate(
            flops=2 * 4 * ROWS * D * (WIDTH + SHARD), bytes_accessed=16 * 1024 * 1024, transcendentals=400000
        ),
    )(at, first, second, bias, wo, *pieces)


def backward_kernel(
    x_ref, gab_ref, wo_ref, qkv_ref, forget_ref, probs_ref, w_ref,
    low_ref, dqkvf_ref, gain_grad_ref,
):
    block = pl.program_id(0)
    gm = dot(gab_ref[...], wo_ref[...], ABT).astype(BF16)
    qkv = qkv_ref[...]
    halves = half_masks()
    lane = lax.broadcasted_iota(jnp.int32, (ROWS, 128), 1)
    rows = lax.broadcasted_iota(jnp.int32, (ROWS, ROWS), 0)
    cols = lax.broadcasted_iota(jnp.int32, (ROWS, ROWS), 1)
    grad_decays = jnp.zeros((ROWS, 128), F32)
    dqs, dks, dvs = [], [], []
    for pair in range(LOCAL_HEADS // 2):
        q2 = qkv[:, 128 * pair : 128 * pair + 128]
        k2 = qkv[:, SHARD + 128 * pair : SHARD + 128 * pair + 128]
        v2 = qkv[:, 2 * SHARD + 128 * pair : 2 * SHARD + 128 * pair + 128]
        g2 = gm[:, 128 * pair : 128 * pair + 128]
        dq = jnp.zeros((ROWS, 128), F32)
        dk = jnp.zeros((ROWS, 128), F32)
        dv = jnp.zeros((ROWS, 128), F32)
        for side in range(2):
            head = 2 * pair + side
            zero = jnp.zeros_like(q2)
            gh = jnp.where(halves[side], g2, zero)
            probs = probs_ref[0, head]
            grad_probs = dot(gh, v2, ABT)
            inner = jnp.sum(probs * grad_probs, axis=1, keepdims=True)
            ds = (probs * (grad_probs - inner)).astype(BF16)
            dq = dq + dot(ds, jnp.where(halves[side], k2, zero), AB)
            dk = dk + dot(ds, jnp.where(halves[side], q2, zero), ATB)
            dv = dv + dot(probs.astype(BF16), gh, ATB)
            pick = (lane == head).astype(BF16)
            grad_decays = grad_decays + dot(ds, pick, AB) - dot(ds, pick, ATB)
        dqs.append((dq * (HD ** (-0.5))).astype(BF16))
        dks.append((dk * (HD ** (-0.5))).astype(BF16))
        dvs.append(dv.astype(BF16))
    grad_logs = exact_dot((rows <= cols).astype(F32), grad_decays)
    grad_forget = (grad_logs * jax.nn.sigmoid(-forget_ref[...])).astype(BF16)
    dqkvf = jnp.concatenate(dqs + dks + dvs + [grad_forget], axis=1)
    dqkvf_ref[...] = dqkvf
    incoming = dot(dqkvf, w_ref[...], ABT)
    x = x_ref[0, :ROWS].astype(F32)
    factor = lax.rsqrt(jnp.mean(x * x, axis=1, keepdims=True) + EPSILON)
    gain_part = jnp.sum(incoming * x * factor, axis=0, keepdims=True)

    @pl.when(block == 0)
    def _():
        gain_grad_ref[...] = gain_part

    @pl.when(block > 0)
    def _():
        gain_grad_ref[...] = gain_grad_ref[...] + gain_part

    low_ref[...] = incoming.astype(BF16)


def attention_backward(half, x, gab, wo, qkv, forget, probs, w):
    whole = lambda b: (0, 0)
    row = lambda b: (2 * half + b, 0)
    out = lambda b: (b, 0)
    return pl.pallas_call(
        backward_kernel,
        grid=(2,),
        in_specs=[
            pl.BlockSpec((1, ROWS + 16, D), lambda b: (b, 0, 0)),
            pl.BlockSpec((ROWS, D), out),
            pl.BlockSpec((SHARD, D), whole),
            pl.BlockSpec((ROWS, 3 * SHARD), row),
            pl.BlockSpec((ROWS, 128), row),
            pl.BlockSpec((1, LOCAL_HEADS, ROWS, ROWS), lambda b: (2 * half + b, 0, 0, 0)),
            pl.BlockSpec((D, WIDTH), whole),
        ],
        out_specs=[
            pl.BlockSpec((ROWS, D), out),
            pl.BlockSpec((ROWS, WIDTH), out),
            pl.BlockSpec((1, D), whole),
        ],
        out_shape=[
            jax.ShapeDtypeStruct((2 * ROWS, D), BF16),
            jax.ShapeDtypeStruct((2 * ROWS, WIDTH), BF16),
            jax.ShapeDtypeStruct((1, D), F32),
        ],
        compiler_params=pltpu.CompilerParams(vmem_limit_bytes=26 * 1024 * 1024),
        cost_estimate=pl.CostEstimate(
            flops=2 * 2 * ROWS * D * (WIDTH + SHARD), bytes_accessed=10 * 1024 * 1024, transcendentals=40000
        ),
    )(x, gab, wo, qkv, forget, probs, w)


FBLOCK = 256


def ffn_kernel(
    at_ref, first_ref, second_ref, gb_ref, wd_ref, gate_ref, up_ref, sister_ref, z_ref, z_other_ref, y_ref, y_other_ref,
    keep_ref, send_ref, hidden_ref, dg_ref, du_ref, n2_ref, w_ref, sem,
):
    j, bit_z, bit_y = at_ref[2], at_ref[3], at_ref[4]
    lanes = pl.ds(pl.multiple_of(j * FSHARD, FSHARD), FSHARD)

    def rows(r, first, count):
        return pl.ds(pl.multiple_of((r ^ j) * SHARD + first, 192), count)

    half = SHARD // 2
    pieces = (
        (sister_ref, rows(1, 0, SHARD)),
        (z_ref, rows(2, bit_z * half, half)),
        (z_other_ref, rows(2, half - bit_z * half, half)),
        (y_ref, rows(3, bit_y * half, half)),
        (y_other_ref, rows(3, half - bit_y * half, half)),
    )
    own = rows(0, 0, SHARD)
    fill(
        [
            (gate_ref.at[:, lanes], w_ref.at[own, pl.ds(0, FSHARD)], sem.at[0]),
            (up_ref.at[:, lanes], w_ref.at[own, pl.ds(FSHARD, FSHARD)], sem.at[1]),
        ]
        + [(ref, w_ref.at[at], sem.at[2 + n]) for n, (ref, at) in enumerate(pieces)]
    )
    n2_ref[: 2 * ROWS] = first_ref[...]
    n2_ref[2 * ROWS :] = second_ref[...]
    n2, gb = n2_ref[...], gb_ref[...]
    for step in range(FSHARD // FBLOCK):
        cols = slice(step * FBLOCK, step * FBLOCK + FBLOCK)
        gate = dot(n2, w_ref[:, cols], AB)
        up = dot(n2, w_ref[:, FSHARD + step * FBLOCK : FSHARD + step * FBLOCK + FBLOCK], AB)
        grad_hidden = dot(gb, wd_ref[cols, :], ABT)
        sig = jax.nn.sigmoid(gate)
        act = gate * sig
        hidden_ref[:, cols] = (act * up).astype(BF16)
        dg_ref[:, cols] = (grad_hidden * up * sig * (1.0 + gate * (1.0 - sig))).astype(BF16)
        du_ref[:, cols] = (grad_hidden * act).astype(BF16)
    for step in range(4):
        feat = slice(step * SHARD, step * SHARD + SHARD)
        part = dot(dg_ref[...], w_ref[feat, :FSHARD], ABT) + dot(du_ref[...], w_ref[feat, FSHARD:], ABT)
        part = part.astype(BF16)
        keep_ref[:, feat] = part[: 2 * ROWS]
        send_ref[:, feat] = part[2 * ROWS :]


def ffn(at, first, second, gb, wd, w_gate, w_up, pieces):
    vmem = pl.BlockSpec(memory_space=pltpu.VMEM)
    wide = [jax.ShapeDtypeStruct((4 * ROWS, FSHARD), BF16)] * 3
    return pl.pallas_call(
        ffn_kernel,
        in_specs=[pl.BlockSpec(memory_space=pltpu.SMEM)] + [vmem] * 4 + [pl.BlockSpec(memory_space=pl.ANY)] * 7,
        out_specs=[vmem] * 6,
        out_shape=[jax.ShapeDtypeStruct((2 * ROWS, D), BF16)] * 2 + wide + [jax.ShapeDtypeStruct((4 * ROWS, D), BF16)],
        scratch_shapes=[pltpu.VMEM((D, 2 * FSHARD), BF16), pltpu.SemaphoreType.DMA((7,))],
        compiler_params=pltpu.CompilerParams(vmem_limit_bytes=32 * 1024 * 1024),
        cost_estimate=COST,
    )(at, first, second, gb, wd, w_gate, w_up, *pieces)


STAGES = ((1, 3), (3, 1))


def labels(j):
    core = j & 1
    return (0, 3 - 2 * core, 1 + 2 * core, 2)


def piece_of(part, index, label):
    a, b = label[index // 4], label[index % 4]
    return (b, a) if part == 0 else (a, b)


def place(outs, part, index):
    return outs[2 * part + index // 8], index % 8


FUNITS = 72
QUNITS = ((0, 8), (8, 15))
OUNITS = ((0, 8), (8, 18))
AUNITS = tuple(4 * (q1 - q0) + (o1 - o0) for (q0, q1), (o0, o1) in zip(QUNITS, OUNITS))
NQ, NO = 240, 288


def ffn_grad_kernel(part, at_ref, n2_ref, gb_ref, hidden_ref, grad_ref, keep_ref, send_ref, cols_ref, down_ref):
    y, z, j = at_ref[0], at_ref[1], at_ref[2]
    label = labels(j)
    n2 = n2_ref[...]
    for step in range(4):
        pz = label[step] ^ z
        lanes = pl.ds(pl.multiple_of(pz * FBLOCK, FBLOCK), FBLOCK)
        cols_ref[...] = dot(n2, grad_ref[:, lanes], ATB).astype(BF16).reshape(16, 96, FBLOCK)
        gb = gb_ref[:, 768 * part : 768 * part + 768]
        down_ref[...] = dot(hidden_ref[:, lanes], gb, ATB).astype(BF16).reshape(4, 64, 768)
        for other in range(4):
            py = label[other] ^ y
            index = 4 * step + other if part == 0 else 4 * other + step
            out, slot = (keep_ref, send_ref)[index // 8], index % 8
            for r in range(4):
                for half in range(2):
                    block = cols_ref[(r ^ j) * 4 + py, :, 128 * half : 128 * half + 128]
                    out[slot, 12 * r + 6 * half : 12 * r + 6 * half + 6] = block.reshape(6, 16, 128)
            for t in range(6):
                block = down_ref[py, :, 128 * t : 128 * t + 128]
                out[slot, 48 + 4 * t : 52 + 4 * t] = block.reshape(4, 16, 128)


def ffn_gradients(part, at, n2, gb, hidden, grad):
    vmem = pl.BlockSpec(memory_space=pltpu.VMEM)
    return pl.pallas_call(
        functools.partial(ffn_grad_kernel, part),
        in_specs=[pl.BlockSpec(memory_space=pltpu.SMEM)] + [vmem] * 4,
        out_specs=[vmem] * 2,
        out_shape=[jax.ShapeDtypeStruct((8, FUNITS, 16, 128), BF16)] * 2,
        scratch_shapes=[pltpu.VMEM((16, 96, FBLOCK), BF16), pltpu.VMEM((4, 64, 768), BF16)],
        compiler_params=pltpu.CompilerParams(vmem_limit_bytes=20 * 1024 * 1024),
        cost_estimate=COST,
    )(at, n2, gb, hidden, grad)


def ffn_unpack_kernel(at_ref, pieces_ref, gate_ref, up_ref, down_ref):
    j = at_ref[2]
    for part in range(2):
        target = (gate_ref, up_ref)[part]
        for pz in range(4):
            for r in range(4):
                for half in range(2):
                    left = pl.multiple_of((r ^ j) * FSHARD + (pz * FBLOCK + half * 128), 128)
                    first = FUNITS * part + 12 * r + 6 * half
                    block = pieces_ref[pz, first : first + 6].reshape(96, 128)
                    target[:, pl.ds(left, 128)] = block.astype(F32)
            for t in range(6):
                left = 768 * part + 128 * t
                first = FUNITS * part + 48 + 4 * t
                block = pieces_ref[pz, first : first + 4].reshape(64, 128)
                down_ref[pz, 0, :, left : left + 128] = block.astype(F32)


def ffn_unpack(at, pieces):
    gate, up, down = pl.pallas_call(
        ffn_unpack_kernel,
        grid=(4,),
        in_specs=[
            pl.BlockSpec(memory_space=pltpu.SMEM),
            pl.BlockSpec((4, 2 * FUNITS, 16, 128), lambda b: (b, 0, 0, 0)),
        ],
        out_specs=[
            pl.BlockSpec((96, FF), lambda b: (b, 0)),
            pl.BlockSpec((96, FF), lambda b: (b, 0)),
            pl.BlockSpec((4, 1, 64, D), lambda b: (0, b, 0, 0)),
        ],
        out_shape=[
            jax.ShapeDtypeStruct((SHARD, FF), F32),
            jax.ShapeDtypeStruct((SHARD, FF), F32),
            jax.ShapeDtypeStruct((4, 4, 64, D), F32),
        ],
        compiler_params=pltpu.CompilerParams(vmem_limit_bytes=60 * 1024 * 1024),
        cost_estimate=COST,
    )(at, pieces)
    return gate, up, down.reshape(FSHARD, D)


def attention_grad_kernel(at_ref, normed_ref, d1_ref, d2_ref, mixed_ref, g1_ref, g2_ref, gains_ref, *rest):
    outs, (q_ref, o_ref) = rest[:4], rest[4:]
    y, z, j = at_ref[0], at_ref[1], at_ref[2]
    label = labels(j)
    d1, d2 = d1_ref[...], d2_ref[...]
    upper, lower = pl.ds(0, 2 * ROWS), pl.ds(2 * ROWS, 2 * ROWS)
    row = lax.broadcasted_iota(jnp.int32, (16, 128), 0)
    lane = lax.broadcasted_iota(jnp.int32, (16, 128), 1)
    pick = (lane == row + LOCAL_HEADS).astype(BF16)
    pick = jnp.where(row < 2, pick, jnp.zeros_like(pick))
    bias = sum(jnp.sum(d[:, 3 * SHARD :].astype(F32), axis=0, keepdims=True) for d in (d1, d2))
    bias = pltpu.roll(bias, 8, 1)

    def units(source, width, per, p, t):
        odd = (p & 1) == 1
        group = (p >> 1) * 3 + jnp.where(odd, (per + t) // width, t // width)
        return source[group, jnp.where(odd, (per + t) % width, t % width)]

    def piece(part, index):
        ry, rz = piece_of(part, index, label)
        return (ry ^ y) * 4 + (rz ^ z)

    for r in range(4):
        lanes = pl.ds(pl.multiple_of((r ^ j) * SHARD, SHARD), SHARD)
        grad = dot(normed_ref[upper, lanes], d1, ATB) + dot(normed_ref[lower, lanes], d2, ATB)
        extra = grad[:, 3 * SHARD :] + dot(gains_ref[:, lanes], pick, ATB) + bias
        for col in range(9):
            block = grad[:, 128 * col : 128 * col + 128].astype(BF16).reshape(24, 1, 16, 128)
            q_ref[:, col : col + 1] = block
        q_ref[:, 9:10] = extra.astype(BF16).reshape(24, 1, 16, 128)
        for part in range(2):
            lo, hi = QUNITS[part]
            for index in range(16):
                out, slot = place(outs, part, index)
                for t in range(lo, hi):
                    out[slot, (hi - lo) * r + t - lo] = units(q_ref, 10, 15, piece(part, index), t)
    grad = dot(mixed_ref[upper, :], g1_ref[...], ATB) + dot(mixed_ref[lower, :], g2_ref[...], ATB)
    for col in range(12):
        o_ref[:, col : col + 1] = grad[:, 128 * col : 128 * col + 128].astype(BF16).reshape(24, 1, 16, 128)
    for part in range(2):
        lo, hi = OUNITS[part]
        first = AUNITS[part] - (hi - lo)
        for index in range(16):
            out, slot = place(outs, part, index)
            for t in range(lo, hi):
                out[slot, first + t - lo] = units(o_ref, 12, 18, piece(part, index), t)


def attention_gradients(at, normed, d1, d2, mixed, g1, g2, gains):
    vmem = pl.BlockSpec(memory_space=pltpu.VMEM)
    return pl.pallas_call(
        attention_grad_kernel,
        in_specs=[pl.BlockSpec(memory_space=pltpu.SMEM)] + [vmem] * 7,
        out_specs=[vmem] * 4,
        out_shape=[jax.ShapeDtypeStruct((8, AUNITS[i // 2], 16, 128), BF16) for i in range(4)],
        scratch_shapes=[
            pltpu.VMEM((24, 10, 16, 128), BF16),
            pltpu.VMEM((24, 12, 16, 128), BF16),
        ],
        compiler_params=pltpu.CompilerParams(vmem_limit_bytes=26 * 1024 * 1024),
        cost_estimate=pl.CostEstimate(
            flops=2 * 4 * ROWS * D * (WIDTH + SHARD), bytes_accessed=10 * 1024 * 1024, transcendentals=0
        ),
    )(at, normed, d1, d2, mixed, g1, g2, gains)


def attention_unpack_kernel(at_ref, *refs):
    ins, (gq_ref, gk_ref, gv_ref, go_ref, forget_ref, small_ref, q_ref, o_ref) = refs[:4], refs[4:]
    y, z, j = at_ref[0], at_ref[1], at_ref[2]
    label = labels(j)
    for part in range(2):
        qlo, qhi = QUNITS[part]
        olo, ohi = OUNITS[part]
        n = qhi - qlo
        for index in range(16):
            ry, rz = piece_of(part, index, label)
            source, slot = place(ins, part, index)
            p = (ry ^ y) * 4 + (rz ^ z)
            for r in range(4):
                q_ref[r ^ j, pl.ds(p * 15 + qlo, n)] = source[slot, n * r : n * r + n]
            o_ref[pl.ds(p * 18 + olo, ohi - olo)] = source[slot, 4 * n : 4 * n + ohi - olo]
    for group in range(24):
        rows = slice(16 * group, 16 * group + 16)
        for device in range(4):
            for col in range(10):
                if col < 9:
                    target = (gq_ref, gk_ref, gv_ref)[col // 3]
                    left = SHARD * device + 128 * (col % 3)
                    target[rows, left : left + 128] = q_ref[device, 10 * group + col].astype(F32)
        for col in range(12):
            go_ref[rows, 128 * col : 128 * col + 128] = o_ref[12 * group + col].astype(F32)
    lane = lax.broadcasted_iota(jnp.int32, (128, 128), 1)
    for third in range(3):
        forget = jnp.zeros((128, 128), F32)
        total = jnp.zeros((128, 128), F32)
        for device in range(4):
            parts = [q_ref[device, 10 * group + 9] for group in range(8 * third, 8 * third + 8)]
            extra = jnp.concatenate(parts, axis=0).astype(F32)
            mine = (lane >= LOCAL_HEADS * device) & (lane < LOCAL_HEADS * device + LOCAL_HEADS)
            moved = pltpu.roll(extra, LOCAL_HEADS * device, 1) if device else extra
            forget = jnp.where(mine, moved, forget)
            total = total + extra
        forget_ref[128 * third : 128 * third + 128, :] = forget[:, :H]
        small_ref[:, 128 * third : 128 * third + 128] = total.T[:16]
    first = q_ref[j, pl.ds(9, 1)].astype(F32)
    small_ref[8:16, 0:128] = first.reshape(16, 128)[:8]


def attention_unpack(at, pieces):
    vmem = pl.BlockSpec(memory_space=pltpu.VMEM)
    return pl.pallas_call(
        attention_unpack_kernel,
        in_specs=[pl.BlockSpec(memory_space=pltpu.SMEM)] + [vmem] * 4,
        out_specs=[vmem] * 6,
        out_shape=[jax.ShapeDtypeStruct((SHARD, D), F32)] * 4
        + [jax.ShapeDtypeStruct((SHARD, H), F32), jax.ShapeDtypeStruct((16, SHARD), F32)],
        scratch_shapes=[
            pltpu.VMEM((4, NQ, 16, 128), BF16),
            pltpu.VMEM((NO, 16, 128), BF16),
        ],
        compiler_params=pltpu.CompilerParams(vmem_limit_bytes=24 * 1024 * 1024),
        cost_estimate=COST,
    )(at, *pieces)


def small_call(kernel, out, *args):
    vmem = pl.BlockSpec(memory_space=pltpu.VMEM)
    return pl.pallas_call(
        kernel,
        in_specs=[vmem] * len(args),
        out_specs=[vmem] * len(out),
        out_shape=[jax.ShapeDtypeStruct((n, 16, 128), BF16) for n in out],
        compiler_params=pltpu.CompilerParams(vmem_limit_bytes=8 * 1024 * 1024),
        cost_estimate=COST,
    )(*args)


def for_sister(pieces, columns):
    def kernel(first_ref, second_ref, out_ref):
        at = 0
        for r in (1, 3):
            for ref, n in zip((first_ref, second_ref), columns):
                out_ref[at : at + n] = ref[r * n : r * n + n]
                at += n

    return small_call(kernel, [2 * sum(columns)], *pieces)[0]


def for_chips(pieces, sister, columns):
    n = sum(columns)
    tails = [p.shape[0] - 4 * m for p, m in zip(pieces, columns)]

    def kernel(first_ref, second_ref, sister_ref, near_ref, far_ref):
        at, tail = 0, 2 * n
        for ref, m, last in zip((first_ref, second_ref), columns, tails):
            near_ref[at : at + m] = ref[0:m]
            far_ref[at : at + m] = ref[2 * m : 3 * m]
            near_ref[tail : tail + last] = ref[4 * m : 4 * m + last]
            at, tail = at + m, tail + last
        near_ref[n : 2 * n] = sister_ref[0:n]
        far_ref[n : 2 * n] = sister_ref[n : 2 * n]

    return small_call(kernel, [2 * n + sum(tails), 2 * n], *pieces, sister)


def join_chips(near, far, a, b, t, columns):
    n = sum(columns)
    last = near.shape[0] - 2 * n
    tails = [last // 2, last // 2] if columns[0] == columns[1] else [hi - lo for lo, hi in OUNITS]

    def kernel(near_ref, far_ref, a_ref, b_ref, t_ref, first_ref, second_ref):
        def total(x_ref, y_ref, lo, m):
            return (x_ref[lo : lo + m].astype(F32) + y_ref[lo : lo + m].astype(F32)).astype(BF16)

        at, tail = 0, 2 * n
        for ref, m, end in zip((first_ref, second_ref), columns, tails):
            ref[0:m] = total(near_ref, t_ref, at, m)
            ref[m : 2 * m] = total(near_ref, t_ref, n + at, m)
            ref[2 * m : 3 * m] = total(a_ref, b_ref, at, m)
            ref[3 * m : 4 * m] = total(a_ref, b_ref, n + at, m)
            ref[4 * m : 4 * m + end] = total(near_ref, t_ref, tail, end)
            at, tail = at + m, tail + end

    return small_call(kernel, [4 * m + end for m, end in zip(columns, tails)], near, far, a, b, t)


def make_body(sizes):
    ny, nxh, nz = sizes

    def send(value, move):
        pairs = []
        for y in range(ny):
            for x in range(2 * nxh):
                for z in range(nz):
                    for c in range(2):
                        ty, tx, tz, tc = move(y, x, z, c)
                        tx %= 2 * nxh
                        src = (((y * nxh + x // 2) * nz + z) * 2 + x % 2) * 2 + c
                        dst = (((ty * nxh + tx // 2) * nz + tz) * 2 + tx % 2) * 2 + tc
                        pairs.append((src, dst))
        return lax.ppermute(value, AXES, pairs)

    def swap_plane(value, axis, stage):
        if axis == "y":
            return send(value, lambda y, x, z, c: (y ^ STAGES[c][stage], x, z, c))
        return send(value, lambda y, x, z, c: (y, x, z ^ STAGES[c][stage], c))

    def after(value, *others):
        return lax.optimization_barrier((value, *others))[0]

    swap_core = lambda v: send(v, lambda y, x, z, c: (y, x, z, 1 - c))
    swap_x = lambda v: send(v, lambda y, x, z, c: (y, x ^ 1, z, c))
    swap_out = lambda v: send(v, lambda y, x, z, c: (y, x ^ 3, z, c))
    cross_mixed = lambda v: send(v, lambda y, x, z, c: (y, x ^ (1 if c else 3), z, 1 - c))
    cross_x = lambda v: send(v, lambda y, x, z, c: (y, x ^ 1, z, 1 - c))
    x_plus = lambda v: send(v, lambda y, x, z, c: (y, x + 1, z, c))
    x_minus = lambda v: send(v, lambda y, x, z, c: (y, x - 1, z, c))
    x_two = lambda v: send(v, lambda y, x, z, c: (y, x + 2, z, c))

    def total(parts):
        return functools.reduce(lambda a, b: a + b, [p.astype(F32) for p in parts])

    def combine(keep, received):
        return total([keep, received]).astype(BF16)

    class Order:
        def __init__(self):
            self.work = ()

        def arrive(self, *values):
            out = lax.optimization_barrier((*values, *self.work))[: len(values)]
            return out if len(values) > 1 else out[0]

        def then(self, *work):
            self.work = work

    def move(part, step):
        return ("zy"[part != step // 2], step % 2)

    class Lane:
        def __init__(self, order, part, keep, sending):
            self.order, self.part, self.held, self.sending, self.step = order, part, [keep], sending, 0

        def start(self):
            self.got = swap_plane(self.sending, *move(self.part, self.step))

        def arrive(self):
            self.held.append(self.order.arrive(self.got))
            half = 4 >> self.step
            span = slice(half, 2 * half) if half else slice(0, 1)
            self.sending = total([h[span] for h in self.held]).astype(BF16)
            self.order.then(self.sending)
            self.step += 1

        def gather(self, piece):
            self.sending, self.step = piece[None], 3

        def collect(self):
            self.got = self.order.arrive(self.got)
            if self.step:
                self.sending = jnp.concatenate([self.sending, self.got], axis=0)
                self.order.then(self.sending)
            self.step -= 1

    def both(lanes, *names):
        for name in names:
            for lane in lanes:
                getattr(lane, name)()

    def each(lanes, *names):
        for lane in lanes:
            for name in names:
                getattr(lane, name)()

    def spread_steps(order, pieces, columns):
        sister = swap_core(for_sister(pieces, columns))
        yield
        sister = order.arrive(sister)
        near, far = for_chips(pieces, sister, columns)
        order.then(far, near)
        a, b, t = x_plus(far), x_minus(far), x_two(near)
        yield
        a, b, t = order.arrive(a, b, t)
        out = join_chips(near, far, a, b, t, columns)
        order.then(*out)
        return out

    def finish(steps):
        try:
            next(steps)
        except StopIteration as stop:
            return stop.value

    def body(
        tokens, lengths, w_query, w_key, w_value, w_out, w_forget, forget_bias, norm_attn,
        w_gate, w_up, w_down, norm_ffn, cotangent,
    ):
        y, z, core = lax.axis_index("y"), lax.axis_index("z"), lax.axis_index("c")
        j = lax.axis_index("xl") * 2 + core
        bits = [(jnp.where(n == 0, z & 1, z >> 1), jnp.where(n == 0, y & 1, y >> 1)) for n in (core, 1 - core)]
        (bit_z, bit_y), (_, sister_bit_y) = bits
        at = jnp.stack([y, z, j, bit_z, bit_y, sister_bit_y]).astype(jnp.int32)

        own_cols, far_cols, sister_cols, cross_cols = columns(at, w_query, w_key, w_value, w_forget)
        far, cross, sister = swap_out(far_cols), cross_mixed(cross_cols), swap_core(sister_cols)
        cot_first = swap_x(after(cotangent, far_cols))

        small = jnp.concatenate([norm_attn, norm_ffn, lengths[0].astype(BF16)])
        small = after(small, far_cols)
        small = jnp.pad(small[None], ((0, 15), (0, D - small.shape[0])))
        packed = jnp.concatenate([tokens, small], axis=0)
        packed_first = swap_x(packed)

        sister_gu, cross_gu, far_gu = gate_up_columns(after(at, far_cols, packed), w_gate, w_up)

        order = Order()
        order.then(far_gu)
        packed_first = order.arrive(packed_first)
        pair = jnp.stack([packed, packed_first])
        order.then(pair)
        packed_second = swap_core(pair)
        sister, cross, far, cot_first = order.arrive(sister, cross, far, cot_first)
        order.then(sister, cross, far)
        fetch_z = swap_out(after(far_gu, far))
        fetch_y = cross_x(after(cross_gu, cross))
        sister_gu = swap_core(after(sister_gu, sister))
        packed_all = jnp.concatenate([pair, order.arrive(packed_second)], axis=0)
        x_rows = packed_all[:, :ROWS].reshape(4 * ROWS, D)
        small_all = packed_all[:, ROWS]
        lens = small_all[:, 2 * SHARD : 2 * SHARD + SLOTS].astype(jnp.int32)
        by_device = jnp.stack([small_all[0], small_all[2], small_all[1], small_all[3]])
        by_device = jnp.concatenate(
            [lax.dynamic_index_in_dim(by_device, j ^ r, 0, keepdims=True) for r in range(4)], axis=0
        ).astype(F32)
        gain_one = by_device[:, :SHARD].reshape(1, D)
        gain_two = by_device[:, SHARD : 2 * SHARD].reshape(1, D)
        bias = jnp.pad(forget_bias.astype(F32), (0, 128 - LOCAL_HEADS))[None]

        keep, sent, normed, qkv, forget, probs, mixed, w_qkvf = attention_forward(
            at, pair, packed_second, bias, w_out, (own_cols, sister, far, cross)
        )
        first, fetch_z, fetch_y, sister_gu = lax.optimization_barrier(
            (swap_core(sent), fetch_z, fetch_y, sister_gu)
        )
        chip = combine(keep, first)
        other = swap_x(chip)
        other_z, other_y = swap_plane(fetch_z, "z", 0), swap_plane(fetch_y, "y", 0)
        cot_pair = jnp.stack([cotangent, cot_first])
        cot_rows = jnp.concatenate([cot_pair, swap_core(cot_pair)], axis=0).reshape(4 * ROWS, D)
        live = (jnp.arange(ROWS)[None, :] < jnp.sum(lens, axis=1, keepdims=True)).reshape(4 * ROWS, 1)
        grad_branch = jnp.where(live, cot_rows, jnp.zeros_like(cot_rows))
        other, other_z, other_y, grad_branch = lax.optimization_barrier((other, other_z, other_y, grad_branch))

        def both_chips(chip, other):
            return chip.astype(F32) + jnp.concatenate([other[ROWS:], other[:ROWS]], axis=0).astype(F32)

        middle = x_rows[: 2 * ROWS].astype(F32) + both_chips(chip, other)
        factor_two = lax.rsqrt(jnp.mean(middle * middle, axis=1, keepdims=True) + EPSILON)
        n2_half = (middle * factor_two * gain_two).astype(BF16)
        n2_other = swap_core(n2_half)

        keep, sent, hidden, dgate, dup, n2 = ffn(
            at, n2_half, n2_other, grad_branch, w_down, w_gate, w_up, (sister_gu, fetch_z, other_z, fetch_y, other_y)
        )
        order = Order()
        first = swap_core(sent)
        ffn_parts = ffn_gradients(0, at, n2, grad_branch, hidden, dgate)
        order.then(ffn_parts[0])
        chip = combine(keep, order.arrive(first))
        ffn_parts = ffn_parts + ffn_gradients(1, at, after(n2, chip), grad_branch, hidden, dup)
        order.then(ffn_parts[2])
        ffn_lanes = [Lane(order, k, *ffn_parts[2 * k : 2 * k + 2]) for k in range(2)]
        both(ffn_lanes, "start")
        other = swap_x(chip)
        down = dot(after(hidden, ffn_parts[2]), w_down, AB).astype(BF16)
        order.then(down)
        incoming_two = both_chips(chip, order.arrive(other))
        scaled = incoming_two * gain_two
        inner = jnp.mean(scaled * middle, axis=1, keepdims=True)
        grad_middle = grad_branch[: 2 * ROWS].astype(F32) + (
            scaled * factor_two - middle * (factor_two * factor_two * factor_two) * inner
        )
        gain_two_part = 0.5 * jnp.sum(incoming_two * middle * factor_two, axis=0)
        gab_half = grad_middle.astype(BF16)
        order.then(gab_half)
        gab_other = swap_core(gab_half)

        kept = (w_out, qkv, forget, probs, w_qkvf)
        keep, d1, gain_first = attention_backward(0, pair, gab_half, *kept)
        order.then(d1)
        each(ffn_lanes[:1], "arrive", "start")
        gab_other = order.arrive(gab_other)
        sent, d2, gain_second = attention_backward(1, packed_second, gab_other, *kept)
        order.then(d2)
        token_first = swap_core(sent)
        each(ffn_lanes[1:], "arrive", "start")
        gains = jnp.concatenate([gain_first + gain_second, gain_two_part[None]], axis=0).astype(BF16)
        gains = jnp.pad(gains, ((0, 14), (0, 0)))
        attn_parts = attention_gradients(at, normed, d1, order.arrive(d2), mixed, gab_half, gab_other, gains)
        order.then(attn_parts[0])
        attn_lanes = [Lane(order, k, *attn_parts[2 * k : 2 * k + 2]) for k in range(2)]
        both(attn_lanes, "start")
        each(ffn_lanes, "arrive", "start")
        each(ffn_lanes, "arrive", "start")
        each(attn_lanes, "arrive", "start")
        each(ffn_lanes, "arrive")
        ffn_spread = spread_steps(order, [lane.sending[0] for lane in ffn_lanes], [12, 12])
        next(ffn_spread)
        each(attn_lanes, "arrive", "start")
        next(ffn_spread)
        each(attn_lanes, "arrive", "start")
        ffn_pieces = finish(ffn_spread)
        ffn_gathered = lax.all_gather(jnp.concatenate(ffn_pieces, axis=0), PLANE)
        each(attn_lanes, "arrive")
        attn_spread = spread_steps(
            order, [lane.sending[0] for lane in attn_lanes], [hi - lo for lo, hi in QUNITS]
        )
        next(attn_spread)
        token_chip = combine(keep, order.arrive(token_first))
        order.then(token_chip)
        next(attn_spread)
        token_other = swap_x(token_chip[ROWS:])
        attn_pieces = finish(attn_spread)
        for lane, piece in zip(attn_lanes, attn_pieces):
            lane.gather(piece)
        both(attn_lanes, "start")
        down_first = swap_core(down[2 * ROWS :])
        each(attn_lanes, "collect", "start")
        token_other = order.arrive(token_other)
        down_chip = combine(down[: 2 * ROWS], order.arrive(down_first))
        order.then(down_chip)
        down_other = swap_x(down_chip[ROWS:])
        each(attn_lanes, "collect", "start")
        each(attn_lanes, "collect", "start")
        down_other = order.arrive(down_other)
        grad_gate, grad_up, grad_down = ffn_unpack(at, ffn_gathered)
        order.then(grad_down)
        each(attn_lanes, "collect")
        branch = down_chip[:ROWS].astype(F32) + down_other.astype(F32)
        output = jnp.where(live[:ROWS], middle[:ROWS] + branch, 0.0).astype(BF16)

        own = x_rows[:ROWS].astype(F32)
        factor_one = lax.rsqrt(jnp.mean(own * own, axis=1, keepdims=True) + EPSILON)
        scaled = (token_chip[:ROWS].astype(F32) + token_other.astype(F32)) * gain_one
        inner = jnp.mean(scaled * own, axis=1, keepdims=True)
        grad_tokens = grad_middle[:ROWS] + (
            scaled * factor_one - own * (factor_one * factor_one * factor_one) * inner
        )

        grad_query, grad_key, grad_value, grad_out, grad_forget, small = attention_unpack(
            at, [v for lane in attn_lanes for v in (lane.sending, lane.got)]
        )
        grad_norm_attn, grad_norm_ffn = small[LOCAL_HEADS], small[LOCAL_HEADS + 1]
        grad_bias = small[8, 8 : 8 + LOCAL_HEADS]
        return (
            output, grad_tokens, grad_query, grad_key, grad_value, grad_out, grad_forget, grad_bias,
            grad_norm_attn, grad_gate, grad_up, grad_down, grad_norm_ffn,
        )

    return body


SIZES = {32: (4, 2, 4), 16: (4, 1, 4)}


def solution(mesh):
    sizes = SIZES[mesh.shape["wide"]]
    ny, nxh, nz = sizes
    fine = Mesh(mesh.devices.reshape(ny, nxh, nz, 2, 2), AXES)
    rows, shard, vector = P(AXES, None), P(("xl", "c"), None), P(("xl", "c"))
    return jax.shard_map(
        make_body(sizes),
        mesh=fine,
        in_specs=(
            rows, rows, shard, shard, shard, shard, shard, vector, vector, shard, shard, shard, vector, rows,
        ),
        out_specs=(
            rows, rows, shard, shard, shard, shard, shard, vector, vector, shard, shard, shard, vector,
        ),
        check_vma=False,
    )
```

```python
import functools

import jax
import jax.numpy as jnp
from jax import lax
from jax.experimental import pallas as pl
from jax.experimental.pallas import tpu as pltpu
from jax.sharding import Mesh, PartitionSpec as P

D = 1536
H = 24
HD = 64
FF = 4096
ROWS = 128
SLOTS = 4
EPSILON = 1e-06
SHARD = D // 4
FSHARD = FF // 4
LOCAL_HEADS = H // 4
WIDTH = 3 * SHARD + 128
AXES = ("y", "xh", "z", "xl", "c")
PLANE = ("y", "z")
F32 = jnp.float32
BF16 = jnp.bfloat16


def dot(former, latter, dims):
    return lax.dot_general(former, latter, (dims, ((), ())), preferred_element_type=F32)


COST = pl.CostEstimate(flops=0, bytes_accessed=0, transcendentals=0)

AB = ((1,), (0,))
ABT = ((1,), (1,))
ATB = ((0,), (0,))


def exact_dot(former, latter):
    return lax.dot_general(
        former, latter, ((AB), ((), ())), precision=lax.Precision.HIGHEST, preferred_element_type=F32
    )


def attend_mask(lens):
    rows = lax.broadcasted_iota(jnp.int32, (ROWS, ROWS), 0).astype(F32)
    cols = lax.broadcasted_iota(jnp.int32, (ROWS, ROWS), 1).astype(F32)
    seg_rows = jnp.zeros((ROWS, ROWS), F32)
    seg_cols = jnp.zeros((ROWS, ROWS), F32)
    end = jnp.zeros((1, 1), F32)
    for slot in range(SLOTS):
        end = end + lens[:, slot : slot + 1]
        seg_rows = seg_rows + (rows >= end).astype(F32)
        seg_cols = seg_cols + (cols >= end).astype(F32)
    return (rows >= cols) & (seg_rows == seg_cols)


def fill(copies):
    copies = [pltpu.make_async_copy(*c) for c in copies]
    for c in copies:
        c.start()
    for c in copies:
        c.wait()


def columns_kernel(at_ref, f_ref, q_ref, k_ref, v_ref, own_ref, far_ref, sister_ref, cross_ref, held_ref, sem):
    j = at_ref[2]
    targets = (2, 3, 1, 0)
    ins = []
    for n, r in enumerate(targets):
        lanes = pl.ds(pl.multiple_of((r ^ j) * SHARD, SHARD), SHARD)
        for m, source in enumerate((q_ref, k_ref, v_ref)):
            target = held_ref.at[n, :, pl.ds(SHARD * m, SHARD)]
            ins.append(pltpu.make_async_copy(source.at[:, lanes], target, sem.at[3 * n + m]))
            ins[-1].start()
    forget = jnp.concatenate([f_ref[...].astype(F32), jnp.zeros((128 - H, SHARD), F32)], axis=0).T
    lane = lax.broadcasted_iota(jnp.int32, (SHARD, 128), 1)
    for n, r in enumerate(targets):
        mine = pltpu.roll(forget, lax.rem(128 - LOCAL_HEADS * (r ^ j), 128), 1)
        held_ref[n, :, 3 * SHARD :] = jnp.where(lane < LOCAL_HEADS, mine, 0.0).astype(BF16)
    for copy in ins:
        copy.wait()
    fill(
        [
            (held_ref.at[0], far_ref, sem.at[12]),
            (held_ref.at[1], cross_ref, sem.at[13]),
            (held_ref.at[2], sister_ref, sem.at[14]),
            (held_ref.at[3], own_ref, sem.at[15]),
        ]
    )


def columns(at, w_query, w_key, w_value, w_forget):
    anywhere = pl.BlockSpec(memory_space=pl.ANY)
    return pl.pallas_call(
        columns_kernel,
        in_specs=[pl.BlockSpec(memory_space=pltpu.SMEM), pl.BlockSpec(memory_space=pltpu.VMEM)] + [anywhere] * 3,
        out_specs=[anywhere] * 4,
        out_shape=[jax.ShapeDtypeStruct((SHARD, WIDTH), BF16)] * 4,
        scratch_shapes=[pltpu.VMEM((4, SHARD, WIDTH), BF16), pltpu.SemaphoreType.DMA((16,))],
        compiler_params=pltpu.CompilerParams(vmem_limit_bytes=60 * 1024 * 1024),
        cost_estimate=COST,
    )(at, w_forget, w_query, w_key, w_value)


def gate_up_columns_kernel(at_ref, gate_ref, up_ref, sister_ref, cross_ref, far_ref, held_ref, sem):
    j, bit_z, sister_bit_y = at_ref[2], at_ref[3], at_ref[5]
    half = SHARD // 2
    some = lambda bit: pl.ds(pl.multiple_of(bit * half, half), half)
    targets = ((1, sister_ref, pl.ds(0, SHARD)), (3, cross_ref, some(sister_bit_y)), (2, far_ref, some(bit_z)))
    ins, outs, first = [], [], 0
    for n, (r, ref, rows) in enumerate(targets):
        lanes = pl.ds(pl.multiple_of((r ^ j) * FSHARD, FSHARD), FSHARD)
        held = held_ref.at[pl.ds(first, ref.shape[0])]
        for m, source in enumerate((gate_ref, up_ref)):
            ins.append((source.at[rows, lanes], held.at[:, pl.ds(FSHARD * m, FSHARD)], sem.at[2 * n + m]))
        outs.append((held, ref, sem.at[6 + n]))
        first += ref.shape[0]
    fill(ins)
    fill(outs)


def gate_up_columns(at, w_gate, w_up):
    anywhere = pl.BlockSpec(memory_space=pl.ANY)
    return pl.pallas_call(
        gate_up_columns_kernel,
        in_specs=[pl.BlockSpec(memory_space=pltpu.SMEM)] + [anywhere] * 2,
        out_specs=[anywhere] * 3,
        out_shape=[jax.ShapeDtypeStruct((n, 2 * FSHARD), BF16) for n in (SHARD, SHARD // 2, SHARD // 2)],
        scratch_shapes=[pltpu.VMEM((2 * SHARD, 2 * FSHARD), BF16), pltpu.SemaphoreType.DMA((9,))],
        compiler_params=pltpu.CompilerParams(vmem_limit_bytes=60 * 1024 * 1024),
        cost_estimate=COST,
    )(at, w_gate, w_up)


def column_copies(j, pieces, w_ref, sem):
    rows = lambda r: pl.ds(pl.multiple_of((r ^ j) * SHARD, SHARD), SHARD)
    return [pltpu.make_async_copy(ref, w_ref.at[rows(r)], sem.at[r]) for r, ref in enumerate(pieces)]


def forward_kernel(
    at_ref, first_ref, second_ref, bias_ref, wo_ref, own_ref, sister_ref, far_ref, cross_ref,
    keep_ref, send_ref, normed_out, qkv_out, forget_out, probs_out, mixed_out,
    w_ref, normed_ref, qkv_ref, forget_ref, probs_ref, mixed_ref, gain_ref, sem,
):
    j = at_ref[2]
    copies = column_copies(j, (own_ref, sister_ref, far_ref, cross_ref), w_ref, sem)
    for copy in copies:
        copy.start()
    for r in range(4):
        lanes = pl.ds(pl.multiple_of((r ^ j) * SHARD, SHARD), SHARD)
        ref = (first_ref, second_ref)[r % 2]
        gain_ref[:, lanes] = ref[r // 2, ROWS : ROWS + 1, :SHARD].astype(F32)
    for block in range(4):
        x = (first_ref, second_ref)[block // 2][block % 2, :ROWS].astype(F32)
        factor = lax.rsqrt(jnp.mean(x * x, axis=1, keepdims=True) + EPSILON)
        normed_ref[block * ROWS : block * ROWS + ROWS] = (x * factor * gain_ref[...]).astype(BF16)
    for copy in copies:
        copy.wait()

    out = lambda ref, target, n: pltpu.make_async_copy(ref, target, sem.at[4 + n])
    leaving = [out(normed_ref, normed_out, 0)]
    leaving[0].start()
    normed = normed_ref[...]
    forget_ref[...] = dot(normed, w_ref[:, 3 * SHARD :], AB) + bias_ref[...]
    for col in range(3):
        lanes = slice(SHARD * col, SHARD * col + SHARD)
        qkv_ref[:, lanes] = dot(normed, w_ref[:, lanes], AB).astype(BF16)
    leaving += [out(forget_ref, forget_out, 1), out(qkv_ref, qkv_out, 2)]
    for copy in leaving[1:]:
        copy.start()

    rows = lax.broadcasted_iota(jnp.int32, (ROWS, ROWS), 0)
    cols = lax.broadcasted_iota(jnp.int32, (ROWS, ROWS), 1)
    lower = (rows >= cols).astype(F32)
    left = lax.broadcasted_iota(jnp.int32, (ROWS, 128), 1) < HD
    for block in range(4):
        at = slice(block * ROWS, block * ROWS + ROWS)
        lens = (first_ref, second_ref)[block // 2][block % 2, ROWS : ROWS + 1, 2 * SHARD : 2 * SHARD + SLOTS]
        decays = exact_dot(lower, jax.nn.log_sigmoid(forget_ref[at, :]))
        decays_t = decays.T
        allowed = attend_mask(lens.astype(F32))
        for pair in range(LOCAL_HEADS // 2):
            lane = 128 * pair
            q2, k2, v2 = (qkv_ref[at, SHARD * n + lane : SHARD * n + lane + 128] for n in range(3))
            zero = jnp.zeros_like(k2)
            keys = jnp.concatenate([jnp.where(left, k2, zero), jnp.where(left, zero, k2)], axis=0)
            values = jnp.concatenate([jnp.where(left, v2, zero), jnp.where(left, zero, v2)], axis=0)
            both = dot(q2, keys, ABT)
            low = []
            for side in range(2):
                head = 2 * pair + side
                scores = both[:, ROWS * side : ROWS * side + ROWS] * (HD ** (-0.5))
                scores = scores + decays[:, head : head + 1] - decays_t[head : head + 1, :]
                scores = jnp.where(allowed, scores, -1e30)
                highest = jnp.max(scores, axis=1, keepdims=True)
                weights = jnp.exp(scores - highest)
                probs = weights / jnp.sum(weights, axis=1, keepdims=True)
                probs_ref[block, head] = probs
                low.append(probs.astype(BF16))
            mixed_ref[at, lane : lane + 128] = dot(jnp.concatenate(low, axis=1), values, AB).astype(BF16)
        leaving.append(out(probs_ref.at[block], probs_out.at[block], 4 + block))
        leaving[-1].start()
    leaving.append(out(mixed_ref, mixed_out, 3))
    leaving[-1].start()
    for col in range(4):
        lanes = slice(SHARD * col, SHARD * col + SHARD)
        partial = dot(mixed_ref[...], wo_ref[:, lanes], AB).astype(BF16)
        keep_ref[:, lanes] = partial[: 2 * ROWS]
        send_ref[:, lanes] = partial[2 * ROWS :]
    for copy in leaving:
        copy.wait()


def attention_forward(at, first, second, bias, wo, pieces):
    vmem, anywhere = pl.BlockSpec(memory_space=pltpu.VMEM), pl.BlockSpec(memory_space=pltpu.HBM)
    saved = [
        ((4 * ROWS, D), BF16),
        ((4 * ROWS, 3 * SHARD), BF16),
        ((4 * ROWS, 128), F32),
        ((4, LOCAL_HEADS, ROWS, ROWS), F32),
        ((4 * ROWS, SHARD), BF16),
    ]
    return pl.pallas_call(
        forward_kernel,
        in_specs=[pl.BlockSpec(memory_space=pltpu.SMEM)] + [vmem] * 4 + [anywhere] * 4,
        out_specs=[vmem] * 2 + [anywhere] * 5,
        out_shape=[jax.ShapeDtypeStruct((2 * ROWS, D), BF16)] * 2 + [pltpu.HBM(*v) for v in saved],
        scratch_shapes=[pltpu.VMEM((D, WIDTH), BF16)]
        + [pltpu.VMEM(*v) for v in saved]
        + [pltpu.VMEM((1, D), F32), pltpu.SemaphoreType.DMA((12,))],
        compiler_params=pltpu.CompilerParams(vmem_limit_bytes=32 * 1024 * 1024),
        cost_estimate=COST,
    )(at, first, second, bias, wo, *pieces)


def backward_kernel(
    half, at_ref, x_ref, gab_ref, wo_ref, qkv_in, forget_in, probs_in, own_ref, sister_ref, far_ref, cross_ref,
    low_ref, dqkvf_ref, gain_grad_ref, qkv_ref, forget_ref, probs_ref, w_ref, sem,
):
    rows = pl.ds(2 * ROWS * half, 2 * ROWS)
    saved = [
        pltpu.make_async_copy(qkv_in.at[rows], qkv_ref, sem.at[4]),
        pltpu.make_async_copy(forget_in.at[rows], forget_ref, sem.at[5]),
        pltpu.make_async_copy(probs_in.at[pl.ds(2 * half, 2)], probs_ref, sem.at[6]),
    ]
    copies = column_copies(at_ref[2], (own_ref, sister_ref, far_ref, cross_ref), w_ref, sem)
    for copy in saved + copies:
        copy.start()
    gm = dot(gab_ref[...], wo_ref[...], ABT).astype(BF16)
    for copy in saved:
        copy.wait()

    lane = lax.broadcasted_iota(jnp.int32, (ROWS, 128), 1)
    left = lane < HD
    upper = lax.broadcasted_iota(jnp.int32, (ROWS, ROWS), 0) <= lax.broadcasted_iota(jnp.int32, (ROWS, ROWS), 1)
    ones = jnp.ones((ROWS, 128), BF16)
    for block in range(2):
        at = slice(block * ROWS, block * ROWS + ROWS)
        grad_decays = jnp.zeros((ROWS, 128), F32)
        for pair in range(LOCAL_HEADS // 2):
            first = 128 * pair
            q2, k2, v2 = (qkv_ref[at, SHARD * n + first : SHARD * n + first + 128] for n in range(3))
            g2 = gm[at, first : first + 128]
            zero = jnp.zeros_like(k2)
            keys = jnp.concatenate([jnp.where(left, k2, zero), jnp.where(left, zero, k2)], axis=0)
            values = jnp.concatenate([jnp.where(left, v2, zero), jnp.where(left, zero, v2)], axis=0)
            both = dot(g2, values, ABT)
            grads, low = [], []
            for side in range(2):
                probs = probs_ref[block, 2 * pair + side]
                grad_probs = both[:, ROWS * side : ROWS * side + ROWS]
                inner = jnp.sum(probs * grad_probs, axis=1, keepdims=True)
                grads.append((probs * (grad_probs - inner)).astype(BF16))
                low.append(probs.astype(BF16))
            grads, low = jnp.concatenate(grads, axis=1), jnp.concatenate(low, axis=1)
            pick = lambda v: jnp.where(left, v[:ROWS], v[ROWS:])
            dq = dot(grads, keys, AB) * (HD ** (-0.5))
            dk = pick(dot(grads, q2, ATB)) * (HD ** (-0.5))
            for n, value in enumerate((dq, dk, pick(dot(low, g2, ATB)))):
                dqkvf_ref[at, SHARD * n + first : SHARD * n + first + 128] = value.astype(BF16)
            over_queries = dot(grads, ones, ATB)
            for side in range(2):
                here = lane == 2 * pair + side
                over_keys = dot(grads[:, ROWS * side : ROWS * side + ROWS], here.astype(BF16), AB)
                grad_decays = grad_decays + over_keys
                grad_decays = grad_decays - jnp.where(here, over_queries[ROWS * side : ROWS * side + ROWS], 0.0)
        grad_logs = exact_dot(upper.astype(F32), grad_decays)
        dqkvf_ref[at, 3 * SHARD :] = (grad_logs * jax.nn.sigmoid(-forget_ref[at, :])).astype(BF16)

    for copy in copies:
        copy.wait()
    scaled = []
    for block in range(2):
        x = x_ref[block, :ROWS].astype(F32)
        scaled.append(x * lax.rsqrt(jnp.mean(x * x, axis=1, keepdims=True) + EPSILON))
    for col in range(4):
        lanes = slice(SHARD * col, SHARD * col + SHARD)
        incoming = dot(dqkvf_ref[...], w_ref[lanes, :], ABT)
        low_ref[:, lanes] = incoming.astype(BF16)
        gain_grad_ref[:, lanes] = sum(
            jnp.sum(incoming[ROWS * n : ROWS * n + ROWS] * scaled[n][:, lanes], axis=0, keepdims=True) for n in range(2)
        )


def attention_backward(half, at, x, gab, wo, qkv, forget, probs, pieces):
    vmem, anywhere = pl.BlockSpec(memory_space=pltpu.VMEM), pl.BlockSpec(memory_space=pltpu.HBM)
    return pl.pallas_call(
        functools.partial(backward_kernel, half),
        in_specs=[pl.BlockSpec(memory_space=pltpu.SMEM)] + [vmem] * 3 + [anywhere] * 7,
        out_specs=[vmem] * 3,
        out_shape=[
            jax.ShapeDtypeStruct((2 * ROWS, D), BF16),
            jax.ShapeDtypeStruct((2 * ROWS, WIDTH), BF16),
            jax.ShapeDtypeStruct((1, D), F32),
        ],
        scratch_shapes=[
            pltpu.VMEM((2 * ROWS, 3 * SHARD), BF16),
            pltpu.VMEM((2 * ROWS, 128), F32),
            pltpu.VMEM((2, LOCAL_HEADS, ROWS, ROWS), F32),
            pltpu.VMEM((D, WIDTH), BF16),
            pltpu.SemaphoreType.DMA((7,)),
        ],
        compiler_params=pltpu.CompilerParams(vmem_limit_bytes=24 * 1024 * 1024),
        cost_estimate=COST,
    )(at, x, gab, wo, qkv, forget, probs, *pieces)


FBLOCK = 256


def ffn_kernel(
    at_ref, first_ref, second_ref, gb_ref, wd_ref, gate_ref, up_ref, sister_ref, z_ref, z_other_ref, y_ref, y_other_ref,
    keep_ref, send_ref, hidden_ref, dg_ref, du_ref, n2_ref, w_ref, sem,
):
    j, bit_z, bit_y = at_ref[2], at_ref[3], at_ref[4]
    lanes = pl.ds(pl.multiple_of(j * FSHARD, FSHARD), FSHARD)

    def rows(r, first, count):
        return pl.ds(pl.multiple_of((r ^ j) * SHARD + first, 192), count)

    half = SHARD // 2
    pieces = (
        (sister_ref, rows(1, 0, SHARD)),
        (z_ref, rows(2, bit_z * half, half)),
        (z_other_ref, rows(2, half - bit_z * half, half)),
        (y_ref, rows(3, bit_y * half, half)),
        (y_other_ref, rows(3, half - bit_y * half, half)),
    )
    own = rows(0, 0, SHARD)
    fill(
        [
            (gate_ref.at[:, lanes], w_ref.at[own, pl.ds(0, FSHARD)], sem.at[0]),
            (up_ref.at[:, lanes], w_ref.at[own, pl.ds(FSHARD, FSHARD)], sem.at[1]),
        ]
        + [(ref, w_ref.at[at], sem.at[2 + n]) for n, (ref, at) in enumerate(pieces)]
    )
    n2_ref[: 2 * ROWS] = first_ref[...]
    n2_ref[2 * ROWS :] = second_ref[...]
    n2, gb = n2_ref[...], gb_ref[...]
    for step in range(FSHARD // FBLOCK):
        cols = slice(step * FBLOCK, step * FBLOCK + FBLOCK)
        gate = dot(n2, w_ref[:, cols], AB)
        up = dot(n2, w_ref[:, FSHARD + step * FBLOCK : FSHARD + step * FBLOCK + FBLOCK], AB)
        grad_hidden = dot(gb, wd_ref[cols, :], ABT)
        sig = jax.nn.sigmoid(gate)
        act = gate * sig
        hidden_ref[:, cols] = (act * up).astype(BF16)
        dg_ref[:, cols] = (grad_hidden * up * sig * (1.0 + gate * (1.0 - sig))).astype(BF16)
        du_ref[:, cols] = (grad_hidden * act).astype(BF16)
    for step in range(4):
        feat = slice(step * SHARD, step * SHARD + SHARD)
        part = dot(dg_ref[...], w_ref[feat, :FSHARD], ABT) + dot(du_ref[...], w_ref[feat, FSHARD:], ABT)
        part = part.astype(BF16)
        keep_ref[:, feat] = part[: 2 * ROWS]
        send_ref[:, feat] = part[2 * ROWS :]


def ffn(at, first, second, gb, wd, w_gate, w_up, pieces):
    vmem = pl.BlockSpec(memory_space=pltpu.VMEM)
    wide = [jax.ShapeDtypeStruct((4 * ROWS, FSHARD), BF16)] * 3
    return pl.pallas_call(
        ffn_kernel,
        in_specs=[pl.BlockSpec(memory_space=pltpu.SMEM)] + [vmem] * 4 + [pl.BlockSpec(memory_space=pltpu.HBM)] * 7,
        out_specs=[vmem] * 6,
        out_shape=[jax.ShapeDtypeStruct((2 * ROWS, D), BF16)] * 2 + wide + [jax.ShapeDtypeStruct((4 * ROWS, D), BF16)],
        scratch_shapes=[pltpu.VMEM((D, 2 * FSHARD), BF16), pltpu.SemaphoreType.DMA((7,))],
        compiler_params=pltpu.CompilerParams(vmem_limit_bytes=32 * 1024 * 1024),
        cost_estimate=COST,
    )(at, first, second, gb, wd, w_gate, w_up, *pieces)


STAGES = ((1, 3), (3, 1))


def labels(j):
    core = j & 1
    return (0, 3 - 2 * core, 1 + 2 * core, 2)


def piece_of(part, index, label):
    a, b = label[index // 4], label[index % 4]
    return (b, a) if part == 0 else (a, b)


def place(outs, part, index):
    return outs[2 * part + index // 8], index % 8


FUNITS = 72
QUNITS = ((0, 8), (8, 15))
OUNITS = ((0, 8), (8, 18))
AUNITS = tuple(4 * (q1 - q0) + (o1 - o0) for (q0, q1), (o0, o1) in zip(QUNITS, OUNITS))
NQ, NO = 240, 288


def ffn_grad_kernel(part, at_ref, n2_ref, gb_ref, hidden_ref, grad_ref, keep_ref, send_ref, cols_ref, down_ref):
    y, z, j = at_ref[0], at_ref[1], at_ref[2]
    label = labels(j)
    n2 = n2_ref[...]
    for step in range(4):
        pz = label[step] ^ z
        lanes = pl.ds(pl.multiple_of(pz * FBLOCK, FBLOCK), FBLOCK)
        cols_ref[...] = dot(n2, grad_ref[:, lanes], ATB).astype(BF16).reshape(16, 96, FBLOCK)
        gb = gb_ref[:, 768 * part : 768 * part + 768]
        down_ref[...] = dot(hidden_ref[:, lanes], gb, ATB).astype(BF16).reshape(4, 64, 768)
        for other in range(4):
            py = label[other] ^ y
            index = 4 * step + other if part == 0 else 4 * other + step
            out, slot = (keep_ref, send_ref)[index // 8], index % 8
            for r in range(4):
                for half in range(2):
                    block = cols_ref[(r ^ j) * 4 + py, :, 128 * half : 128 * half + 128]
                    out[slot, 12 * r + 6 * half : 12 * r + 6 * half + 6] = block.reshape(6, 16, 128)
            for t in range(6):
                block = down_ref[py, :, 128 * t : 128 * t + 128]
                out[slot, 48 + 4 * t : 52 + 4 * t] = block.reshape(4, 16, 128)


def ffn_gradients(part, at, n2, gb, hidden, grad):
    vmem = pl.BlockSpec(memory_space=pltpu.VMEM)
    return pl.pallas_call(
        functools.partial(ffn_grad_kernel, part),
        in_specs=[pl.BlockSpec(memory_space=pltpu.SMEM)] + [vmem] * 4,
        out_specs=[vmem] * 2,
        out_shape=[jax.ShapeDtypeStruct((8, FUNITS, 16, 128), BF16)] * 2,
        scratch_shapes=[pltpu.VMEM((16, 96, FBLOCK), BF16), pltpu.VMEM((4, 64, 768), BF16)],
        compiler_params=pltpu.CompilerParams(vmem_limit_bytes=20 * 1024 * 1024),
        cost_estimate=COST,
    )(at, n2, gb, hidden, grad)


def ffn_unpack_kernel(at_ref, *refs):
    ins, (gate_ref, up_ref, down_ref) = refs[:4], refs[4:]
    y, z, j = at_ref[0], at_ref[1], at_ref[2]
    label = labels(j)
    for part in range(2):
        target = (gate_ref, up_ref)[part]
        for index in range(16):
            ry, rz = piece_of(part, index, label)
            source, slot = place(ins, part, index)
            py, pz = ry ^ y, rz ^ z
            rows = pl.ds(pl.multiple_of(py * 96, 32), 96)
            for r in range(4):
                for half in range(2):
                    left = (r ^ j) * FSHARD + pz * FBLOCK + half * 128
                    block = source[slot, 12 * r + 6 * half : 12 * r + 6 * half + 6].reshape(96, 128)
                    target[rows, pl.ds(pl.multiple_of(left, 128), 128)] = block.astype(F32)
            rows = pl.ds(pl.multiple_of(pz * 256 + py * 64, 64), 64)
            for t in range(6):
                left = 768 * part + 128 * t
                block = source[slot, 48 + 4 * t : 52 + 4 * t].reshape(64, 128)
                down_ref[rows, left : left + 128] = block.astype(F32)


def ffn_unpack(at, pieces):
    vmem = pl.BlockSpec(memory_space=pltpu.VMEM)
    return pl.pallas_call(
        ffn_unpack_kernel,
        in_specs=[pl.BlockSpec(memory_space=pltpu.SMEM)] + [vmem] * 4,
        out_specs=[vmem] * 3,
        out_shape=[
            jax.ShapeDtypeStruct((SHARD, FF), F32),
            jax.ShapeDtypeStruct((SHARD, FF), F32),
            jax.ShapeDtypeStruct((FSHARD, D), F32),
        ],
        compiler_params=pltpu.CompilerParams(vmem_limit_bytes=40 * 1024 * 1024),
        cost_estimate=COST,
    )(at, *pieces)


def attention_grad_kernel(at_ref, normed_ref, d1_ref, d2_ref, mixed_ref, g1_ref, g2_ref, gains_ref, *rest):
    outs, (q_ref, o_ref) = rest[:4], rest[4:]
    y, z, j = at_ref[0], at_ref[1], at_ref[2]
    label = labels(j)
    d1, d2 = d1_ref[...], d2_ref[...]
    upper, lower = pl.ds(0, 2 * ROWS), pl.ds(2 * ROWS, 2 * ROWS)
    row = lax.broadcasted_iota(jnp.int32, (16, 128), 0)
    lane = lax.broadcasted_iota(jnp.int32, (16, 128), 1)
    pick = (lane == row + LOCAL_HEADS).astype(BF16)
    pick = jnp.where(row < 2, pick, jnp.zeros_like(pick))
    bias = sum(jnp.sum(d[:, 3 * SHARD :].astype(F32), axis=0, keepdims=True) for d in (d1, d2))
    bias = pltpu.roll(bias, 8, 1)

    def units(source, width, per, p, t):
        odd = (p & 1) == 1
        group = (p >> 1) * 3 + jnp.where(odd, (per + t) // width, t // width)
        return source[group, jnp.where(odd, (per + t) % width, t % width)]

    def piece(part, index):
        ry, rz = piece_of(part, index, label)
        return (ry ^ y) * 4 + (rz ^ z)

    for r in range(4):
        lanes = pl.ds(pl.multiple_of((r ^ j) * SHARD, SHARD), SHARD)
        grad = dot(normed_ref[upper, lanes], d1, ATB) + dot(normed_ref[lower, lanes], d2, ATB)
        extra = grad[:, 3 * SHARD :] + dot(gains_ref[:, lanes], pick, ATB) + bias
        for col in range(9):
            block = grad[:, 128 * col : 128 * col + 128].astype(BF16).reshape(24, 1, 16, 128)
            q_ref[:, col : col + 1] = block
        q_ref[:, 9:10] = extra.astype(BF16).reshape(24, 1, 16, 128)
        for part in range(2):
            lo, hi = QUNITS[part]
            for index in range(16):
                out, slot = place(outs, part, index)
                for t in range(lo, hi):
                    out[slot, (hi - lo) * r + t - lo] = units(q_ref, 10, 15, piece(part, index), t)
    grad = dot(mixed_ref[upper, :], g1_ref[...], ATB) + dot(mixed_ref[lower, :], g2_ref[...], ATB)
    for col in range(12):
        o_ref[:, col : col + 1] = grad[:, 128 * col : 128 * col + 128].astype(BF16).reshape(24, 1, 16, 128)
    for part in range(2):
        lo, hi = OUNITS[part]
        first = AUNITS[part] - (hi - lo)
        for index in range(16):
            out, slot = place(outs, part, index)
            for t in range(lo, hi):
                out[slot, first + t - lo] = units(o_ref, 12, 18, piece(part, index), t)


def attention_gradients(at, normed, d1, d2, mixed, g1, g2, gains):
    vmem = pl.BlockSpec(memory_space=pltpu.VMEM)
    return pl.pallas_call(
        attention_grad_kernel,
        in_specs=[pl.BlockSpec(memory_space=pltpu.SMEM)] + [vmem] * 7,
        out_specs=[vmem] * 4,
        out_shape=[jax.ShapeDtypeStruct((8, AUNITS[i // 2], 16, 128), BF16) for i in range(4)],
        scratch_shapes=[
            pltpu.VMEM((24, 10, 16, 128), BF16),
            pltpu.VMEM((24, 12, 16, 128), BF16),
        ],
        compiler_params=pltpu.CompilerParams(vmem_limit_bytes=26 * 1024 * 1024),
        cost_estimate=pl.CostEstimate(
            flops=2 * 4 * ROWS * D * (WIDTH + SHARD), bytes_accessed=10 * 1024 * 1024, transcendentals=0
        ),
    )(at, normed, d1, d2, mixed, g1, g2, gains)


def attention_unpack_kernel(at_ref, *refs):
    ins, (gq_ref, gk_ref, gv_ref, go_ref, forget_ref, small_ref, q_ref, o_ref) = refs[:4], refs[4:]
    y, z, j = at_ref[0], at_ref[1], at_ref[2]
    label = labels(j)
    for part in range(2):
        qlo, qhi = QUNITS[part]
        olo, ohi = OUNITS[part]
        n = qhi - qlo
        for index in range(16):
            ry, rz = piece_of(part, index, label)
            source, slot = place(ins, part, index)
            p = (ry ^ y) * 4 + (rz ^ z)
            for r in range(4):
                q_ref[r ^ j, pl.ds(p * 15 + qlo, n)] = source[slot, n * r : n * r + n]
            o_ref[pl.ds(p * 18 + olo, ohi - olo)] = source[slot, 4 * n : 4 * n + ohi - olo]
    for group in range(24):
        rows = slice(16 * group, 16 * group + 16)
        for device in range(4):
            for col in range(10):
                if col < 9:
                    target = (gq_ref, gk_ref, gv_ref)[col // 3]
                    left = SHARD * device + 128 * (col % 3)
                    target[rows, left : left + 128] = q_ref[device, 10 * group + col].astype(F32)
        for col in range(12):
            go_ref[rows, 128 * col : 128 * col + 128] = o_ref[12 * group + col].astype(F32)
    lane = lax.broadcasted_iota(jnp.int32, (128, 128), 1)
    for third in range(3):
        forget = jnp.zeros((128, 128), F32)
        total = jnp.zeros((128, 128), F32)
        for device in range(4):
            parts = [q_ref[device, 10 * group + 9] for group in range(8 * third, 8 * third + 8)]
            extra = jnp.concatenate(parts, axis=0).astype(F32)
            mine = (lane >= LOCAL_HEADS * device) & (lane < LOCAL_HEADS * device + LOCAL_HEADS)
            moved = pltpu.roll(extra, LOCAL_HEADS * device, 1) if device else extra
            forget = jnp.where(mine, moved, forget)
            total = total + extra
        forget_ref[:, 128 * third : 128 * third + 128] = forget.T[:H]
        small_ref[:, 128 * third : 128 * third + 128] = total.T[:16]
    first = q_ref[j, pl.ds(9, 1)].astype(F32)
    small_ref[8:16, 0:128] = first.reshape(16, 128)[:8]


def attention_unpack(at, pieces):
    vmem = pl.BlockSpec(memory_space=pltpu.VMEM)
    return pl.pallas_call(
        attention_unpack_kernel,
        in_specs=[pl.BlockSpec(memory_space=pltpu.SMEM)] + [vmem] * 4,
        out_specs=[vmem] * 6,
        out_shape=[jax.ShapeDtypeStruct((SHARD, D), F32)] * 4
        + [jax.ShapeDtypeStruct((H, SHARD), F32), jax.ShapeDtypeStruct((16, SHARD), F32)],
        scratch_shapes=[
            pltpu.VMEM((4, NQ, 16, 128), BF16),
            pltpu.VMEM((NO, 16, 128), BF16),
        ],
        compiler_params=pltpu.CompilerParams(vmem_limit_bytes=24 * 1024 * 1024),
        cost_estimate=COST,
    )(at, *pieces)


def small_call(kernel, out, *args):
    vmem = pl.BlockSpec(memory_space=pltpu.VMEM)
    return pl.pallas_call(
        kernel,
        in_specs=[vmem] * len(args),
        out_specs=[vmem] * len(out),
        out_shape=[jax.ShapeDtypeStruct((n, 16, 128), BF16) for n in out],
        compiler_params=pltpu.CompilerParams(vmem_limit_bytes=8 * 1024 * 1024),
        cost_estimate=COST,
    )(*args)


def add_slots(held, first, count):
    n = held[0].shape[1]

    def kernel(*refs):
        refs[-1][...] = functools.reduce(lambda a, b: a + b, [ref[...].astype(F32) for ref in refs[:-1]]).astype(BF16)

    return pl.pallas_call(
        kernel,
        grid=(1,),
        in_specs=[pl.BlockSpec((count, n, 16, 128), lambda i: (first // count, 0, 0, 0))] * len(held),
        out_specs=pl.BlockSpec((count, n, 16, 128), lambda i: (0, 0, 0, 0)),
        out_shape=jax.ShapeDtypeStruct((count, n, 16, 128), BF16),
        compiler_params=pltpu.CompilerParams(vmem_limit_bytes=20 * 1024 * 1024),
        cost_estimate=COST,
    )(*held)


def join(upper, lower):
    slots, n = upper.shape[:2]

    def kernel(upper_ref, lower_ref, out_ref):
        out_ref[:slots] = upper_ref[...]
        out_ref[slots:] = lower_ref[...]

    vmem = pl.BlockSpec(memory_space=pltpu.VMEM)
    return pl.pallas_call(
        kernel,
        in_specs=[vmem] * 2,
        out_specs=vmem,
        out_shape=jax.ShapeDtypeStruct((2 * slots, n, 16, 128), BF16),
        compiler_params=pltpu.CompilerParams(vmem_limit_bytes=8 * 1024 * 1024),
        cost_estimate=COST,
    )(upper, lower)


def for_sister(pieces, columns):
    def kernel(first_ref, second_ref, out_ref):
        at = 0
        for r in (1, 3):
            for ref, n in zip((first_ref, second_ref), columns):
                out_ref[at : at + n] = ref[r * n : r * n + n]
                at += n

    return small_call(kernel, [2 * sum(columns)], *pieces)[0]


def for_chips(pieces, sister, columns):
    n = sum(columns)
    tails = [p.shape[0] - 4 * m for p, m in zip(pieces, columns)]

    def kernel(first_ref, second_ref, sister_ref, near_ref, far_ref):
        at, tail = 0, 2 * n
        for ref, m, last in zip((first_ref, second_ref), columns, tails):
            near_ref[at : at + m] = ref[0:m]
            far_ref[at : at + m] = ref[2 * m : 3 * m]
            near_ref[tail : tail + last] = ref[4 * m : 4 * m + last]
            at, tail = at + m, tail + last
        near_ref[n : 2 * n] = sister_ref[0:n]
        far_ref[n : 2 * n] = sister_ref[n : 2 * n]

    return small_call(kernel, [2 * n + sum(tails), 2 * n], *pieces, sister)


def join_chips(near, far, a, b, t, columns):
    n = sum(columns)
    last = near.shape[0] - 2 * n
    tails = [last // 2, last // 2] if columns[0] == columns[1] else [hi - lo for lo, hi in OUNITS]

    def kernel(near_ref, far_ref, a_ref, b_ref, t_ref, first_ref, second_ref):
        def total(x_ref, y_ref, lo, m):
            return (x_ref[lo : lo + m].astype(F32) + y_ref[lo : lo + m].astype(F32)).astype(BF16)

        at, tail = 0, 2 * n
        for ref, m, end in zip((first_ref, second_ref), columns, tails):
            ref[0:m] = total(near_ref, t_ref, at, m)
            ref[m : 2 * m] = total(near_ref, t_ref, n + at, m)
            ref[2 * m : 3 * m] = total(a_ref, b_ref, at, m)
            ref[3 * m : 4 * m] = total(a_ref, b_ref, n + at, m)
            ref[4 * m : 4 * m + end] = total(near_ref, t_ref, tail, end)
            at, tail = at + m, tail + end

    return small_call(kernel, [4 * m + end for m, end in zip(columns, tails)], near, far, a, b, t)


def make_body(sizes):
    ny, nxh, nz = sizes

    def send(value, move):
        pairs = []
        for y in range(ny):
            for x in range(2 * nxh):
                for z in range(nz):
                    for c in range(2):
                        ty, tx, tz, tc = move(y, x, z, c)
                        tx %= 2 * nxh
                        src = (((y * nxh + x // 2) * nz + z) * 2 + x % 2) * 2 + c
                        dst = (((ty * nxh + tx // 2) * nz + tz) * 2 + tx % 2) * 2 + tc
                        pairs.append((src, dst))
        return lax.ppermute(value, AXES, pairs)

    def swap_plane(value, axis, stage):
        if axis == "y":
            return send(value, lambda y, x, z, c: (y ^ STAGES[c][stage], x, z, c))
        return send(value, lambda y, x, z, c: (y, x, z ^ STAGES[c][stage], c))

    def after(value, *others):
        return lax.optimization_barrier((value, *others))[0]

    swap_core = lambda v: send(v, lambda y, x, z, c: (y, x, z, 1 - c))
    swap_x = lambda v: send(v, lambda y, x, z, c: (y, x ^ 1, z, c))
    swap_out = lambda v: send(v, lambda y, x, z, c: (y, x ^ 3, z, c))
    cross_mixed = lambda v: send(v, lambda y, x, z, c: (y, x ^ (1 if c else 3), z, 1 - c))
    cross_x = lambda v: send(v, lambda y, x, z, c: (y, x ^ 1, z, 1 - c))
    x_plus = lambda v: send(v, lambda y, x, z, c: (y, x + 1, z, c))
    x_minus = lambda v: send(v, lambda y, x, z, c: (y, x - 1, z, c))
    x_two = lambda v: send(v, lambda y, x, z, c: (y, x + 2, z, c))

    def total(parts):
        return functools.reduce(lambda a, b: a + b, [p.astype(F32) for p in parts])

    def combine(keep, received):
        return total([keep, received]).astype(BF16)

    class Order:
        def __init__(self):
            self.work = ()

        def arrive(self, *values):
            out = lax.optimization_barrier((*values, *self.work))[: len(values)]
            return out if len(values) > 1 else out[0]

        def then(self, *work):
            self.work = work

    def move(part, step):
        return ("zy"[part != step // 2], step % 2)

    class Lane:
        def __init__(self, order, part, keep, sending):
            self.order, self.part, self.held, self.sending, self.step = order, part, [keep], sending, 0

        def start(self):
            self.got = swap_plane(self.sending, *move(self.part, self.step))

        def arrive(self):
            self.held.append(self.order.arrive(self.got))
            half = 4 >> self.step
            self.sending = add_slots(self.held, half, max(half, 1))
            self.order.then(self.sending)
            self.step += 1

        def gather(self, piece):
            self.sending, self.step = piece[None], 3

        def collect(self):
            self.got = self.order.arrive(self.got)
            if self.step:
                self.sending = join(self.sending, self.got)
                self.order.then(self.sending)
            self.step -= 1

    def together(order, lanes):
        for lane, got in zip(lanes, order.arrive(*[lane.got for lane in lanes])):
            lane.got = got

    def both(lanes, *names):
        for name in names:
            for lane in lanes:
                getattr(lane, name)()

    def each(lanes, *names):
        for lane in lanes:
            for name in names:
                getattr(lane, name)()

    def spread_steps(order, pieces, columns):
        sister = swap_core(for_sister(pieces, columns))
        yield
        sister = order.arrive(sister)
        near, far = for_chips(pieces, sister, columns)
        order.then(far, near)
        a, b, t = x_plus(far), x_minus(far), x_two(near)
        yield
        a, b, t = order.arrive(a, b, t)
        out = join_chips(near, far, a, b, t, columns)
        order.then(*out)
        return out

    def finish(steps):
        try:
            next(steps)
        except StopIteration as stop:
            return stop.value

    def body(
        tokens, lengths, w_query, w_key, w_value, w_out, w_forget, forget_bias, norm_attn,
        w_gate, w_up, w_down, norm_ffn, cotangent,
    ):
        y, z, core = lax.axis_index("y"), lax.axis_index("z"), lax.axis_index("c")
        j = lax.axis_index("xl") * 2 + core
        bits = [(jnp.where(n == 0, z & 1, z >> 1), jnp.where(n == 0, y & 1, y >> 1)) for n in (core, 1 - core)]
        (bit_z, bit_y), (_, sister_bit_y) = bits
        at = jnp.stack([y, z, j, bit_z, bit_y, sister_bit_y]).astype(jnp.int32)

        own_cols, far_cols, sister_cols, cross_cols = columns(at, w_query, w_key, w_value, w_forget.T)
        far, cross, sister = swap_out(far_cols), cross_mixed(cross_cols), swap_core(sister_cols)
        cot_first = swap_x(after(cotangent, far_cols))

        small = jnp.concatenate([norm_attn, norm_ffn, lengths[0].astype(BF16)])
        small = after(small, far_cols)
        small = jnp.pad(small[None], ((0, 15), (0, D - small.shape[0])))
        packed = jnp.concatenate([tokens, small], axis=0)
        packed_first = swap_x(packed)

        sister_gu, cross_gu, far_gu = gate_up_columns(after(at, far_cols, packed), w_gate, w_up)

        order = Order()
        order.then(far_gu)
        packed_first = order.arrive(packed_first)
        pair = jnp.stack([packed, packed_first])
        order.then(pair)
        packed_second = swap_core(pair)
        sister, cross, far, cot_first = order.arrive(sister, cross, far, cot_first)
        order.then(sister, cross, far)
        fetch_z = swap_out(after(far_gu, far))
        fetch_y = cross_x(after(cross_gu, cross))
        sister_gu = swap_core(after(sister_gu, sister))
        packed_all = jnp.concatenate([pair, order.arrive(packed_second)], axis=0)
        x_rows = packed_all[:, :ROWS].reshape(4 * ROWS, D)
        small_all = packed_all[:, ROWS]
        lens = small_all[:, 2 * SHARD : 2 * SHARD + SLOTS].astype(jnp.int32)
        by_device = jnp.stack([small_all[0], small_all[2], small_all[1], small_all[3]])
        by_device = jnp.concatenate(
            [lax.dynamic_index_in_dim(by_device, j ^ r, 0, keepdims=True) for r in range(4)], axis=0
        ).astype(F32)
        gain_one = by_device[:, :SHARD].reshape(1, D)
        gain_two = by_device[:, SHARD : 2 * SHARD].reshape(1, D)
        bias = jnp.pad(forget_bias.astype(F32), (0, 128 - LOCAL_HEADS))[None]

        keep, sent, normed, qkv, forget, probs, mixed = attention_forward(
            at, pair, packed_second, bias, w_out, (own_cols, sister, far, cross)
        )
        first, fetch_z, fetch_y, sister_gu = lax.optimization_barrier(
            (swap_core(sent), fetch_z, fetch_y, sister_gu)
        )
        chip = combine(keep, first)
        other = swap_x(chip)
        other_z, other_y = swap_plane(fetch_z, "z", 0), swap_plane(fetch_y, "y", 0)
        cot_pair = jnp.stack([cotangent, after(cot_first, chip)])
        cot_rows = jnp.concatenate([cot_pair, swap_core(cot_pair)], axis=0).reshape(4 * ROWS, D)
        live = (jnp.arange(ROWS)[None, :] < jnp.sum(lens, axis=1, keepdims=True)).reshape(4 * ROWS, 1)
        grad_branch = jnp.where(live, cot_rows, jnp.zeros_like(cot_rows))
        other, other_z, other_y, grad_branch = lax.optimization_barrier((other, other_z, other_y, grad_branch))

        def both_chips(chip, other):
            return chip.astype(F32) + jnp.concatenate([other[ROWS:], other[:ROWS]], axis=0).astype(F32)

        middle = x_rows[: 2 * ROWS].astype(F32) + both_chips(chip, other)
        factor_two = lax.rsqrt(jnp.mean(middle * middle, axis=1, keepdims=True) + EPSILON)
        n2_half = (middle * factor_two * gain_two).astype(BF16)
        n2_other = swap_core(n2_half)

        keep, sent, hidden, dgate, dup, n2 = ffn(
            at, n2_half, n2_other, grad_branch, w_down, w_gate, w_up, (sister_gu, fetch_z, other_z, fetch_y, other_y)
        )
        order = Order()
        first = swap_core(sent)
        ffn_parts = ffn_gradients(0, at, n2, grad_branch, hidden, dgate)
        order.then(ffn_parts[0])
        chip = combine(keep, order.arrive(first))
        ffn_parts = ffn_parts + ffn_gradients(1, at, after(n2, chip), grad_branch, hidden, dup)
        order.then(ffn_parts[2])
        ffn_lanes = [Lane(order, k, *ffn_parts[2 * k : 2 * k + 2]) for k in range(2)]
        both(ffn_lanes, "start")
        other = swap_x(chip)
        down = dot(after(hidden, ffn_parts[2]), w_down, AB).astype(BF16)
        order.then(down)
        incoming_two = both_chips(chip, order.arrive(other))
        scaled = incoming_two * gain_two
        inner = jnp.mean(scaled * middle, axis=1, keepdims=True)
        grad_middle = grad_branch[: 2 * ROWS].astype(F32) + (
            scaled * factor_two - middle * (factor_two * factor_two * factor_two) * inner
        )
        gain_two_part = 0.5 * jnp.sum(incoming_two * middle * factor_two, axis=0)
        gab_half = grad_middle.astype(BF16)
        order.then(gab_half)
        gab_other = swap_core(gab_half)
        down_first = swap_core(down[2 * ROWS :])

        kept = (w_out, qkv, forget, probs, (own_cols, sister, far, cross))
        keep, d1, gain_first = attention_backward(0, at, pair, gab_half, *kept)
        order.then(d1)
        each(ffn_lanes, "arrive", "start")
        gab_other = order.arrive(gab_other)
        sent, d2, gain_second = attention_backward(1, at, packed_second, gab_other, *kept)
        order.then(d2)
        token_first = swap_core(sent)
        each(ffn_lanes[:1], "arrive", "start")
        gains = jnp.concatenate([gain_first + gain_second, gain_two_part[None]], axis=0).astype(BF16)
        gains = jnp.pad(gains, ((0, 14), (0, 0)))
        attn_parts = attention_gradients(at, normed, d1, order.arrive(d2), mixed, gab_half, gab_other, gains)
        order.then(attn_parts[0])
        each(ffn_lanes[1:], "arrive", "start")
        down_chip, token_chip = combine(down[: 2 * ROWS], down_first), combine(keep, order.arrive(token_first))
        order.then(down_chip, token_chip)
        down_other, token_other = swap_x(down_chip[ROWS:]), swap_x(token_chip[ROWS:])
        each(ffn_lanes, "arrive", "start")
        each(ffn_lanes, "arrive")
        attn_parts = after(attn_parts, ffn_lanes[1].sending)
        attn_lanes = [Lane(order, k, *attn_parts[2 * k : 2 * k + 2]) for k in range(2)]
        both(attn_lanes, "start")
        ffn_spread = spread_steps(order, [lane.sending[0] for lane in ffn_lanes], [12, 12])
        next(ffn_spread)
        next(ffn_spread)
        each(attn_lanes, "arrive", "start")
        ffn_pieces = finish(ffn_spread)
        for lane, piece in zip(ffn_lanes, ffn_pieces):
            lane.gather(piece)
        both(ffn_lanes, "start")

        def next_step(lanes, name):
            together(order, lanes)
            each(lanes, name, "start")

        next_step(ffn_lanes, "collect")
        next_step(attn_lanes, "arrive")
        next_step(ffn_lanes, "collect")
        next_step(attn_lanes, "arrive")
        together(order, attn_lanes)
        each(attn_lanes, "arrive")
        attn_spread = spread_steps(
            order, [lane.sending[0] for lane in attn_lanes], [hi - lo for lo, hi in QUNITS]
        )
        next(attn_spread)
        next_step(ffn_lanes, "collect")
        next(attn_spread)
        attn_pieces = finish(attn_spread)
        for lane, piece in zip(attn_lanes, attn_pieces):
            lane.gather(piece)
        both(attn_lanes, "start")
        next_step(attn_lanes, "collect")
        next_step(attn_lanes, "collect")
        down_other, token_other = order.arrive(down_other, token_other)
        together(order, ffn_lanes)
        each(ffn_lanes, "collect")
        grad_gate, grad_up, grad_down = ffn_unpack(at, [v for lane in ffn_lanes for v in (lane.sending, lane.got)])
        order.then(grad_down)
        next_step(attn_lanes, "collect")
        each(attn_lanes, "collect")
        branch = down_chip[:ROWS].astype(F32) + down_other.astype(F32)
        output = jnp.where(live[:ROWS], middle[:ROWS] + branch, 0.0).astype(BF16)

        own = x_rows[:ROWS].astype(F32)
        factor_one = lax.rsqrt(jnp.mean(own * own, axis=1, keepdims=True) + EPSILON)
        scaled = (token_chip[:ROWS].astype(F32) + token_other.astype(F32)) * gain_one
        inner = jnp.mean(scaled * own, axis=1, keepdims=True)
        grad_tokens = grad_middle[:ROWS] + (
            scaled * factor_one - own * (factor_one * factor_one * factor_one) * inner
        )

        grad_query, grad_key, grad_value, grad_out, grad_forget, small = attention_unpack(
            at, [v for lane in attn_lanes for v in (lane.sending, lane.got)]
        )
        grad_forget = grad_forget.T
        grad_norm_attn, grad_norm_ffn = small[LOCAL_HEADS], small[LOCAL_HEADS + 1]
        grad_bias = small[8, 8 : 8 + LOCAL_HEADS]
        return (
            output, grad_tokens, grad_query, grad_key, grad_value, grad_out, grad_forget, grad_bias,
            grad_norm_attn, grad_gate, grad_up, grad_down, grad_norm_ffn,
        )

    return body


SIZES = {32: (4, 2, 4), 16: (4, 1, 4)}


def solution(mesh):
    sizes = SIZES[mesh.shape["wide"]]
    ny, nxh, nz = sizes
    fine = Mesh(mesh.devices.reshape(ny, nxh, nz, 2, 2), AXES)
    rows, shard, vector = P(AXES, None), P(("xl", "c"), None), P(("xl", "c"))
    return jax.shard_map(
        make_body(sizes),
        mesh=fine,
        in_specs=(
            rows, rows, shard, shard, shard, shard, shard, vector, vector, shard, shard, shard, vector, rows,
        ),
        out_specs=(
            rows, rows, shard, shard, shard, shard, shard, vector, vector, shard, shard, shard, vector,
        ),
        check_vma=False,
    )
```

```python
import functools

import jax
import jax.numpy as jnp
from jax import lax
from jax.experimental import pallas as pl
from jax.experimental.pallas import tpu as pltpu
from jax.sharding import Mesh, PartitionSpec as P

D = 1536
H = 24
HD = 64
FF = 4096
ROWS = 128
SLOTS = 4
EPSILON = 1e-06
SHARD = D // 4
FSHARD = FF // 4
LOCAL_HEADS = H // 4
WIDTH = 3 * SHARD + 128
AXES = ("y", "xh", "z", "xl", "c")
PLANE = ("y", "z")
F32 = jnp.float32
BF16 = jnp.bfloat16


def dot(former, latter, dims):
    return lax.dot_general(former, latter, (dims, ((), ())), preferred_element_type=F32)


COST = pl.CostEstimate(flops=0, bytes_accessed=0, transcendentals=0)
GRADIENT_COST = pl.CostEstimate(flops=4 * 10**9, bytes_accessed=12 * 10**6, transcendentals=0)

AB = ((1,), (0,))
ABT = ((1,), (1,))
ATB = ((0,), (0,))


def exact_dot(former, latter):
    return lax.dot_general(
        former, latter, ((AB), ((), ())), precision=lax.Precision.HIGHEST, preferred_element_type=F32
    )


def attend_mask(lens):
    rows = lax.broadcasted_iota(jnp.int32, (ROWS, ROWS), 0).astype(F32)
    cols = lax.broadcasted_iota(jnp.int32, (ROWS, ROWS), 1).astype(F32)
    seg_rows = jnp.zeros((ROWS, ROWS), F32)
    seg_cols = jnp.zeros((ROWS, ROWS), F32)
    end = jnp.zeros((1, 1), F32)
    for slot in range(SLOTS):
        end = end + lens[:, slot : slot + 1]
        seg_rows = seg_rows + (rows >= end).astype(F32)
        seg_cols = seg_cols + (cols >= end).astype(F32)
    return (rows >= cols) & (seg_rows == seg_cols)


def fill(copies):
    copies = [pltpu.make_async_copy(*c) for c in copies]
    for c in copies:
        c.start()
    for c in copies:
        c.wait()


def columns_kernel(at_ref, f_ref, q_ref, k_ref, v_ref, own_ref, far_ref, sister_ref, cross_ref, held_ref, sem):
    j = at_ref[2]
    targets = (2, 3, 1, 0)
    ins = []
    for n, r in enumerate(targets):
        lanes = pl.ds(pl.multiple_of((r ^ j) * SHARD, SHARD), SHARD)
        for m, source in enumerate((q_ref, k_ref, v_ref)):
            target = held_ref.at[n, :, pl.ds(SHARD * m, SHARD)]
            ins.append(pltpu.make_async_copy(source.at[:, lanes], target, sem.at[3 * n + m]))
            ins[-1].start()
    forget = jnp.concatenate([f_ref[...].astype(F32), jnp.zeros((128 - H, SHARD), F32)], axis=0).T
    lane = lax.broadcasted_iota(jnp.int32, (SHARD, 128), 1)
    for n, r in enumerate(targets):
        mine = pltpu.roll(forget, lax.rem(128 - LOCAL_HEADS * (r ^ j), 128), 1)
        held_ref[n, :, 3 * SHARD :] = jnp.where(lane < LOCAL_HEADS, mine, 0.0).astype(BF16)
    for copy in ins:
        copy.wait()
    fill(
        [
            (held_ref.at[0], far_ref, sem.at[12]),
            (held_ref.at[1], cross_ref, sem.at[13]),
            (held_ref.at[2], sister_ref, sem.at[14]),
            (held_ref.at[3], own_ref, sem.at[15]),
        ]
    )


def columns(at, w_query, w_key, w_value, w_forget):
    anywhere = pl.BlockSpec(memory_space=pl.ANY)
    return pl.pallas_call(
        columns_kernel,
        in_specs=[pl.BlockSpec(memory_space=pltpu.SMEM), pl.BlockSpec(memory_space=pltpu.VMEM)] + [anywhere] * 3,
        out_specs=[anywhere] * 4,
        out_shape=[jax.ShapeDtypeStruct((SHARD, WIDTH), BF16)] * 4,
        scratch_shapes=[pltpu.VMEM((4, SHARD, WIDTH), BF16), pltpu.SemaphoreType.DMA((16,))],
        compiler_params=pltpu.CompilerParams(vmem_limit_bytes=60 * 1024 * 1024),
        cost_estimate=COST,
    )(at, w_forget, w_query, w_key, w_value)


def gate_up_columns_kernel(at_ref, gate_ref, up_ref, sister_ref, cross_ref, far_ref, held_ref, sem):
    j, bit_z, sister_bit_y = at_ref[2], at_ref[3], at_ref[5]
    half = SHARD // 2
    some = lambda bit: pl.ds(pl.multiple_of(bit * half, half), half)
    targets = ((1, sister_ref, pl.ds(0, SHARD)), (3, cross_ref, some(sister_bit_y)), (2, far_ref, some(bit_z)))
    ins, outs, first = [], [], 0
    for n, (r, ref, rows) in enumerate(targets):
        lanes = pl.ds(pl.multiple_of((r ^ j) * FSHARD, FSHARD), FSHARD)
        held = held_ref.at[pl.ds(first, ref.shape[0])]
        for m, source in enumerate((gate_ref, up_ref)):
            ins.append((source.at[rows, lanes], held.at[:, pl.ds(FSHARD * m, FSHARD)], sem.at[2 * n + m]))
        outs.append((held, ref, sem.at[6 + n]))
        first += ref.shape[0]
    fill(ins)
    fill(outs)


def gate_up_columns(at, w_gate, w_up):
    anywhere = pl.BlockSpec(memory_space=pl.ANY)
    return pl.pallas_call(
        gate_up_columns_kernel,
        in_specs=[pl.BlockSpec(memory_space=pltpu.SMEM)] + [anywhere] * 2,
        out_specs=[anywhere] * 3,
        out_shape=[jax.ShapeDtypeStruct((n, 2 * FSHARD), BF16) for n in (SHARD, SHARD // 2, SHARD // 2)],
        scratch_shapes=[pltpu.VMEM((2 * SHARD, 2 * FSHARD), BF16), pltpu.SemaphoreType.DMA((9,))],
        compiler_params=pltpu.CompilerParams(vmem_limit_bytes=60 * 1024 * 1024),
        cost_estimate=COST,
    )(at, w_gate, w_up)


def column_copies(j, pieces, w_ref, sem):
    rows = lambda r: pl.ds(pl.multiple_of((r ^ j) * SHARD, SHARD), SHARD)
    return [pltpu.make_async_copy(ref, w_ref.at[rows(r)], sem.at[r]) for r, ref in enumerate(pieces)]


def forward_kernel(
    at_ref, first_ref, second_ref, bias_ref, wo_ref, own_ref, sister_ref, far_ref, cross_ref,
    keep_ref, send_ref, normed_out, qkv_out, forget_out, probs_out, mixed_out,
    w_ref, normed_ref, qkv_ref, forget_ref, probs_ref, mixed_ref, gain_ref, sem,
):
    j = at_ref[2]
    copies = column_copies(j, (own_ref, sister_ref, far_ref, cross_ref), w_ref, sem)
    for copy in copies:
        copy.start()
    for r in range(4):
        lanes = pl.ds(pl.multiple_of((r ^ j) * SHARD, SHARD), SHARD)
        ref = (first_ref, second_ref)[r % 2]
        gain_ref[:, lanes] = ref[r // 2, ROWS : ROWS + 1, :SHARD].astype(F32)
    for block in range(4):
        x = (first_ref, second_ref)[block // 2][block % 2, :ROWS].astype(F32)
        factor = lax.rsqrt(jnp.mean(x * x, axis=1, keepdims=True) + EPSILON)
        normed_ref[block * ROWS : block * ROWS + ROWS] = (x * factor * gain_ref[...]).astype(BF16)
    for copy in copies:
        copy.wait()

    out = lambda ref, target, n: pltpu.make_async_copy(ref, target, sem.at[4 + n])
    leaving = [out(normed_ref, normed_out, 0)]
    leaving[0].start()
    normed = normed_ref[...]
    forget_ref[...] = dot(normed, w_ref[:, 3 * SHARD :], AB) + bias_ref[...]
    for col in range(3):
        lanes = slice(SHARD * col, SHARD * col + SHARD)
        qkv_ref[:, lanes] = dot(normed, w_ref[:, lanes], AB).astype(BF16)
    leaving += [out(forget_ref, forget_out, 1), out(qkv_ref, qkv_out, 2)]
    for copy in leaving[1:]:
        copy.start()

    rows = lax.broadcasted_iota(jnp.int32, (ROWS, ROWS), 0)
    cols = lax.broadcasted_iota(jnp.int32, (ROWS, ROWS), 1)
    lower = (rows >= cols).astype(F32)
    left = lax.broadcasted_iota(jnp.int32, (ROWS, 128), 1) < HD
    for block in range(4):
        at = slice(block * ROWS, block * ROWS + ROWS)
        lens = (first_ref, second_ref)[block // 2][block % 2, ROWS : ROWS + 1, 2 * SHARD : 2 * SHARD + SLOTS]
        decays = exact_dot(lower, jax.nn.log_sigmoid(forget_ref[at, :]))
        decays_t = decays.T
        allowed = attend_mask(lens.astype(F32))
        for pair in range(LOCAL_HEADS // 2):
            lane = 128 * pair
            q2, k2, v2 = (qkv_ref[at, SHARD * n + lane : SHARD * n + lane + 128] for n in range(3))
            zero = jnp.zeros_like(k2)
            keys = jnp.concatenate([jnp.where(left, k2, zero), jnp.where(left, zero, k2)], axis=0)
            values = jnp.concatenate([jnp.where(left, v2, zero), jnp.where(left, zero, v2)], axis=0)
            both = dot(q2, keys, ABT)
            low = []
            for side in range(2):
                head = 2 * pair + side
                scores = both[:, ROWS * side : ROWS * side + ROWS] * (HD ** (-0.5))
                scores = scores + decays[:, head : head + 1] - decays_t[head : head + 1, :]
                scores = jnp.where(allowed, scores, -1e30)
                highest = jnp.max(scores, axis=1, keepdims=True)
                weights = jnp.exp(scores - highest)
                probs = weights / jnp.sum(weights, axis=1, keepdims=True)
                probs_ref[block, head] = probs
                low.append(probs.astype(BF16))
            mixed_ref[at, lane : lane + 128] = dot(jnp.concatenate(low, axis=1), values, AB).astype(BF16)
        leaving.append(out(probs_ref.at[block], probs_out.at[block], 4 + block))
        leaving[-1].start()
    leaving.append(out(mixed_ref, mixed_out, 3))
    leaving[-1].start()
    for col in range(4):
        lanes = slice(SHARD * col, SHARD * col + SHARD)
        partial = dot(mixed_ref[...], wo_ref[:, lanes], AB).astype(BF16)
        keep_ref[:, lanes] = partial[: 2 * ROWS]
        send_ref[:, lanes] = partial[2 * ROWS :]
    for copy in leaving:
        copy.wait()


def attention_forward(at, first, second, bias, wo, pieces):
    vmem, anywhere = pl.BlockSpec(memory_space=pltpu.VMEM), pl.BlockSpec(memory_space=pltpu.HBM)
    saved = [
        ((4 * ROWS, D), BF16),
        ((4 * ROWS, 3 * SHARD), BF16),
        ((4 * ROWS, 128), F32),
        ((4, LOCAL_HEADS, ROWS, ROWS), F32),
        ((4 * ROWS, SHARD), BF16),
    ]
    return pl.pallas_call(
        forward_kernel,
        in_specs=[pl.BlockSpec(memory_space=pltpu.SMEM)] + [vmem] * 4 + [anywhere] * 4,
        out_specs=[vmem] * 2 + [anywhere] * 5,
        out_shape=[jax.ShapeDtypeStruct((2 * ROWS, D), BF16)] * 2 + [pltpu.HBM(*v) for v in saved],
        scratch_shapes=[pltpu.VMEM((D, WIDTH), BF16)]
        + [pltpu.VMEM(*v) for v in saved]
        + [pltpu.VMEM((1, D), F32), pltpu.SemaphoreType.DMA((12,))],
        compiler_params=pltpu.CompilerParams(vmem_limit_bytes=32 * 1024 * 1024),
        cost_estimate=COST,
    )(at, first, second, bias, wo, *pieces)


def backward_kernel(
    half, at_ref, x_ref, gab_ref, wo_ref, qkv_in, forget_in, probs_in, own_ref, sister_ref, far_ref, cross_ref,
    low_ref, dqkvf_ref, gain_grad_ref, qkv_ref, forget_ref, probs_ref, w_ref, sem,
):
    rows = pl.ds(2 * ROWS * half, 2 * ROWS)
    saved = [
        pltpu.make_async_copy(qkv_in.at[rows], qkv_ref, sem.at[4]),
        pltpu.make_async_copy(forget_in.at[rows], forget_ref, sem.at[5]),
        pltpu.make_async_copy(probs_in.at[pl.ds(2 * half, 2)], probs_ref, sem.at[6]),
    ]
    copies = column_copies(at_ref[2], (own_ref, sister_ref, far_ref, cross_ref), w_ref, sem)
    for copy in saved + copies:
        copy.start()
    gm = dot(gab_ref[...], wo_ref[...], ABT).astype(BF16)
    for copy in saved:
        copy.wait()

    lane = lax.broadcasted_iota(jnp.int32, (ROWS, 128), 1)
    left = lane < HD
    upper = lax.broadcasted_iota(jnp.int32, (ROWS, ROWS), 0) <= lax.broadcasted_iota(jnp.int32, (ROWS, ROWS), 1)
    ones = jnp.ones((ROWS, 128), BF16)
    for block in range(2):
        at = slice(block * ROWS, block * ROWS + ROWS)
        grad_decays = jnp.zeros((ROWS, 128), F32)
        for pair in range(LOCAL_HEADS // 2):
            first = 128 * pair
            q2, k2, v2 = (qkv_ref[at, SHARD * n + first : SHARD * n + first + 128] for n in range(3))
            g2 = gm[at, first : first + 128]
            zero = jnp.zeros_like(k2)
            keys = jnp.concatenate([jnp.where(left, k2, zero), jnp.where(left, zero, k2)], axis=0)
            values = jnp.concatenate([jnp.where(left, v2, zero), jnp.where(left, zero, v2)], axis=0)
            both = dot(g2, values, ABT)
            grads, low = [], []
            for side in range(2):
                probs = probs_ref[block, 2 * pair + side]
                grad_probs = both[:, ROWS * side : ROWS * side + ROWS]
                inner = jnp.sum(probs * grad_probs, axis=1, keepdims=True)
                grads.append((probs * (grad_probs - inner)).astype(BF16))
                low.append(probs.astype(BF16))
            grads, low = jnp.concatenate(grads, axis=1), jnp.concatenate(low, axis=1)
            pick = lambda v: jnp.where(left, v[:ROWS], v[ROWS:])
            dq = dot(grads, keys, AB) * (HD ** (-0.5))
            dk = pick(dot(grads, q2, ATB)) * (HD ** (-0.5))
            for n, value in enumerate((dq, dk, pick(dot(low, g2, ATB)))):
                dqkvf_ref[at, SHARD * n + first : SHARD * n + first + 128] = value.astype(BF16)
            over_queries = dot(grads, ones, ATB)
            for side in range(2):
                here = lane == 2 * pair + side
                over_keys = dot(grads[:, ROWS * side : ROWS * side + ROWS], here.astype(BF16), AB)
                grad_decays = grad_decays + over_keys
                grad_decays = grad_decays - jnp.where(here, over_queries[ROWS * side : ROWS * side + ROWS], 0.0)
        grad_logs = exact_dot(upper.astype(F32), grad_decays)
        dqkvf_ref[at, 3 * SHARD :] = (grad_logs * jax.nn.sigmoid(-forget_ref[at, :])).astype(BF16)

    for copy in copies:
        copy.wait()
    scaled = []
    for block in range(2):
        x = x_ref[block, :ROWS].astype(F32)
        scaled.append(x * lax.rsqrt(jnp.mean(x * x, axis=1, keepdims=True) + EPSILON))
    for col in range(4):
        lanes = slice(SHARD * col, SHARD * col + SHARD)
        incoming = dot(dqkvf_ref[...], w_ref[lanes, :], ABT)
        low_ref[:, lanes] = incoming.astype(BF16)
        gain_grad_ref[:, lanes] = sum(
            jnp.sum(incoming[ROWS * n : ROWS * n + ROWS] * scaled[n][:, lanes], axis=0, keepdims=True) for n in range(2)
        )


def attention_backward(half, at, x, gab, wo, qkv, forget, probs, pieces):
    vmem, anywhere = pl.BlockSpec(memory_space=pltpu.VMEM), pl.BlockSpec(memory_space=pltpu.HBM)
    return pl.pallas_call(
        functools.partial(backward_kernel, half),
        in_specs=[pl.BlockSpec(memory_space=pltpu.SMEM)] + [vmem] * 3 + [anywhere] * 7,
        out_specs=[vmem] * 3,
        out_shape=[
            jax.ShapeDtypeStruct((2 * ROWS, D), BF16),
            jax.ShapeDtypeStruct((2 * ROWS, WIDTH), BF16),
            jax.ShapeDtypeStruct((1, D), F32),
        ],
        scratch_shapes=[
            pltpu.VMEM((2 * ROWS, 3 * SHARD), BF16),
            pltpu.VMEM((2 * ROWS, 128), F32),
            pltpu.VMEM((2, LOCAL_HEADS, ROWS, ROWS), F32),
            pltpu.VMEM((D, WIDTH), BF16),
            pltpu.SemaphoreType.DMA((7,)),
        ],
        compiler_params=pltpu.CompilerParams(vmem_limit_bytes=24 * 1024 * 1024),
        cost_estimate=GRADIENT_COST,
    )(at, x, gab, wo, qkv, forget, probs, *pieces)


FBLOCK = 256


def ffn_kernel(
    at_ref, first_ref, second_ref, gb_ref, wd_ref, gate_ref, up_ref, sister_ref, z_ref, z_other_ref, y_ref, y_other_ref,
    keep_ref, send_ref, hidden_ref, dg_ref, du_ref, n2_ref, w_ref, sem,
):
    j, bit_z, bit_y = at_ref[2], at_ref[3], at_ref[4]
    lanes = pl.ds(pl.multiple_of(j * FSHARD, FSHARD), FSHARD)

    def rows(r, first, count):
        return pl.ds(pl.multiple_of((r ^ j) * SHARD + first, 192), count)

    half = SHARD // 2
    pieces = (
        (sister_ref, rows(1, 0, SHARD)),
        (z_ref, rows(2, bit_z * half, half)),
        (z_other_ref, rows(2, half - bit_z * half, half)),
        (y_ref, rows(3, bit_y * half, half)),
        (y_other_ref, rows(3, half - bit_y * half, half)),
    )
    own = rows(0, 0, SHARD)
    fill(
        [
            (gate_ref.at[:, lanes], w_ref.at[own, pl.ds(0, FSHARD)], sem.at[0]),
            (up_ref.at[:, lanes], w_ref.at[own, pl.ds(FSHARD, FSHARD)], sem.at[1]),
        ]
        + [(ref, w_ref.at[at], sem.at[2 + n]) for n, (ref, at) in enumerate(pieces)]
    )
    n2_ref[: 2 * ROWS] = first_ref[...]
    n2_ref[2 * ROWS :] = second_ref[...]
    n2, gb = n2_ref[...], gb_ref[...]
    for step in range(FSHARD // FBLOCK):
        cols = slice(step * FBLOCK, step * FBLOCK + FBLOCK)
        gate = dot(n2, w_ref[:, cols], AB)
        up = dot(n2, w_ref[:, FSHARD + step * FBLOCK : FSHARD + step * FBLOCK + FBLOCK], AB)
        grad_hidden = dot(gb, wd_ref[cols, :], ABT)
        sig = jax.nn.sigmoid(gate)
        act = gate * sig
        hidden_ref[:, cols] = (act * up).astype(BF16)
        dg_ref[:, cols] = (grad_hidden * up * sig * (1.0 + gate * (1.0 - sig))).astype(BF16)
        du_ref[:, cols] = (grad_hidden * act).astype(BF16)
    for step in range(4):
        feat = slice(step * SHARD, step * SHARD + SHARD)
        part = dot(dg_ref[...], w_ref[feat, :FSHARD], ABT) + dot(du_ref[...], w_ref[feat, FSHARD:], ABT)
        part = part.astype(BF16)
        keep_ref[:, feat] = part[: 2 * ROWS]
        send_ref[:, feat] = part[2 * ROWS :]


def ffn(at, first, second, gb, wd, w_gate, w_up, pieces):
    vmem = pl.BlockSpec(memory_space=pltpu.VMEM)
    wide = [jax.ShapeDtypeStruct((4 * ROWS, FSHARD), BF16)] * 3
    return pl.pallas_call(
        ffn_kernel,
        in_specs=[pl.BlockSpec(memory_space=pltpu.SMEM)] + [vmem] * 4 + [pl.BlockSpec(memory_space=pltpu.HBM)] * 7,
        out_specs=[vmem] * 6,
        out_shape=[jax.ShapeDtypeStruct((2 * ROWS, D), BF16)] * 2 + wide + [jax.ShapeDtypeStruct((4 * ROWS, D), BF16)],
        scratch_shapes=[pltpu.VMEM((D, 2 * FSHARD), BF16), pltpu.SemaphoreType.DMA((7,))],
        compiler_params=pltpu.CompilerParams(vmem_limit_bytes=32 * 1024 * 1024),
        cost_estimate=COST,
    )(at, first, second, gb, wd, w_gate, w_up, *pieces)


STAGES = ((1, 3), (3, 1))


def labels(j):
    core = j & 1
    return (0, 3 - 2 * core, 1 + 2 * core, 2)


def piece_of(part, index, label):
    a, b = label[index // 4], label[index % 4]
    return (b, a) if part == 0 else (a, b)


def place(outs, part, index):
    return outs[2 * part + index // 8], index % 8


FUNITS = 72
QUNITS = ((0, 8), (8, 15))
OUNITS = ((0, 8), (8, 18))
AUNITS = tuple(4 * (q1 - q0) + (o1 - o0) for (q0, q1), (o0, o1) in zip(QUNITS, OUNITS))
NQ, NO = 240, 288


def ffn_grad_kernel(part, at_ref, n2_ref, gb_ref, hidden_ref, grad_ref, keep_ref, send_ref, cols_ref, down_ref):
    y, z, j = at_ref[0], at_ref[1], at_ref[2]
    label = labels(j)
    n2 = n2_ref[...]
    for step in range(4):
        pz = label[step] ^ z
        lanes = pl.ds(pl.multiple_of(pz * FBLOCK, FBLOCK), FBLOCK)
        cols_ref[...] = dot(n2, grad_ref[:, lanes], ATB).astype(BF16).reshape(16, 96, FBLOCK)
        gb = gb_ref[:, 768 * part : 768 * part + 768]
        down_ref[...] = dot(hidden_ref[:, lanes], gb, ATB).astype(BF16).reshape(4, 64, 768)
        for other in range(4):
            py = label[other] ^ y
            index = 4 * step + other if part == 0 else 4 * other + step
            out, slot = (keep_ref, send_ref)[index // 8], index % 8
            for r in range(4):
                for half in range(2):
                    block = cols_ref[(r ^ j) * 4 + py, :, 128 * half : 128 * half + 128]
                    out[slot, 12 * r + 6 * half : 12 * r + 6 * half + 6] = block.reshape(6, 16, 128)
            for t in range(6):
                block = down_ref[py, :, 128 * t : 128 * t + 128]
                out[slot, 48 + 4 * t : 52 + 4 * t] = block.reshape(4, 16, 128)


def ffn_gradients(part, at, n2, gb, hidden, grad):
    vmem = pl.BlockSpec(memory_space=pltpu.VMEM)
    return pl.pallas_call(
        functools.partial(ffn_grad_kernel, part),
        in_specs=[pl.BlockSpec(memory_space=pltpu.SMEM)] + [vmem] * 4,
        out_specs=[vmem] * 2,
        out_shape=[jax.ShapeDtypeStruct((8, FUNITS, 16, 128), BF16)] * 2,
        scratch_shapes=[pltpu.VMEM((16, 96, FBLOCK), BF16), pltpu.VMEM((4, 64, 768), BF16)],
        compiler_params=pltpu.CompilerParams(vmem_limit_bytes=20 * 1024 * 1024),
        cost_estimate=GRADIENT_COST,
    )(at, n2, gb, hidden, grad)


def ffn_unpack_kernel(at_ref, *refs):
    ins, (gate_ref, up_ref, down_ref) = refs[:4], refs[4:]
    y, z, j = at_ref[0], at_ref[1], at_ref[2]
    label = labels(j)
    for part in range(2):
        target = (gate_ref, up_ref)[part]
        for index in range(16):
            ry, rz = piece_of(part, index, label)
            source, slot = place(ins, part, index)
            py, pz = ry ^ y, rz ^ z
            rows = pl.ds(pl.multiple_of(py * 96, 32), 96)
            for r in range(4):
                for half in range(2):
                    left = (r ^ j) * FSHARD + pz * FBLOCK + half * 128
                    block = source[slot, 12 * r + 6 * half : 12 * r + 6 * half + 6].reshape(96, 128)
                    target[rows, pl.ds(pl.multiple_of(left, 128), 128)] = block.astype(F32)
            rows = pl.ds(pl.multiple_of(pz * 256 + py * 64, 64), 64)
            for t in range(6):
                left = 768 * part + 128 * t
                block = source[slot, 48 + 4 * t : 52 + 4 * t].reshape(64, 128)
                down_ref[rows, left : left + 128] = block.astype(F32)


def ffn_unpack(at, pieces):
    vmem = pl.BlockSpec(memory_space=pltpu.VMEM)
    return pl.pallas_call(
        ffn_unpack_kernel,
        in_specs=[pl.BlockSpec(memory_space=pltpu.SMEM)] + [vmem] * 4,
        out_specs=[vmem] * 3,
        out_shape=[
            jax.ShapeDtypeStruct((SHARD, FF), F32),
            jax.ShapeDtypeStruct((SHARD, FF), F32),
            jax.ShapeDtypeStruct((FSHARD, D), F32),
        ],
        compiler_params=pltpu.CompilerParams(vmem_limit_bytes=30 * 1024 * 1024),
        cost_estimate=GRADIENT_COST,
    )(at, *pieces)


def attention_grad_kernel(at_ref, normed_ref, d1_ref, d2_ref, mixed_ref, g1_ref, g2_ref, gains_ref, *rest):
    outs, (q_ref, o_ref) = rest[:4], rest[4:]
    y, z, j = at_ref[0], at_ref[1], at_ref[2]
    label = labels(j)
    d1, d2 = d1_ref[...], d2_ref[...]
    upper, lower = pl.ds(0, 2 * ROWS), pl.ds(2 * ROWS, 2 * ROWS)
    row = lax.broadcasted_iota(jnp.int32, (16, 128), 0)
    lane = lax.broadcasted_iota(jnp.int32, (16, 128), 1)
    pick = (lane == row + LOCAL_HEADS).astype(BF16)
    pick = jnp.where(row < 2, pick, jnp.zeros_like(pick))
    bias = sum(jnp.sum(d[:, 3 * SHARD :].astype(F32), axis=0, keepdims=True) for d in (d1, d2))
    bias = pltpu.roll(bias, 8, 1)

    def units(source, width, per, p, t):
        odd = (p & 1) == 1
        group = (p >> 1) * 3 + jnp.where(odd, (per + t) // width, t // width)
        return source[group, jnp.where(odd, (per + t) % width, t % width)]

    def piece(part, index):
        ry, rz = piece_of(part, index, label)
        return (ry ^ y) * 4 + (rz ^ z)

    for r in range(4):
        lanes = pl.ds(pl.multiple_of((r ^ j) * SHARD, SHARD), SHARD)
        grad = dot(normed_ref[upper, lanes], d1, ATB) + dot(normed_ref[lower, lanes], d2, ATB)
        extra = grad[:, 3 * SHARD :] + dot(gains_ref[:, lanes], pick, ATB) + bias
        for col in range(9):
            block = grad[:, 128 * col : 128 * col + 128].astype(BF16).reshape(24, 1, 16, 128)
            q_ref[:, col : col + 1] = block
        q_ref[:, 9:10] = extra.astype(BF16).reshape(24, 1, 16, 128)
        for part in range(2):
            lo, hi = QUNITS[part]
            for index in range(16):
                out, slot = place(outs, part, index)
                for t in range(lo, hi):
                    out[slot, (hi - lo) * r + t - lo] = units(q_ref, 10, 15, piece(part, index), t)
    grad = dot(mixed_ref[upper, :], g1_ref[...], ATB) + dot(mixed_ref[lower, :], g2_ref[...], ATB)
    for col in range(12):
        o_ref[:, col : col + 1] = grad[:, 128 * col : 128 * col + 128].astype(BF16).reshape(24, 1, 16, 128)
    for part in range(2):
        lo, hi = OUNITS[part]
        first = AUNITS[part] - (hi - lo)
        for index in range(16):
            out, slot = place(outs, part, index)
            for t in range(lo, hi):
                out[slot, first + t - lo] = units(o_ref, 12, 18, piece(part, index), t)


def attention_gradients(at, normed, d1, d2, mixed, g1, g2, gains):
    vmem = pl.BlockSpec(memory_space=pltpu.VMEM)
    return pl.pallas_call(
        attention_grad_kernel,
        in_specs=[pl.BlockSpec(memory_space=pltpu.SMEM)] + [vmem] * 7,
        out_specs=[vmem] * 4,
        out_shape=[jax.ShapeDtypeStruct((8, AUNITS[i // 2], 16, 128), BF16) for i in range(4)],
        scratch_shapes=[
            pltpu.VMEM((24, 10, 16, 128), BF16),
            pltpu.VMEM((24, 12, 16, 128), BF16),
        ],
        compiler_params=pltpu.CompilerParams(vmem_limit_bytes=26 * 1024 * 1024),
        cost_estimate=GRADIENT_COST,
    )(at, normed, d1, d2, mixed, g1, g2, gains)


def attention_unpack_kernel(at_ref, *refs):
    ins, (gq_ref, gk_ref, gv_ref, go_ref, forget_ref, small_ref, q_ref, o_ref) = refs[:4], refs[4:]
    y, z, j = at_ref[0], at_ref[1], at_ref[2]
    label = labels(j)
    for part in range(2):
        qlo, qhi = QUNITS[part]
        olo, ohi = OUNITS[part]
        n = qhi - qlo
        for index in range(16):
            ry, rz = piece_of(part, index, label)
            source, slot = place(ins, part, index)
            p = (ry ^ y) * 4 + (rz ^ z)
            for r in range(4):
                q_ref[r ^ j, pl.ds(p * 15 + qlo, n)] = source[slot, n * r : n * r + n]
            o_ref[pl.ds(p * 18 + olo, ohi - olo)] = source[slot, 4 * n : 4 * n + ohi - olo]
    for group in range(24):
        rows = slice(16 * group, 16 * group + 16)
        for device in range(4):
            for col in range(10):
                if col < 9:
                    target = (gq_ref, gk_ref, gv_ref)[col // 3]
                    left = SHARD * device + 128 * (col % 3)
                    target[rows, left : left + 128] = q_ref[device, 10 * group + col].astype(F32)
        for col in range(12):
            go_ref[rows, 128 * col : 128 * col + 128] = o_ref[12 * group + col].astype(F32)
    lane = lax.broadcasted_iota(jnp.int32, (128, 128), 1)
    for third in range(3):
        forget = jnp.zeros((128, 128), F32)
        total = jnp.zeros((128, 128), F32)
        for device in range(4):
            parts = [q_ref[device, 10 * group + 9] for group in range(8 * third, 8 * third + 8)]
            extra = jnp.concatenate(parts, axis=0).astype(F32)
            mine = (lane >= LOCAL_HEADS * device) & (lane < LOCAL_HEADS * device + LOCAL_HEADS)
            moved = pltpu.roll(extra, LOCAL_HEADS * device, 1) if device else extra
            forget = jnp.where(mine, moved, forget)
            total = total + extra
        forget_ref[:, 128 * third : 128 * third + 128] = forget.T[:H]
        small_ref[:, 128 * third : 128 * third + 128] = total.T[:16]
    first = q_ref[j, pl.ds(9, 1)].astype(F32)
    small_ref[8:16, 0:128] = first.reshape(16, 128)[:8]


def attention_unpack(at, pieces):
    vmem = pl.BlockSpec(memory_space=pltpu.VMEM)
    return pl.pallas_call(
        attention_unpack_kernel,
        in_specs=[pl.BlockSpec(memory_space=pltpu.SMEM)] + [vmem] * 4,
        out_specs=[vmem] * 6,
        out_shape=[jax.ShapeDtypeStruct((SHARD, D), F32)] * 4
        + [jax.ShapeDtypeStruct((H, SHARD), F32), jax.ShapeDtypeStruct((16, SHARD), F32)],
        scratch_shapes=[
            pltpu.VMEM((4, NQ, 16, 128), BF16),
            pltpu.VMEM((NO, 16, 128), BF16),
        ],
        compiler_params=pltpu.CompilerParams(vmem_limit_bytes=24 * 1024 * 1024),
        cost_estimate=COST,
    )(at, *pieces)


def small_call(kernel, out, *args):
    vmem = pl.BlockSpec(memory_space=pltpu.VMEM)
    return pl.pallas_call(
        kernel,
        in_specs=[vmem] * len(args),
        out_specs=[vmem] * len(out),
        out_shape=[jax.ShapeDtypeStruct((n, 16, 128), BF16) for n in out],
        compiler_params=pltpu.CompilerParams(vmem_limit_bytes=8 * 1024 * 1024),
        cost_estimate=COST,
    )(*args)


def add_slots(held, first, count):
    n = held[0].shape[1]

    def kernel(*refs):
        refs[-1][...] = functools.reduce(lambda a, b: a + b, [ref[...].astype(F32) for ref in refs[:-1]]).astype(BF16)

    return pl.pallas_call(
        kernel,
        grid=(1,),
        in_specs=[pl.BlockSpec((count, n, 16, 128), lambda i: (first // count, 0, 0, 0))] * len(held),
        out_specs=pl.BlockSpec((count, n, 16, 128), lambda i: (0, 0, 0, 0)),
        out_shape=jax.ShapeDtypeStruct((count, n, 16, 128), BF16),
        compiler_params=pltpu.CompilerParams(vmem_limit_bytes=20 * 1024 * 1024),
        cost_estimate=COST,
    )(*held)


def join(upper, lower):
    slots, n = upper.shape[:2]

    def kernel(upper_ref, lower_ref, out_ref):
        out_ref[:slots] = upper_ref[...]
        out_ref[slots:] = lower_ref[...]

    vmem = pl.BlockSpec(memory_space=pltpu.VMEM)
    return pl.pallas_call(
        kernel,
        in_specs=[vmem] * 2,
        out_specs=vmem,
        out_shape=jax.ShapeDtypeStruct((2 * slots, n, 16, 128), BF16),
        compiler_params=pltpu.CompilerParams(vmem_limit_bytes=8 * 1024 * 1024),
        cost_estimate=COST,
    )(upper, lower)


def row_call(kernel, out, *args):
    vmem = pl.BlockSpec(memory_space=pltpu.VMEM)
    return pl.pallas_call(
        kernel,
        in_specs=[vmem] * len(args),
        out_specs=[vmem] * len(out),
        out_shape=[jax.ShapeDtypeStruct(*v) for v in out],
        compiler_params=pltpu.CompilerParams(vmem_limit_bytes=20 * 1024 * 1024),
        cost_estimate=COST,
    )(*args)


HALF = (2 * ROWS, D)


def add_rows(former, latter):
    def kernel(former_ref, latter_ref, out_ref):
        out_ref[...] = (former_ref[...].astype(F32) + latter_ref[...].astype(F32)).astype(BF16)

    return row_call(kernel, [(former.shape, BF16)], former, latter)[0]


def both_chips(chip_ref, other_ref, block):
    here = slice(ROWS * block, ROWS * block + ROWS)
    there = slice(ROWS * (1 - block), ROWS * (1 - block) + ROWS)
    return chip_ref[here].astype(F32) + other_ref[there].astype(F32)


def middle_rows(rows, chip, other, gain):
    def kernel(x_ref, chip_ref, other_ref, gain_ref, middle_ref, normed_ref):
        for block in range(2):
            here = slice(ROWS * block, ROWS * block + ROWS)
            middle = x_ref[block, :ROWS].astype(F32) + both_chips(chip_ref, other_ref, block)
            factor = lax.rsqrt(jnp.mean(middle * middle, axis=1, keepdims=True) + EPSILON)
            middle_ref[here] = middle
            normed_ref[here] = (middle * factor * gain_ref[...]).astype(BF16)

    return row_call(kernel, [(HALF, F32), (HALF, BF16)], rows, chip, other, gain)


def middle_gradient(chip, other, middle, branch, gain):
    def kernel(chip_ref, other_ref, middle_ref, branch_ref, gain_ref, grad_ref, low_ref, part_ref):
        total = jnp.zeros((1, D), F32)
        for block in range(2):
            here = slice(ROWS * block, ROWS * block + ROWS)
            incoming = both_chips(chip_ref, other_ref, block)
            middle = middle_ref[here]
            factor = lax.rsqrt(jnp.mean(middle * middle, axis=1, keepdims=True) + EPSILON)
            scaled = incoming * gain_ref[...]
            inner = jnp.mean(scaled * middle, axis=1, keepdims=True)
            grad = branch_ref[here].astype(F32) + (scaled * factor - middle * (factor * factor * factor) * inner)
            grad_ref[here] = grad
            low_ref[here] = grad.astype(BF16)
            total = total + jnp.sum(incoming * middle * factor, axis=0, keepdims=True)
        part_ref[...] = total

    out = [(HALF, F32), (HALF, BF16), ((1, D), F32)]
    return row_call(kernel, out, chip, other, middle, branch, gain)


def for_sister(pieces, columns):
    def kernel(first_ref, second_ref, out_ref):
        at = 0
        for r in (1, 3):
            for ref, n in zip((first_ref, second_ref), columns):
                out_ref[at : at + n] = ref[r * n : r * n + n]
                at += n

    return small_call(kernel, [2 * sum(columns)], *pieces)[0]


def for_chips(pieces, sister, columns):
    n = sum(columns)
    tails = [p.shape[0] - 4 * m for p, m in zip(pieces, columns)]

    def kernel(first_ref, second_ref, sister_ref, near_ref, far_ref):
        at, tail = 0, 2 * n
        for ref, m, last in zip((first_ref, second_ref), columns, tails):
            near_ref[at : at + m] = ref[0:m]
            far_ref[at : at + m] = ref[2 * m : 3 * m]
            near_ref[tail : tail + last] = ref[4 * m : 4 * m + last]
            at, tail = at + m, tail + last
        near_ref[n : 2 * n] = sister_ref[0:n]
        far_ref[n : 2 * n] = sister_ref[n : 2 * n]

    return small_call(kernel, [2 * n + sum(tails), 2 * n], *pieces, sister)


def join_chips(near, far, a, b, t, columns):
    n = sum(columns)
    last = near.shape[0] - 2 * n
    tails = [last // 2, last // 2] if columns[0] == columns[1] else [hi - lo for lo, hi in OUNITS]

    def kernel(near_ref, far_ref, a_ref, b_ref, t_ref, first_ref, second_ref):
        def total(x_ref, y_ref, lo, m):
            return (x_ref[lo : lo + m].astype(F32) + y_ref[lo : lo + m].astype(F32)).astype(BF16)

        at, tail = 0, 2 * n
        for ref, m, end in zip((first_ref, second_ref), columns, tails):
            ref[0:m] = total(near_ref, t_ref, at, m)
            ref[m : 2 * m] = total(near_ref, t_ref, n + at, m)
            ref[2 * m : 3 * m] = total(a_ref, b_ref, at, m)
            ref[3 * m : 4 * m] = total(a_ref, b_ref, n + at, m)
            ref[4 * m : 4 * m + end] = total(near_ref, t_ref, tail, end)
            at, tail = at + m, tail + end

    return small_call(kernel, [4 * m + end for m, end in zip(columns, tails)], near, far, a, b, t)


def make_body(sizes):
    ny, nxh, nz = sizes

    def send(value, move):
        pairs = []
        for y in range(ny):
            for x in range(2 * nxh):
                for z in range(nz):
                    for c in range(2):
                        ty, tx, tz, tc = move(y, x, z, c)
                        tx %= 2 * nxh
                        src = (((y * nxh + x // 2) * nz + z) * 2 + x % 2) * 2 + c
                        dst = (((ty * nxh + tx // 2) * nz + tz) * 2 + tx % 2) * 2 + tc
                        pairs.append((src, dst))
        return lax.ppermute(value, AXES, pairs)

    def swap_plane(value, axis, stage):
        if axis == "y":
            return send(value, lambda y, x, z, c: (y ^ STAGES[c][stage], x, z, c))
        return send(value, lambda y, x, z, c: (y, x, z ^ STAGES[c][stage], c))

    def after(value, *others):
        return lax.optimization_barrier((value, *others))[0]

    swap_core = lambda v: send(v, lambda y, x, z, c: (y, x, z, 1 - c))
    swap_x = lambda v: send(v, lambda y, x, z, c: (y, x ^ 1, z, c))
    swap_out = lambda v: send(v, lambda y, x, z, c: (y, x ^ 3, z, c))
    cross_mixed = lambda v: send(v, lambda y, x, z, c: (y, x ^ (1 if c else 3), z, 1 - c))
    cross_x = lambda v: send(v, lambda y, x, z, c: (y, x ^ 1, z, 1 - c))
    x_plus = lambda v: send(v, lambda y, x, z, c: (y, x + 1, z, c))
    x_minus = lambda v: send(v, lambda y, x, z, c: (y, x - 1, z, c))
    x_two = lambda v: send(v, lambda y, x, z, c: (y, x + 2, z, c))

    def total(parts):
        return functools.reduce(lambda a, b: a + b, [p.astype(F32) for p in parts])

    def combine(keep, received):
        return total([keep, received]).astype(BF16)

    class Order:
        def __init__(self):
            self.work = ()

        def arrive(self, *values):
            out = lax.optimization_barrier((*values, *self.work))[: len(values)]
            return out if len(values) > 1 else out[0]

        def then(self, *work):
            self.work = work

    def move(part, step):
        return ("zy"[part != step // 2], step % 2)

    class Lane:
        def __init__(self, order, part, keep, sending):
            self.order, self.part, self.held, self.sending, self.step = order, part, [keep], sending, 0

        def start(self):
            self.got = swap_plane(self.sending, *move(self.part, self.step))

        def arrive(self):
            self.held.append(self.order.arrive(self.got))
            half = 4 >> self.step
            self.sending = add_slots(self.held, half, max(half, 1))
            self.order.then(self.sending)
            self.step += 1

        def gather(self, piece):
            self.sending, self.step = piece[None], 3

        def collect(self):
            self.got = self.order.arrive(self.got)
            if self.step:
                self.sending = join(self.sending, self.got)
                self.order.then(self.sending)
            self.step -= 1

    def together(order, lanes):
        for lane, got in zip(lanes, order.arrive(*[lane.got for lane in lanes])):
            lane.got = got

    def both(lanes, *names):
        for name in names:
            for lane in lanes:
                getattr(lane, name)()

    def each(lanes, *names):
        for lane in lanes:
            for name in names:
                getattr(lane, name)()

    def spread_steps(order, pieces, columns):
        sister = swap_core(for_sister(pieces, columns))
        yield
        sister = order.arrive(sister)
        near, far = for_chips(pieces, sister, columns)
        order.then(far, near)
        a, b, t = x_plus(far), x_minus(far), x_two(near)
        yield
        a, b, t = order.arrive(a, b, t)
        out = join_chips(near, far, a, b, t, columns)
        order.then(*out)
        return out

    def finish(steps):
        try:
            next(steps)
        except StopIteration as stop:
            return stop.value

    def body(
        tokens, lengths, w_query, w_key, w_value, w_out, w_forget, forget_bias, norm_attn,
        w_gate, w_up, w_down, norm_ffn, cotangent,
    ):
        y, z, core = lax.axis_index("y"), lax.axis_index("z"), lax.axis_index("c")
        j = lax.axis_index("xl") * 2 + core
        bits = [(jnp.where(n == 0, z & 1, z >> 1), jnp.where(n == 0, y & 1, y >> 1)) for n in (core, 1 - core)]
        (bit_z, bit_y), (_, sister_bit_y) = bits
        at = jnp.stack([y, z, j, bit_z, bit_y, sister_bit_y]).astype(jnp.int32)

        own_cols, far_cols, sister_cols, cross_cols = columns(at, w_query, w_key, w_value, w_forget.T)
        far, cross, sister = swap_out(far_cols), cross_mixed(cross_cols), swap_core(sister_cols)
        cot_first = swap_x(after(cotangent, far_cols))

        small = jnp.concatenate([norm_attn, norm_ffn, lengths[0].astype(BF16)])
        small = after(small, far_cols)
        small = jnp.pad(small[None], ((0, 15), (0, D - small.shape[0])))
        packed = jnp.concatenate([tokens, small], axis=0)
        packed_first = swap_x(packed)

        sister_gu, cross_gu, far_gu = gate_up_columns(after(at, far_cols, packed), w_gate, w_up)

        order = Order()
        order.then(far_gu)
        packed_first = order.arrive(packed_first)
        pair = jnp.stack([packed, packed_first])
        order.then(pair)
        packed_second = swap_core(pair)
        sister, cross, cot_first = order.arrive(sister, cross, cot_first)
        order.then(sister, cross)
        fetch_y = cross_x(after(cross_gu, cross))
        far = order.arrive(far)
        order.then(sister, cross, far)
        fetch_z = swap_out(after(far_gu, far))
        sister_gu = swap_core(after(sister_gu, sister))
        packed_all = jnp.concatenate([pair, order.arrive(packed_second)], axis=0)
        x_rows = packed_all[:, :ROWS].reshape(4 * ROWS, D)
        small_all = packed_all[:, ROWS]
        lens = small_all[:, 2 * SHARD : 2 * SHARD + SLOTS].astype(jnp.int32)
        by_device = jnp.stack([small_all[0], small_all[2], small_all[1], small_all[3]])
        by_device = jnp.concatenate(
            [lax.dynamic_index_in_dim(by_device, j ^ r, 0, keepdims=True) for r in range(4)], axis=0
        ).astype(F32)
        gain_one = by_device[:, :SHARD].reshape(1, D)
        gain_two = by_device[:, SHARD : 2 * SHARD].reshape(1, D)
        bias = jnp.pad(forget_bias.astype(F32), (0, 128 - LOCAL_HEADS))[None]

        keep, sent, normed, qkv, forget, probs, mixed = attention_forward(
            at, pair, packed_second, bias, w_out, (own_cols, sister, far, cross)
        )
        live = (jnp.arange(ROWS)[None, :] < jnp.sum(lens, axis=1, keepdims=True)).reshape(4 * ROWS, 1)
        cot_pair = jnp.stack([cotangent, after(cot_first, sent)])
        first, fetch_z, fetch_y, sister_gu, cot_pair, live, gain_two = lax.optimization_barrier(
            (swap_core(sent), fetch_z, fetch_y, sister_gu, cot_pair, live, gain_two)
        )
        chip = add_rows(keep, first)
        other = swap_x(chip)
        other_z, other_y = swap_plane(fetch_z, "z", 0), swap_plane(fetch_y, "y", 0)
        cot_rows = jnp.concatenate([cot_pair, swap_core(cot_pair)], axis=0).reshape(4 * ROWS, D)
        grad_branch = jnp.where(live, cot_rows, jnp.zeros_like(cot_rows))
        other, other_z, other_y, grad_branch = lax.optimization_barrier((other, other_z, other_y, grad_branch))

        middle, n2_half = middle_rows(pair, chip, other, gain_two)
        n2_other = swap_core(n2_half)

        keep, sent, hidden, dgate, dup, n2 = ffn(
            at, n2_half, n2_other, grad_branch, w_down, w_gate, w_up, (sister_gu, fetch_z, other_z, fetch_y, other_y)
        )
        order = Order()
        first = swap_core(sent)
        ffn_parts = ffn_gradients(0, at, n2, grad_branch, hidden, dgate)
        order.then(ffn_parts[0])
        chip = add_rows(keep, order.arrive(first))
        ffn_parts = ffn_parts + ffn_gradients(1, at, after(n2, chip), grad_branch, hidden, dup)
        order.then(ffn_parts[2])
        ffn_lanes = [Lane(order, k, *ffn_parts[2 * k : 2 * k + 2]) for k in range(2)]
        both(ffn_lanes, "start")
        other = swap_x(chip)
        down = dot(after(hidden, ffn_parts[2]), w_down, AB).astype(BF16)
        order.then(down)
        grad_middle, gab_half, gain_two_part = middle_gradient(
            chip, order.arrive(other), middle, grad_branch, gain_two
        )
        order.then(gab_half)
        gab_other = swap_core(gab_half)
        down_first = swap_core(down[2 * ROWS :])

        kept = (w_out, qkv, forget, probs, (own_cols, sister, far, cross))
        keep, d1, gain_first = attention_backward(0, at, pair, gab_half, *kept)
        order.then(d1)
        each(ffn_lanes, "arrive", "start")
        gab_other = order.arrive(gab_other)
        sent, d2, gain_second = attention_backward(1, at, packed_second, gab_other, *kept)
        order.then(d2)
        token_first = swap_core(sent)
        each(ffn_lanes[:1], "arrive", "start")
        gains = jnp.concatenate([gain_first + gain_second, 0.5 * gain_two_part], axis=0).astype(BF16)
        gains = jnp.pad(gains, ((0, 14), (0, 0)))
        attn_parts = attention_gradients(at, normed, d1, order.arrive(d2), mixed, gab_half, gab_other, gains)
        order.then(attn_parts[0])
        each(ffn_lanes[1:], "arrive", "start")
        down_chip, token_chip = combine(down[: 2 * ROWS], down_first), add_rows(keep, order.arrive(token_first))
        order.then(down_chip, token_chip)
        down_other, token_other = swap_x(down_chip[ROWS:]), swap_x(token_chip[ROWS:])
        each(ffn_lanes, "arrive", "start")
        each(ffn_lanes, "arrive")
        attn_parts = after(attn_parts, ffn_lanes[1].sending)
        attn_lanes = [Lane(order, k, *attn_parts[2 * k : 2 * k + 2]) for k in range(2)]
        both(attn_lanes, "start")
        ffn_spread = spread_steps(order, [lane.sending[0] for lane in ffn_lanes], [12, 12])
        next(ffn_spread)
        next(ffn_spread)
        each(attn_lanes, "arrive", "start")
        ffn_pieces = finish(ffn_spread)
        for lane, piece in zip(ffn_lanes, ffn_pieces):
            lane.gather(piece)
        both(ffn_lanes, "start")

        def next_step(lanes, name):
            together(order, lanes)
            each(lanes, name, "start")

        next_step(ffn_lanes, "collect")
        next_step(attn_lanes, "arrive")
        next_step(ffn_lanes, "collect")
        next_step(attn_lanes, "arrive")
        together(order, attn_lanes)
        each(attn_lanes, "arrive")
        attn_spread = spread_steps(
            order, [lane.sending[0] for lane in attn_lanes], [hi - lo for lo, hi in QUNITS]
        )
        next(attn_spread)
        next_step(ffn_lanes, "collect")
        next(attn_spread)
        attn_pieces = finish(attn_spread)
        for lane, piece in zip(attn_lanes, attn_pieces):
            lane.gather(piece)
        both(attn_lanes, "start")
        next_step(attn_lanes, "collect")
        next_step(attn_lanes, "collect")
        down_other, token_other = order.arrive(down_other, token_other)
        together(order, ffn_lanes)
        each(ffn_lanes, "collect")
        order.then(*[lane.got for lane in ffn_lanes])
        next_step(attn_lanes, "collect")
        ffn_last = after([v for lane in ffn_lanes for v in (lane.sending, lane.got)], attn_lanes[1].sending)
        grad_gate, grad_up, grad_down = ffn_unpack(at, ffn_last)
        order.then(grad_down)
        each(attn_lanes, "collect")
        branch = down_chip[:ROWS].astype(F32) + down_other.astype(F32)
        output = jnp.where(live[:ROWS], middle[:ROWS] + branch, 0.0).astype(BF16)

        own = x_rows[:ROWS].astype(F32)
        factor_one = lax.rsqrt(jnp.mean(own * own, axis=1, keepdims=True) + EPSILON)
        scaled = (token_chip[:ROWS].astype(F32) + token_other.astype(F32)) * gain_one
        inner = jnp.mean(scaled * own, axis=1, keepdims=True)
        grad_tokens = grad_middle[:ROWS] + (
            scaled * factor_one - own * (factor_one * factor_one * factor_one) * inner
        )

        grad_query, grad_key, grad_value, grad_out, grad_forget, small = attention_unpack(
            at, [v for lane in attn_lanes for v in (lane.sending, lane.got)]
        )
        grad_forget = grad_forget.T
        grad_norm_attn, grad_norm_ffn = small[LOCAL_HEADS], small[LOCAL_HEADS + 1]
        grad_bias = small[8, 8 : 8 + LOCAL_HEADS]
        return (
            output, grad_tokens, grad_query, grad_key, grad_value, grad_out, grad_forget, grad_bias,
            grad_norm_attn, grad_gate, grad_up, grad_down, grad_norm_ffn,
        )

    return body


SIZES = {32: (4, 2, 4), 16: (4, 1, 4)}


def solution(mesh):
    sizes = SIZES[mesh.shape["wide"]]
    ny, nxh, nz = sizes
    fine = Mesh(mesh.devices.reshape(ny, nxh, nz, 2, 2), AXES)
    rows, shard, vector = P(AXES, None), P(("xl", "c"), None), P(("xl", "c"))
    return jax.shard_map(
        make_body(sizes),
        mesh=fine,
        in_specs=(
            rows, rows, shard, shard, shard, shard, shard, vector, vector, shard, shard, shard, vector, rows,
        ),
        out_specs=(
            rows, rows, shard, shard, shard, shard, shard, vector, vector, shard, shard, shard, vector,
        ),
        check_vma=False,
    )
```

```python
import functools

import jax
import jax.numpy as jnp
from jax import lax
from jax.experimental import pallas as pl
from jax.experimental.pallas import tpu as pltpu
from jax.sharding import Mesh, PartitionSpec as P

D = 1536
H = 24
HD = 64
FF = 4096
ROWS = 128
SLOTS = 4
EPSILON = 1e-06
SHARD = D // 4
FSHARD = FF // 4
LOCAL_HEADS = H // 4
WIDTH = 3 * SHARD + 128
AXES = ("y", "xh", "z", "xl", "c")
PLANE = ("y", "z")
F32 = jnp.float32
BF16 = jnp.bfloat16


def dot(former, latter, dims):
    return lax.dot_general(former, latter, (dims, ((), ())), preferred_element_type=F32)


COST = pl.CostEstimate(flops=0, bytes_accessed=0, transcendentals=0)
GRADIENT_COST = pl.CostEstimate(flops=4 * 10**9, bytes_accessed=12 * 10**6, transcendentals=0)

AB = ((1,), (0,))
ABT = ((1,), (1,))
ATB = ((0,), (0,))


def exact_dot(former, latter):
    return lax.dot_general(
        former, latter, ((AB), ((), ())), precision=lax.Precision.HIGHEST, preferred_element_type=F32
    )


def attend_mask(lens):
    rows = lax.broadcasted_iota(jnp.int32, (ROWS, ROWS), 0).astype(F32)
    cols = lax.broadcasted_iota(jnp.int32, (ROWS, ROWS), 1).astype(F32)
    seg_rows = jnp.zeros((ROWS, ROWS), F32)
    seg_cols = jnp.zeros((ROWS, ROWS), F32)
    end = jnp.zeros((1, 1), F32)
    for slot in range(SLOTS):
        end = end + lens[:, slot : slot + 1]
        seg_rows = seg_rows + (rows >= end).astype(F32)
        seg_cols = seg_cols + (cols >= end).astype(F32)
    return (rows >= cols) & (seg_rows == seg_cols)


def fill(copies):
    copies = [pltpu.make_async_copy(*c) for c in copies]
    for c in copies:
        c.start()
    for c in copies:
        c.wait()


def columns_kernel(at_ref, f_ref, q_ref, k_ref, v_ref, own_ref, far_ref, sister_ref, cross_ref, held_ref, sem):
    j = at_ref[2]
    targets = (2, 3, 1, 0)
    ins = []
    for n, r in enumerate(targets):
        lanes = pl.ds(pl.multiple_of((r ^ j) * SHARD, SHARD), SHARD)
        for m, source in enumerate((q_ref, k_ref, v_ref)):
            target = held_ref.at[n, :, pl.ds(SHARD * m, SHARD)]
            ins.append(pltpu.make_async_copy(source.at[:, lanes], target, sem.at[3 * n + m]))
            ins[-1].start()
    forget = jnp.concatenate([f_ref[...].astype(F32), jnp.zeros((128 - H, SHARD), F32)], axis=0).T
    lane = lax.broadcasted_iota(jnp.int32, (SHARD, 128), 1)
    for n, r in enumerate(targets):
        mine = pltpu.roll(forget, lax.rem(128 - LOCAL_HEADS * (r ^ j), 128), 1)
        held_ref[n, :, 3 * SHARD :] = jnp.where(lane < LOCAL_HEADS, mine, 0.0).astype(BF16)
    for copy in ins:
        copy.wait()
    fill(
        [
            (held_ref.at[0], far_ref, sem.at[12]),
            (held_ref.at[1], cross_ref, sem.at[13]),
            (held_ref.at[2], sister_ref, sem.at[14]),
            (held_ref.at[3], own_ref, sem.at[15]),
        ]
    )


def columns(at, w_query, w_key, w_value, w_forget):
    anywhere = pl.BlockSpec(memory_space=pl.ANY)
    return pl.pallas_call(
        columns_kernel,
        in_specs=[pl.BlockSpec(memory_space=pltpu.SMEM), pl.BlockSpec(memory_space=pltpu.VMEM)] + [anywhere] * 3,
        out_specs=[anywhere] * 4,
        out_shape=[jax.ShapeDtypeStruct((SHARD, WIDTH), BF16)] * 4,
        scratch_shapes=[pltpu.VMEM((4, SHARD, WIDTH), BF16), pltpu.SemaphoreType.DMA((16,))],
        compiler_params=pltpu.CompilerParams(vmem_limit_bytes=60 * 1024 * 1024),
        cost_estimate=COST,
    )(at, w_forget, w_query, w_key, w_value)


def gate_up_columns_kernel(at_ref, gate_ref, up_ref, sister_ref, cross_ref, far_ref, held_ref, sem):
    j, bit_z, sister_bit_y = at_ref[2], at_ref[3], at_ref[5]
    half = SHARD // 2
    some = lambda bit: pl.ds(pl.multiple_of(bit * half, half), half)
    targets = ((1, sister_ref, pl.ds(0, SHARD)), (3, cross_ref, some(sister_bit_y)), (2, far_ref, some(bit_z)))
    ins, outs, first = [], [], 0
    for n, (r, ref, rows) in enumerate(targets):
        lanes = pl.ds(pl.multiple_of((r ^ j) * FSHARD, FSHARD), FSHARD)
        held = held_ref.at[pl.ds(first, ref.shape[0])]
        for m, source in enumerate((gate_ref, up_ref)):
            ins.append((source.at[rows, lanes], held.at[:, pl.ds(FSHARD * m, FSHARD)], sem.at[2 * n + m]))
        outs.append((held, ref, sem.at[6 + n]))
        first += ref.shape[0]
    fill(ins)
    fill(outs)


def gate_up_columns(at, w_gate, w_up):
    anywhere = pl.BlockSpec(memory_space=pl.ANY)
    return pl.pallas_call(
        gate_up_columns_kernel,
        in_specs=[pl.BlockSpec(memory_space=pltpu.SMEM)] + [anywhere] * 2,
        out_specs=[anywhere] * 3,
        out_shape=[jax.ShapeDtypeStruct((n, 2 * FSHARD), BF16) for n in (SHARD, SHARD // 2, SHARD // 2)],
        scratch_shapes=[pltpu.VMEM((2 * SHARD, 2 * FSHARD), BF16), pltpu.SemaphoreType.DMA((9,))],
        compiler_params=pltpu.CompilerParams(vmem_limit_bytes=60 * 1024 * 1024),
        cost_estimate=COST,
    )(at, w_gate, w_up)


def column_copies(j, pieces, w_ref, sem):
    rows = lambda r: pl.ds(pl.multiple_of((r ^ j) * SHARD, SHARD), SHARD)
    return [pltpu.make_async_copy(ref, w_ref.at[rows(r)], sem.at[r]) for r, ref in enumerate(pieces)]


def forward_kernel(
    at_ref, first_ref, second_ref, bias_ref, wo_ref, own_ref, sister_ref, far_ref, cross_ref,
    keep_ref, send_ref, normed_out, qkv_out, forget_out, probs_out, mixed_out,
    w_ref, normed_ref, qkv_ref, forget_ref, probs_ref, mixed_ref, gain_ref, sem,
):
    j = at_ref[2]
    copies = column_copies(j, (own_ref, sister_ref, far_ref, cross_ref), w_ref, sem)
    for copy in copies:
        copy.start()
    for r in range(4):
        lanes = pl.ds(pl.multiple_of((r ^ j) * SHARD, SHARD), SHARD)
        ref = (first_ref, second_ref)[r % 2]
        gain_ref[:, lanes] = ref[r // 2, ROWS : ROWS + 1, :SHARD].astype(F32)
    for block in range(4):
        x = (first_ref, second_ref)[block // 2][block % 2, :ROWS].astype(F32)
        factor = lax.rsqrt(jnp.mean(x * x, axis=1, keepdims=True) + EPSILON)
        normed_ref[block * ROWS : block * ROWS + ROWS] = (x * factor * gain_ref[...]).astype(BF16)
    for copy in copies:
        copy.wait()

    out = lambda ref, target, n: pltpu.make_async_copy(ref, target, sem.at[4 + n])
    leaving = [out(normed_ref, normed_out, 0)]
    leaving[0].start()
    normed = normed_ref[...]
    forget_ref[...] = dot(normed, w_ref[:, 3 * SHARD :], AB) + bias_ref[...]
    for col in range(3):
        lanes = slice(SHARD * col, SHARD * col + SHARD)
        qkv_ref[:, lanes] = dot(normed, w_ref[:, lanes], AB).astype(BF16)
    leaving += [out(forget_ref, forget_out, 1), out(qkv_ref, qkv_out, 2)]
    for copy in leaving[1:]:
        copy.start()

    rows = lax.broadcasted_iota(jnp.int32, (ROWS, ROWS), 0)
    cols = lax.broadcasted_iota(jnp.int32, (ROWS, ROWS), 1)
    lower = (rows >= cols).astype(F32)
    left = lax.broadcasted_iota(jnp.int32, (ROWS, 128), 1) < HD
    for block in range(4):
        at = slice(block * ROWS, block * ROWS + ROWS)
        lens = (first_ref, second_ref)[block // 2][block % 2, ROWS : ROWS + 1, 2 * SHARD : 2 * SHARD + SLOTS]
        decays = exact_dot(lower, jax.nn.log_sigmoid(forget_ref[at, :]))
        decays_t = decays.T
        allowed = attend_mask(lens.astype(F32))
        for pair in range(LOCAL_HEADS // 2):
            lane = 128 * pair
            q2, k2, v2 = (qkv_ref[at, SHARD * n + lane : SHARD * n + lane + 128] for n in range(3))
            zero = jnp.zeros_like(k2)
            keys = jnp.concatenate([jnp.where(left, k2, zero), jnp.where(left, zero, k2)], axis=0)
            values = jnp.concatenate([jnp.where(left, v2, zero), jnp.where(left, zero, v2)], axis=0)
            both = dot(q2, keys, ABT)
            low = []
            for side in range(2):
                head = 2 * pair + side
                scores = both[:, ROWS * side : ROWS * side + ROWS] * (HD ** (-0.5))
                scores = scores + decays[:, head : head + 1] - decays_t[head : head + 1, :]
                scores = jnp.where(allowed, scores, -1e30)
                highest = jnp.max(scores, axis=1, keepdims=True)
                weights = jnp.exp(scores - highest)
                probs = weights / jnp.sum(weights, axis=1, keepdims=True)
                probs_ref[block, head] = probs
                low.append(probs.astype(BF16))
            mixed_ref[at, lane : lane + 128] = dot(jnp.concatenate(low, axis=1), values, AB).astype(BF16)
        leaving.append(out(probs_ref.at[block], probs_out.at[block], 4 + block))
        leaving[-1].start()
    leaving.append(out(mixed_ref, mixed_out, 3))
    leaving[-1].start()
    for col in range(4):
        lanes = slice(SHARD * col, SHARD * col + SHARD)
        partial = dot(mixed_ref[...], wo_ref[:, lanes], AB).astype(BF16)
        keep_ref[:, lanes] = partial[: 2 * ROWS]
        send_ref[:, lanes] = partial[2 * ROWS :]
    for copy in leaving:
        copy.wait()


def attention_forward(at, first, second, bias, wo, pieces):
    vmem, anywhere = pl.BlockSpec(memory_space=pltpu.VMEM), pl.BlockSpec(memory_space=pltpu.HBM)
    saved = [
        ((4 * ROWS, D), BF16),
        ((4 * ROWS, 3 * SHARD), BF16),
        ((4 * ROWS, 128), F32),
        ((4, LOCAL_HEADS, ROWS, ROWS), F32),
        ((4 * ROWS, SHARD), BF16),
    ]
    return pl.pallas_call(
        forward_kernel,
        in_specs=[pl.BlockSpec(memory_space=pltpu.SMEM)] + [vmem] * 4 + [anywhere] * 4,
        out_specs=[vmem] * 2 + [anywhere] * 5,
        out_shape=[jax.ShapeDtypeStruct((2 * ROWS, D), BF16)] * 2 + [pltpu.HBM(*v) for v in saved],
        scratch_shapes=[pltpu.VMEM((D, WIDTH), BF16)]
        + [pltpu.VMEM(*v) for v in saved]
        + [pltpu.VMEM((1, D), F32), pltpu.SemaphoreType.DMA((12,))],
        compiler_params=pltpu.CompilerParams(vmem_limit_bytes=32 * 1024 * 1024),
        cost_estimate=COST,
    )(at, first, second, bias, wo, *pieces)


def backward_kernel(
    half, at_ref, x_ref, gab_ref, wo_ref, qkv_in, forget_in, probs_in, own_ref, sister_ref, far_ref, cross_ref,
    low_ref, dqkvf_ref, gain_grad_ref, qkv_ref, forget_ref, probs_ref, w_ref, sem,
):
    rows = pl.ds(2 * ROWS * half, 2 * ROWS)
    saved = [
        pltpu.make_async_copy(qkv_in.at[rows], qkv_ref, sem.at[4]),
        pltpu.make_async_copy(forget_in.at[rows], forget_ref, sem.at[5]),
        pltpu.make_async_copy(probs_in.at[pl.ds(2 * half, 2)], probs_ref, sem.at[6]),
    ]
    copies = column_copies(at_ref[2], (own_ref, sister_ref, far_ref, cross_ref), w_ref, sem)
    for copy in saved + copies:
        copy.start()
    gm = dot(gab_ref[...], wo_ref[...], ABT).astype(BF16)
    for copy in saved:
        copy.wait()

    lane = lax.broadcasted_iota(jnp.int32, (ROWS, 128), 1)
    left = lane < HD
    upper = lax.broadcasted_iota(jnp.int32, (ROWS, ROWS), 0) <= lax.broadcasted_iota(jnp.int32, (ROWS, ROWS), 1)
    ones = jnp.ones((ROWS, 128), BF16)
    for block in range(2):
        at = slice(block * ROWS, block * ROWS + ROWS)
        grad_decays = jnp.zeros((ROWS, 128), F32)
        for pair in range(LOCAL_HEADS // 2):
            first = 128 * pair
            q2, k2, v2 = (qkv_ref[at, SHARD * n + first : SHARD * n + first + 128] for n in range(3))
            g2 = gm[at, first : first + 128]
            zero = jnp.zeros_like(k2)
            keys = jnp.concatenate([jnp.where(left, k2, zero), jnp.where(left, zero, k2)], axis=0)
            values = jnp.concatenate([jnp.where(left, v2, zero), jnp.where(left, zero, v2)], axis=0)
            both = dot(g2, values, ABT)
            grads, low = [], []
            for side in range(2):
                probs = probs_ref[block, 2 * pair + side]
                grad_probs = both[:, ROWS * side : ROWS * side + ROWS]
                inner = jnp.sum(probs * grad_probs, axis=1, keepdims=True)
                grads.append((probs * (grad_probs - inner)).astype(BF16))
                low.append(probs.astype(BF16))
            grads, low = jnp.concatenate(grads, axis=1), jnp.concatenate(low, axis=1)
            pick = lambda v: jnp.where(left, v[:ROWS], v[ROWS:])
            dq = dot(grads, keys, AB) * (HD ** (-0.5))
            dk = pick(dot(grads, q2, ATB)) * (HD ** (-0.5))
            for n, value in enumerate((dq, dk, pick(dot(low, g2, ATB)))):
                dqkvf_ref[at, SHARD * n + first : SHARD * n + first + 128] = value.astype(BF16)
            over_queries = dot(grads, ones, ATB)
            for side in range(2):
                here = lane == 2 * pair + side
                over_keys = dot(grads[:, ROWS * side : ROWS * side + ROWS], here.astype(BF16), AB)
                grad_decays = grad_decays + over_keys
                grad_decays = grad_decays - jnp.where(here, over_queries[ROWS * side : ROWS * side + ROWS], 0.0)
        grad_logs = exact_dot(upper.astype(F32), grad_decays)
        dqkvf_ref[at, 3 * SHARD :] = (grad_logs * jax.nn.sigmoid(-forget_ref[at, :])).astype(BF16)

    for copy in copies:
        copy.wait()
    scaled = []
    for block in range(2):
        x = x_ref[block, :ROWS].astype(F32)
        scaled.append(x * lax.rsqrt(jnp.mean(x * x, axis=1, keepdims=True) + EPSILON))
    for col in range(4):
        lanes = slice(SHARD * col, SHARD * col + SHARD)
        incoming = dot(dqkvf_ref[...], w_ref[lanes, :], ABT)
        low_ref[:, lanes] = incoming.astype(BF16)
        gain_grad_ref[:, lanes] = sum(
            jnp.sum(incoming[ROWS * n : ROWS * n + ROWS] * scaled[n][:, lanes], axis=0, keepdims=True) for n in range(2)
        )


def attention_backward(half, at, x, gab, wo, qkv, forget, probs, pieces):
    vmem, anywhere = pl.BlockSpec(memory_space=pltpu.VMEM), pl.BlockSpec(memory_space=pltpu.HBM)
    return pl.pallas_call(
        functools.partial(backward_kernel, half),
        in_specs=[pl.BlockSpec(memory_space=pltpu.SMEM)] + [vmem] * 3 + [anywhere] * 7,
        out_specs=[vmem] * 3,
        out_shape=[
            jax.ShapeDtypeStruct((2 * ROWS, D), BF16),
            jax.ShapeDtypeStruct((2 * ROWS, WIDTH), BF16),
            jax.ShapeDtypeStruct((1, D), F32),
        ],
        scratch_shapes=[
            pltpu.VMEM((2 * ROWS, 3 * SHARD), BF16),
            pltpu.VMEM((2 * ROWS, 128), F32),
            pltpu.VMEM((2, LOCAL_HEADS, ROWS, ROWS), F32),
            pltpu.VMEM((D, WIDTH), BF16),
            pltpu.SemaphoreType.DMA((7,)),
        ],
        compiler_params=pltpu.CompilerParams(vmem_limit_bytes=24 * 1024 * 1024),
        cost_estimate=GRADIENT_COST,
    )(at, x, gab, wo, qkv, forget, probs, *pieces)


FBLOCK = 256


def ffn_kernel(
    at_ref, first_ref, second_ref, gb_ref, wd_ref, gate_ref, up_ref, sister_ref, z_ref, z_other_ref, y_ref, y_other_ref,
    keep_ref, send_ref, hidden_ref, dg_ref, du_ref, n2_ref, w_ref, sem,
):
    j, bit_z, bit_y = at_ref[2], at_ref[3], at_ref[4]
    lanes = pl.ds(pl.multiple_of(j * FSHARD, FSHARD), FSHARD)

    def rows(r, first, count):
        return pl.ds(pl.multiple_of((r ^ j) * SHARD + first, 192), count)

    half = SHARD // 2
    pieces = (
        (sister_ref, rows(1, 0, SHARD)),
        (z_ref, rows(2, bit_z * half, half)),
        (z_other_ref, rows(2, half - bit_z * half, half)),
        (y_ref, rows(3, bit_y * half, half)),
        (y_other_ref, rows(3, half - bit_y * half, half)),
    )
    own = rows(0, 0, SHARD)
    fill(
        [
            (gate_ref.at[:, lanes], w_ref.at[own, pl.ds(0, FSHARD)], sem.at[0]),
            (up_ref.at[:, lanes], w_ref.at[own, pl.ds(FSHARD, FSHARD)], sem.at[1]),
        ]
        + [(ref, w_ref.at[at], sem.at[2 + n]) for n, (ref, at) in enumerate(pieces)]
    )
    n2_ref[: 2 * ROWS] = first_ref[...]
    n2_ref[2 * ROWS :] = second_ref[...]
    n2, gb = n2_ref[...], gb_ref[...]
    for step in range(FSHARD // FBLOCK):
        cols = slice(step * FBLOCK, step * FBLOCK + FBLOCK)
        gate = dot(n2, w_ref[:, cols], AB)
        up = dot(n2, w_ref[:, FSHARD + step * FBLOCK : FSHARD + step * FBLOCK + FBLOCK], AB)
        grad_hidden = dot(gb, wd_ref[cols, :], ABT)
        sig = jax.nn.sigmoid(gate)
        act = gate * sig
        hidden_ref[:, cols] = (act * up).astype(BF16)
        dg_ref[:, cols] = (grad_hidden * up * sig * (1.0 + gate * (1.0 - sig))).astype(BF16)
        du_ref[:, cols] = (grad_hidden * act).astype(BF16)
    for step in range(4):
        feat = slice(step * SHARD, step * SHARD + SHARD)
        part = dot(dg_ref[...], w_ref[feat, :FSHARD], ABT) + dot(du_ref[...], w_ref[feat, FSHARD:], ABT)
        part = part.astype(BF16)
        keep_ref[:, feat] = part[: 2 * ROWS]
        send_ref[:, feat] = part[2 * ROWS :]


def ffn(at, first, second, gb, wd, w_gate, w_up, pieces):
    vmem = pl.BlockSpec(memory_space=pltpu.VMEM)
    wide = [jax.ShapeDtypeStruct((4 * ROWS, FSHARD), BF16)] * 3
    return pl.pallas_call(
        ffn_kernel,
        in_specs=[pl.BlockSpec(memory_space=pltpu.SMEM)] + [vmem] * 4 + [pl.BlockSpec(memory_space=pltpu.HBM)] * 7,
        out_specs=[vmem] * 6,
        out_shape=[jax.ShapeDtypeStruct((2 * ROWS, D), BF16)] * 2 + wide + [jax.ShapeDtypeStruct((4 * ROWS, D), BF16)],
        scratch_shapes=[pltpu.VMEM((D, 2 * FSHARD), BF16), pltpu.SemaphoreType.DMA((7,))],
        compiler_params=pltpu.CompilerParams(vmem_limit_bytes=32 * 1024 * 1024),
        cost_estimate=COST,
    )(at, first, second, gb, wd, w_gate, w_up, *pieces)


STAGES = ((1, 3), (3, 1))


def labels(j):
    core = j & 1
    return (0, 3 - 2 * core, 1 + 2 * core, 2)


def piece_of(part, index, label):
    a, b = label[index // 4], label[index % 4]
    return (b, a) if part == 0 else (a, b)


def place(outs, part, index):
    return outs[2 * part + index // 8], index % 8


FUNITS = 72
QUNITS = ((0, 8), (8, 15))
OUNITS = ((0, 8), (8, 18))
AUNITS = tuple(4 * (q1 - q0) + (o1 - o0) for (q0, q1), (o0, o1) in zip(QUNITS, OUNITS))
NQ, NO = 240, 288


def ffn_grad_kernel(part, at_ref, n2_ref, gb_ref, hidden_ref, grad_ref, keep_ref, send_ref, cols_ref, down_ref):
    y, z, j = at_ref[0], at_ref[1], at_ref[2]
    label = labels(j)
    n2 = n2_ref[...]
    for step in range(4):
        pz = label[step] ^ z
        lanes = pl.ds(pl.multiple_of(pz * FBLOCK, FBLOCK), FBLOCK)
        cols_ref[...] = dot(n2, grad_ref[:, lanes], ATB).astype(BF16).reshape(16, 96, FBLOCK)
        gb = gb_ref[:, 768 * part : 768 * part + 768]
        down_ref[...] = dot(hidden_ref[:, lanes], gb, ATB).astype(BF16).reshape(4, 64, 768)
        for other in range(4):
            py = label[other] ^ y
            index = 4 * step + other if part == 0 else 4 * other + step
            out, slot = (keep_ref, send_ref)[index // 8], index % 8
            for r in range(4):
                for half in range(2):
                    block = cols_ref[(r ^ j) * 4 + py, :, 128 * half : 128 * half + 128]
                    out[slot, 12 * r + 6 * half : 12 * r + 6 * half + 6] = block.reshape(6, 16, 128)
            for t in range(6):
                block = down_ref[py, :, 128 * t : 128 * t + 128]
                out[slot, 48 + 4 * t : 52 + 4 * t] = block.reshape(4, 16, 128)


def ffn_gradients(part, at, n2, gb, hidden, grad):
    vmem = pl.BlockSpec(memory_space=pltpu.VMEM)
    return pl.pallas_call(
        functools.partial(ffn_grad_kernel, part),
        in_specs=[pl.BlockSpec(memory_space=pltpu.SMEM)] + [vmem] * 4,
        out_specs=[vmem] * 2,
        out_shape=[jax.ShapeDtypeStruct((8, FUNITS, 16, 128), BF16)] * 2,
        scratch_shapes=[pltpu.VMEM((16, 96, FBLOCK), BF16), pltpu.VMEM((4, 64, 768), BF16)],
        compiler_params=pltpu.CompilerParams(vmem_limit_bytes=20 * 1024 * 1024),
        cost_estimate=GRADIENT_COST,
    )(at, n2, gb, hidden, grad)


def ffn_unpack_kernel(at_ref, *refs):
    ins, (gate_ref, up_ref, down_ref) = refs[:4], refs[4:]
    y, z, j = at_ref[0], at_ref[1], at_ref[2]
    label = labels(j)
    for part in range(2):
        target = (gate_ref, up_ref)[part]
        for index in range(16):
            ry, rz = piece_of(part, index, label)
            source, slot = place(ins, part, index)
            py, pz = ry ^ y, rz ^ z
            rows = pl.ds(pl.multiple_of(py * 96, 32), 96)
            for r in range(4):
                for half in range(2):
                    left = (r ^ j) * FSHARD + pz * FBLOCK + half * 128
                    block = source[slot, 12 * r + 6 * half : 12 * r + 6 * half + 6].reshape(96, 128)
                    target[rows, pl.ds(pl.multiple_of(left, 128), 128)] = block.astype(F32)
            rows = pl.ds(pl.multiple_of(pz * 256 + py * 64, 64), 64)
            for t in range(6):
                left = 768 * part + 128 * t
                block = source[slot, 48 + 4 * t : 52 + 4 * t].reshape(64, 128)
                down_ref[rows, left : left + 128] = block.astype(F32)


def ffn_unpack(at, pieces):
    vmem = pl.BlockSpec(memory_space=pltpu.VMEM)
    return pl.pallas_call(
        ffn_unpack_kernel,
        in_specs=[pl.BlockSpec(memory_space=pltpu.SMEM)] + [vmem] * 4,
        out_specs=[vmem] * 3,
        out_shape=[
            jax.ShapeDtypeStruct((SHARD, FF), F32),
            jax.ShapeDtypeStruct((SHARD, FF), F32),
            jax.ShapeDtypeStruct((FSHARD, D), F32),
        ],
        compiler_params=pltpu.CompilerParams(vmem_limit_bytes=30 * 1024 * 1024),
        cost_estimate=GRADIENT_COST,
    )(at, *pieces)


def attention_grad_kernel(at_ref, normed_ref, d1_ref, d2_ref, mixed_ref, g1_ref, g2_ref, gains_ref, *rest):
    outs, (q_ref, o_ref) = rest[:4], rest[4:]
    y, z, j = at_ref[0], at_ref[1], at_ref[2]
    label = labels(j)
    d1, d2 = d1_ref[...], d2_ref[...]
    upper, lower = pl.ds(0, 2 * ROWS), pl.ds(2 * ROWS, 2 * ROWS)
    row = lax.broadcasted_iota(jnp.int32, (16, 128), 0)
    lane = lax.broadcasted_iota(jnp.int32, (16, 128), 1)
    pick = (lane == row + LOCAL_HEADS).astype(BF16)
    pick = jnp.where(row < 2, pick, jnp.zeros_like(pick))
    bias = sum(jnp.sum(d[:, 3 * SHARD :].astype(F32), axis=0, keepdims=True) for d in (d1, d2))
    bias = pltpu.roll(bias, 8, 1)

    def units(source, width, per, p, t):
        odd = (p & 1) == 1
        group = (p >> 1) * 3 + jnp.where(odd, (per + t) // width, t // width)
        return source[group, jnp.where(odd, (per + t) % width, t % width)]

    def piece(part, index):
        ry, rz = piece_of(part, index, label)
        return (ry ^ y) * 4 + (rz ^ z)

    for r in range(4):
        lanes = pl.ds(pl.multiple_of((r ^ j) * SHARD, SHARD), SHARD)
        grad = dot(normed_ref[upper, lanes], d1, ATB) + dot(normed_ref[lower, lanes], d2, ATB)
        extra = grad[:, 3 * SHARD :] + dot(gains_ref[:, lanes], pick, ATB) + bias
        for col in range(9):
            block = grad[:, 128 * col : 128 * col + 128].astype(BF16).reshape(24, 1, 16, 128)
            q_ref[:, col : col + 1] = block
        q_ref[:, 9:10] = extra.astype(BF16).reshape(24, 1, 16, 128)
        for part in range(2):
            lo, hi = QUNITS[part]
            for index in range(16):
                out, slot = place(outs, part, index)
                for t in range(lo, hi):
                    out[slot, (hi - lo) * r + t - lo] = units(q_ref, 10, 15, piece(part, index), t)
    grad = dot(mixed_ref[upper, :], g1_ref[...], ATB) + dot(mixed_ref[lower, :], g2_ref[...], ATB)
    for col in range(12):
        o_ref[:, col : col + 1] = grad[:, 128 * col : 128 * col + 128].astype(BF16).reshape(24, 1, 16, 128)
    for part in range(2):
        lo, hi = OUNITS[part]
        first = AUNITS[part] - (hi - lo)
        for index in range(16):
            out, slot = place(outs, part, index)
            for t in range(lo, hi):
                out[slot, first + t - lo] = units(o_ref, 12, 18, piece(part, index), t)


def attention_gradients(at, normed, d1, d2, mixed, g1, g2, gains):
    vmem = pl.BlockSpec(memory_space=pltpu.VMEM)
    return pl.pallas_call(
        attention_grad_kernel,
        in_specs=[pl.BlockSpec(memory_space=pltpu.SMEM)] + [vmem] * 7,
        out_specs=[vmem] * 4,
        out_shape=[jax.ShapeDtypeStruct((8, AUNITS[i // 2], 16, 128), BF16) for i in range(4)],
        scratch_shapes=[
            pltpu.VMEM((24, 10, 16, 128), BF16),
            pltpu.VMEM((24, 12, 16, 128), BF16),
        ],
        compiler_params=pltpu.CompilerParams(vmem_limit_bytes=26 * 1024 * 1024),
        cost_estimate=GRADIENT_COST,
    )(at, normed, d1, d2, mixed, g1, g2, gains)


def attention_unpack_kernel(at_ref, *refs):
    ins, (gq_ref, gk_ref, gv_ref, go_ref, forget_ref, small_ref, q_ref, o_ref) = refs[:4], refs[4:]
    y, z, j = at_ref[0], at_ref[1], at_ref[2]
    label = labels(j)
    for part in range(2):
        qlo, qhi = QUNITS[part]
        olo, ohi = OUNITS[part]
        n = qhi - qlo
        for index in range(16):
            ry, rz = piece_of(part, index, label)
            source, slot = place(ins, part, index)
            p = (ry ^ y) * 4 + (rz ^ z)
            for r in range(4):
                q_ref[r ^ j, pl.ds(p * 15 + qlo, n)] = source[slot, n * r : n * r + n]
            o_ref[pl.ds(p * 18 + olo, ohi - olo)] = source[slot, 4 * n : 4 * n + ohi - olo]
    for group in range(24):
        rows = slice(16 * group, 16 * group + 16)
        for device in range(4):
            for col in range(10):
                if col < 9:
                    target = (gq_ref, gk_ref, gv_ref)[col // 3]
                    left = SHARD * device + 128 * (col % 3)
                    target[rows, left : left + 128] = q_ref[device, 10 * group + col].astype(F32)
        for col in range(12):
            go_ref[rows, 128 * col : 128 * col + 128] = o_ref[12 * group + col].astype(F32)
    lane = lax.broadcasted_iota(jnp.int32, (128, 128), 1)
    for third in range(3):
        forget = jnp.zeros((128, 128), F32)
        total = jnp.zeros((128, 128), F32)
        for device in range(4):
            parts = [q_ref[device, 10 * group + 9] for group in range(8 * third, 8 * third + 8)]
            extra = jnp.concatenate(parts, axis=0).astype(F32)
            mine = (lane >= LOCAL_HEADS * device) & (lane < LOCAL_HEADS * device + LOCAL_HEADS)
            moved = pltpu.roll(extra, LOCAL_HEADS * device, 1) if device else extra
            forget = jnp.where(mine, moved, forget)
            total = total + extra
        forget_ref[:, 128 * third : 128 * third + 128] = forget.T[:H]
        small_ref[:, 128 * third : 128 * third + 128] = total.T[:16]
    first = q_ref[j, pl.ds(9, 1)].astype(F32)
    small_ref[8:16, 0:128] = first.reshape(16, 128)[:8]


def attention_unpack(at, pieces):
    vmem = pl.BlockSpec(memory_space=pltpu.VMEM)
    return pl.pallas_call(
        attention_unpack_kernel,
        in_specs=[pl.BlockSpec(memory_space=pltpu.SMEM)] + [vmem] * 4,
        out_specs=[vmem] * 6,
        out_shape=[jax.ShapeDtypeStruct((SHARD, D), F32)] * 4
        + [jax.ShapeDtypeStruct((H, SHARD), F32), jax.ShapeDtypeStruct((16, SHARD), F32)],
        scratch_shapes=[
            pltpu.VMEM((4, NQ, 16, 128), BF16),
            pltpu.VMEM((NO, 16, 128), BF16),
        ],
        compiler_params=pltpu.CompilerParams(vmem_limit_bytes=24 * 1024 * 1024),
        cost_estimate=COST,
    )(at, *pieces)


def small_call(kernel, out, *args):
    vmem = pl.BlockSpec(memory_space=pltpu.VMEM)
    return pl.pallas_call(
        kernel,
        in_specs=[vmem] * len(args),
        out_specs=[vmem] * len(out),
        out_shape=[jax.ShapeDtypeStruct((n, 16, 128), BF16) for n in out],
        compiler_params=pltpu.CompilerParams(vmem_limit_bytes=8 * 1024 * 1024),
        cost_estimate=COST,
    )(*args)


def add_slots(held, first, count):
    n = held[0].shape[1]

    def kernel(*refs):
        refs[-1][...] = functools.reduce(lambda a, b: a + b, [ref[...].astype(F32) for ref in refs[:-1]]).astype(BF16)

    return pl.pallas_call(
        kernel,
        grid=(1,),
        in_specs=[pl.BlockSpec((count, n, 16, 128), lambda i: (first // count, 0, 0, 0))] * len(held),
        out_specs=pl.BlockSpec((count, n, 16, 128), lambda i: (0, 0, 0, 0)),
        out_shape=jax.ShapeDtypeStruct((count, n, 16, 128), BF16),
        compiler_params=pltpu.CompilerParams(vmem_limit_bytes=20 * 1024 * 1024),
        cost_estimate=COST,
    )(*held)


def join(upper, lower):
    slots, n = upper.shape[:2]

    def kernel(upper_ref, lower_ref, out_ref):
        out_ref[:slots] = upper_ref[...]
        out_ref[slots:] = lower_ref[...]

    vmem = pl.BlockSpec(memory_space=pltpu.VMEM)
    return pl.pallas_call(
        kernel,
        in_specs=[vmem] * 2,
        out_specs=vmem,
        out_shape=jax.ShapeDtypeStruct((2 * slots, n, 16, 128), BF16),
        compiler_params=pltpu.CompilerParams(vmem_limit_bytes=8 * 1024 * 1024),
        cost_estimate=COST,
    )(upper, lower)


def row_call(kernel, out, *args, mib=20):
    vmem = pl.BlockSpec(memory_space=pltpu.VMEM)
    return pl.pallas_call(
        kernel,
        in_specs=[vmem] * len(args),
        out_specs=[vmem] * len(out),
        out_shape=[jax.ShapeDtypeStruct(*v) for v in out],
        compiler_params=pltpu.CompilerParams(vmem_limit_bytes=mib * 1024 * 1024),
        cost_estimate=COST,
    )(*args)


HALF = (2 * ROWS, D)


def add_rows(former, latter):
    def kernel(former_ref, latter_ref, out_ref):
        out_ref[...] = (former_ref[...].astype(F32) + latter_ref[...].astype(F32)).astype(BF16)

    return row_call(kernel, [(former.shape, BF16)], former, latter, mib=6)[0]


def both_chips(chip_ref, other_ref, block):
    here = slice(ROWS * block, ROWS * block + ROWS)
    there = slice(ROWS * (1 - block), ROWS * (1 - block) + ROWS)
    return chip_ref[here].astype(F32) + other_ref[there].astype(F32)


def middle_rows(rows, chip, other, gain):
    def kernel(x_ref, chip_ref, other_ref, gain_ref, middle_ref, normed_ref):
        for block in range(2):
            here = slice(ROWS * block, ROWS * block + ROWS)
            middle = x_ref[block, :ROWS].astype(F32) + both_chips(chip_ref, other_ref, block)
            factor = lax.rsqrt(jnp.mean(middle * middle, axis=1, keepdims=True) + EPSILON)
            middle_ref[here] = middle
            normed_ref[here] = (middle * factor * gain_ref[...]).astype(BF16)

    return row_call(kernel, [(HALF, F32), (HALF, BF16)], rows, chip, other, gain, mib=14)


def middle_gradient(chip, other, middle, branch, gain):
    def kernel(chip_ref, other_ref, middle_ref, branch_ref, gain_ref, grad_ref, low_ref, part_ref):
        total = jnp.zeros((1, D), F32)
        for block in range(2):
            here = slice(ROWS * block, ROWS * block + ROWS)
            incoming = both_chips(chip_ref, other_ref, block)
            middle = middle_ref[here]
            factor = lax.rsqrt(jnp.mean(middle * middle, axis=1, keepdims=True) + EPSILON)
            scaled = incoming * gain_ref[...]
            inner = jnp.mean(scaled * middle, axis=1, keepdims=True)
            grad = branch_ref[here].astype(F32) + (scaled * factor - middle * (factor * factor * factor) * inner)
            grad_ref[here] = grad
            low_ref[here] = grad.astype(BF16)
            total = total + jnp.sum(incoming * middle * factor, axis=0, keepdims=True)
        part_ref[...] = total

    out = [(HALF, F32), (HALF, BF16), ((1, D), F32)]
    return row_call(kernel, out, chip, other, middle, branch, gain)


def for_sister(pieces, columns):
    def kernel(first_ref, second_ref, out_ref):
        at = 0
        for r in (1, 3):
            for ref, n in zip((first_ref, second_ref), columns):
                out_ref[at : at + n] = ref[r * n : r * n + n]
                at += n

    return small_call(kernel, [2 * sum(columns)], *pieces)[0]


def for_chips(pieces, sister, columns):
    n = sum(columns)
    tails = [p.shape[0] - 4 * m for p, m in zip(pieces, columns)]

    def kernel(first_ref, second_ref, sister_ref, near_ref, far_ref):
        at, tail = 0, 2 * n
        for ref, m, last in zip((first_ref, second_ref), columns, tails):
            near_ref[at : at + m] = ref[0:m]
            far_ref[at : at + m] = ref[2 * m : 3 * m]
            near_ref[tail : tail + last] = ref[4 * m : 4 * m + last]
            at, tail = at + m, tail + last
        near_ref[n : 2 * n] = sister_ref[0:n]
        far_ref[n : 2 * n] = sister_ref[n : 2 * n]

    return small_call(kernel, [2 * n + sum(tails), 2 * n], *pieces, sister)


def join_chips(near, far, a, b, t, columns):
    n = sum(columns)
    last = near.shape[0] - 2 * n
    tails = [last // 2, last // 2] if columns[0] == columns[1] else [hi - lo for lo, hi in OUNITS]

    def kernel(near_ref, far_ref, a_ref, b_ref, t_ref, first_ref, second_ref):
        def total(x_ref, y_ref, lo, m):
            return (x_ref[lo : lo + m].astype(F32) + y_ref[lo : lo + m].astype(F32)).astype(BF16)

        at, tail = 0, 2 * n
        for ref, m, end in zip((first_ref, second_ref), columns, tails):
            ref[0:m] = total(near_ref, t_ref, at, m)
            ref[m : 2 * m] = total(near_ref, t_ref, n + at, m)
            ref[2 * m : 3 * m] = total(a_ref, b_ref, at, m)
            ref[3 * m : 4 * m] = total(a_ref, b_ref, n + at, m)
            ref[4 * m : 4 * m + end] = total(near_ref, t_ref, tail, end)
            at, tail = at + m, tail + end

    return small_call(kernel, [4 * m + end for m, end in zip(columns, tails)], near, far, a, b, t)


def make_body(sizes):
    ny, nxh, nz = sizes

    def send(value, move):
        pairs = []
        for y in range(ny):
            for x in range(2 * nxh):
                for z in range(nz):
                    for c in range(2):
                        ty, tx, tz, tc = move(y, x, z, c)
                        tx %= 2 * nxh
                        src = (((y * nxh + x // 2) * nz + z) * 2 + x % 2) * 2 + c
                        dst = (((ty * nxh + tx // 2) * nz + tz) * 2 + tx % 2) * 2 + tc
                        pairs.append((src, dst))
        return lax.ppermute(value, AXES, pairs)

    def swap_plane(value, axis, stage):
        if axis == "y":
            return send(value, lambda y, x, z, c: (y ^ STAGES[c][stage], x, z, c))
        return send(value, lambda y, x, z, c: (y, x, z ^ STAGES[c][stage], c))

    def after(value, *others):
        return lax.optimization_barrier((value, *others))[0]

    swap_core = lambda v: send(v, lambda y, x, z, c: (y, x, z, 1 - c))
    swap_x = lambda v: send(v, lambda y, x, z, c: (y, x ^ 1, z, c))
    swap_out = lambda v: send(v, lambda y, x, z, c: (y, x ^ 3, z, c))
    cross_mixed = lambda v: send(v, lambda y, x, z, c: (y, x ^ (1 if c else 3), z, 1 - c))
    cross_x = lambda v: send(v, lambda y, x, z, c: (y, x ^ 1, z, 1 - c))
    x_plus = lambda v: send(v, lambda y, x, z, c: (y, x + 1, z, c))
    x_minus = lambda v: send(v, lambda y, x, z, c: (y, x - 1, z, c))
    x_two = lambda v: send(v, lambda y, x, z, c: (y, x + 2, z, c))

    def total(parts):
        return functools.reduce(lambda a, b: a + b, [p.astype(F32) for p in parts])

    def combine(keep, received):
        return total([keep, received]).astype(BF16)

    class Order:
        def __init__(self):
            self.work = ()

        def arrive(self, *values):
            out = lax.optimization_barrier((*values, *self.work))[: len(values)]
            return out if len(values) > 1 else out[0]

        def then(self, *work):
            self.work = work

    def move(part, step):
        return ("zy"[part != step // 2], step % 2)

    class Lane:
        def __init__(self, order, part, keep, sending):
            self.order, self.part, self.held, self.sending, self.step = order, part, [keep], sending, 0

        def start(self):
            self.got = swap_plane(self.sending, *move(self.part, self.step))

        def arrive(self):
            self.held.append(self.order.arrive(self.got))
            half = 4 >> self.step
            self.sending = add_slots(self.held, half, max(half, 1))
            self.order.then(self.sending)
            self.step += 1

        def gather(self, piece):
            self.sending, self.step = piece[None], 3

        def collect(self):
            self.got = self.order.arrive(self.got)
            if self.step:
                self.sending = join(self.sending, self.got)
                self.order.then(self.sending)
            self.step -= 1

    def together(order, lanes):
        for lane, got in zip(lanes, order.arrive(*[lane.got for lane in lanes])):
            lane.got = got

    def both(lanes, *names):
        for name in names:
            for lane in lanes:
                getattr(lane, name)()

    def each(lanes, *names):
        for lane in lanes:
            for name in names:
                getattr(lane, name)()

    def spread_steps(order, pieces, columns):
        sister = swap_core(for_sister(pieces, columns))
        yield
        sister = order.arrive(sister)
        near, far = for_chips(pieces, sister, columns)
        order.then(far, near)
        a, b, t = x_plus(far), x_minus(far), x_two(near)
        yield
        a, b, t = order.arrive(a, b, t)
        out = join_chips(near, far, a, b, t, columns)
        order.then(*out)
        return out

    def finish(steps):
        try:
            next(steps)
        except StopIteration as stop:
            return stop.value

    def body(
        tokens, lengths, w_query, w_key, w_value, w_out, w_forget, forget_bias, norm_attn,
        w_gate, w_up, w_down, norm_ffn, cotangent,
    ):
        y, z, core = lax.axis_index("y"), lax.axis_index("z"), lax.axis_index("c")
        j = lax.axis_index("xl") * 2 + core
        bits = [(jnp.where(n == 0, z & 1, z >> 1), jnp.where(n == 0, y & 1, y >> 1)) for n in (core, 1 - core)]
        (bit_z, bit_y), (_, sister_bit_y) = bits
        at = jnp.stack([y, z, j, bit_z, bit_y, sister_bit_y]).astype(jnp.int32)

        own_cols, far_cols, sister_cols, cross_cols = columns(at, w_query, w_key, w_value, w_forget.T)
        far, cross, sister = swap_out(far_cols), cross_mixed(cross_cols), swap_core(sister_cols)
        cot_first = swap_x(after(cotangent, far_cols))

        small = jnp.concatenate([norm_attn, norm_ffn, lengths[0].astype(BF16)])
        small = after(small, far_cols)
        small = jnp.pad(small[None], ((0, 15), (0, D - small.shape[0])))
        packed = jnp.concatenate([tokens, small], axis=0)
        packed_first = swap_x(packed)

        sister_gu, cross_gu, far_gu = gate_up_columns(after(at, far_cols, packed), w_gate, w_up)

        order = Order()
        order.then(far_gu)
        packed_first = order.arrive(packed_first)
        pair = jnp.stack([packed, packed_first])
        order.then(pair)
        packed_second = swap_core(pair)
        sister, cross, cot_first = order.arrive(sister, cross, cot_first)
        order.then(sister, cross)
        fetch_y = cross_x(after(cross_gu, cross))
        far = order.arrive(far)
        order.then(sister, cross, far)
        fetch_z = swap_out(after(far_gu, far))
        sister_gu = swap_core(after(sister_gu, sister))
        packed_all = jnp.concatenate([pair, order.arrive(packed_second)], axis=0)
        x_rows = packed_all[:, :ROWS].reshape(4 * ROWS, D)
        small_all = packed_all[:, ROWS]
        lens = small_all[:, 2 * SHARD : 2 * SHARD + SLOTS].astype(jnp.int32)
        by_device = jnp.stack([small_all[0], small_all[2], small_all[1], small_all[3]])
        by_device = jnp.concatenate(
            [lax.dynamic_index_in_dim(by_device, j ^ r, 0, keepdims=True) for r in range(4)], axis=0
        ).astype(F32)
        gain_one = by_device[:, :SHARD].reshape(1, D)
        gain_two = by_device[:, SHARD : 2 * SHARD].reshape(1, D)
        bias = jnp.pad(forget_bias.astype(F32), (0, 128 - LOCAL_HEADS))[None]

        keep, sent, normed, qkv, forget, probs, mixed = attention_forward(
            at, pair, packed_second, bias, w_out, (own_cols, sister, far, cross)
        )
        live = (jnp.arange(ROWS)[None, :] < jnp.sum(lens, axis=1, keepdims=True)).reshape(4 * ROWS, 1)
        cot_pair = jnp.stack([cotangent, after(cot_first, sent)])
        first, fetch_z, fetch_y, sister_gu, cot_pair, live, gain_two = lax.optimization_barrier(
            (swap_core(sent), fetch_z, fetch_y, sister_gu, cot_pair, live, gain_two)
        )
        chip = add_rows(keep, first)
        other = swap_x(chip)
        other_z, other_y = swap_plane(fetch_z, "z", 0), swap_plane(fetch_y, "y", 0)
        cot_rows = jnp.concatenate([cot_pair, swap_core(cot_pair)], axis=0).reshape(4 * ROWS, D)
        grad_branch = jnp.where(live, cot_rows, jnp.zeros_like(cot_rows))
        other, other_z, other_y, grad_branch = lax.optimization_barrier((other, other_z, other_y, grad_branch))

        middle, n2_half = middle_rows(pair, chip, other, gain_two)
        n2_other = swap_core(n2_half)

        keep, sent, hidden, dgate, dup, n2 = ffn(
            at, n2_half, n2_other, grad_branch, w_down, w_gate, w_up, (sister_gu, fetch_z, other_z, fetch_y, other_y)
        )
        order = Order()
        first = swap_core(sent)
        ffn_parts = ffn_gradients(0, at, n2, grad_branch, hidden, dgate)
        order.then(ffn_parts[0])
        chip = add_rows(keep, order.arrive(first))
        ffn_parts = ffn_parts + ffn_gradients(1, at, after(n2, chip), grad_branch, hidden, dup)
        order.then(ffn_parts[2])
        ffn_lanes = [Lane(order, k, *ffn_parts[2 * k : 2 * k + 2]) for k in range(2)]
        both(ffn_lanes, "start")
        other = swap_x(chip)
        down = dot(after(hidden, ffn_parts[2]), w_down, AB).astype(BF16)
        order.then(down)
        grad_middle, gab_half, gain_two_part = middle_gradient(
            chip, order.arrive(other), middle, grad_branch, gain_two
        )
        order.then(gab_half)
        gab_other = swap_core(gab_half)
        down_first = swap_core(down[2 * ROWS :])

        kept = (w_out, qkv, forget, probs, (own_cols, sister, far, cross))
        keep, d1, gain_first = attention_backward(0, at, pair, gab_half, *kept)
        order.then(d1)
        each(ffn_lanes, "arrive", "start")
        gab_other = order.arrive(gab_other)
        sent, d2, gain_second = attention_backward(1, at, packed_second, gab_other, *kept)
        order.then(d2)
        token_first = swap_core(sent)
        each(ffn_lanes[:1], "arrive", "start")
        gains = jnp.concatenate([gain_first + gain_second, 0.5 * gain_two_part], axis=0).astype(BF16)
        gains = jnp.pad(gains, ((0, 14), (0, 0)))
        attn_parts = attention_gradients(at, normed, d1, order.arrive(d2), mixed, gab_half, gab_other, gains)
        order.then(attn_parts[0])
        each(ffn_lanes[1:], "arrive", "start")
        down_chip, token_chip = combine(down[: 2 * ROWS], down_first), add_rows(keep, order.arrive(token_first))
        order.then(down_chip, token_chip)
        down_other, token_other = swap_x(down_chip[ROWS:]), swap_x(token_chip[ROWS:])
        each(ffn_lanes, "arrive", "start")
        each(ffn_lanes, "arrive")
        attn_parts = after(attn_parts, ffn_lanes[1].sending)
        attn_lanes = [Lane(order, k, *attn_parts[2 * k : 2 * k + 2]) for k in range(2)]
        both(attn_lanes, "start")
        ffn_spread = spread_steps(order, [lane.sending[0] for lane in ffn_lanes], [12, 12])
        next(ffn_spread)
        next(ffn_spread)
        each(attn_lanes, "arrive", "start")
        ffn_pieces = finish(ffn_spread)
        for lane, piece in zip(ffn_lanes, ffn_pieces):
            lane.gather(piece)
        both(ffn_lanes, "start")

        def next_step(lanes, name):
            together(order, lanes)
            each(lanes, name, "start")

        next_step(ffn_lanes, "collect")
        next_step(attn_lanes, "arrive")
        next_step(ffn_lanes, "collect")
        next_step(attn_lanes, "arrive")
        together(order, attn_lanes)
        each(attn_lanes, "arrive")
        attn_spread = spread_steps(
            order, [lane.sending[0] for lane in attn_lanes], [hi - lo for lo, hi in QUNITS]
        )
        next(attn_spread)
        next_step(ffn_lanes, "collect")
        next(attn_spread)
        attn_pieces = finish(attn_spread)
        for lane, piece in zip(attn_lanes, attn_pieces):
            lane.gather(piece)
        both(attn_lanes, "start")
        next_step(attn_lanes, "collect")
        next_step(attn_lanes, "collect")
        down_other, token_other = order.arrive(down_other, token_other)
        together(order, ffn_lanes)
        each(ffn_lanes, "collect")
        order.then(*[lane.got for lane in ffn_lanes])
        next_step(attn_lanes, "collect")
        ffn_last = after([v for lane in ffn_lanes for v in (lane.sending, lane.got)], attn_lanes[1].sending)
        grad_gate, grad_up, grad_down = ffn_unpack(at, ffn_last)
        order.then(grad_down)
        each(attn_lanes, "collect")
        branch = down_chip[:ROWS].astype(F32) + down_other.astype(F32)
        output = jnp.where(live[:ROWS], middle[:ROWS] + branch, 0.0).astype(BF16)

        own = x_rows[:ROWS].astype(F32)
        factor_one = lax.rsqrt(jnp.mean(own * own, axis=1, keepdims=True) + EPSILON)
        scaled = (token_chip[:ROWS].astype(F32) + token_other.astype(F32)) * gain_one
        inner = jnp.mean(scaled * own, axis=1, keepdims=True)
        grad_tokens = grad_middle[:ROWS] + (
            scaled * factor_one - own * (factor_one * factor_one * factor_one) * inner
        )

        grad_query, grad_key, grad_value, grad_out, grad_forget, small = attention_unpack(
            at, [v for lane in attn_lanes for v in (lane.sending, lane.got)]
        )
        grad_forget = grad_forget.T
        grad_norm_attn, grad_norm_ffn = small[LOCAL_HEADS], small[LOCAL_HEADS + 1]
        grad_bias = small[8, 8 : 8 + LOCAL_HEADS]
        return (
            output, grad_tokens, grad_query, grad_key, grad_value, grad_out, grad_forget, grad_bias,
            grad_norm_attn, grad_gate, grad_up, grad_down, grad_norm_ffn,
        )

    return body


SIZES = {32: (4, 2, 4), 16: (4, 1, 4)}


def solution(mesh):
    sizes = SIZES[mesh.shape["wide"]]
    ny, nxh, nz = sizes
    fine = Mesh(mesh.devices.reshape(ny, nxh, nz, 2, 2), AXES)
    rows, shard, vector = P(AXES, None), P(("xl", "c"), None), P(("xl", "c"))
    return jax.shard_map(
        make_body(sizes),
        mesh=fine,
        in_specs=(
            rows, rows, shard, shard, shard, shard, shard, vector, vector, shard, shard, shard, vector, rows,
        ),
        out_specs=(
            rows, rows, shard, shard, shard, shard, shard, vector, vector, shard, shard, shard, vector,
        ),
        check_vma=False,
    )
```
